256 devices in a mesh: ga: 8 (over z_lo, core), ba: 32 (over x, y, z_hi).
Axes of the slice: x: 4, y: 4, z: 8 (z_hi: 2, z_lo: 4; z = z_hi * 4 + z_lo), core: 2. Of those that a mesh axis runs over, the one named last changes fastest.
Arguments:
- white_noise: float32 [256, 512, 512], P('ba', 'ga'), may hold values from -6 to 6
- amplitude: float32 [512, 512, 256], P('ba', 'ga'), may hold values from 0.2 to 2, as said below
- recharge: float32 [256, 256, 128], P('ga', 'ba'), may hold values from -6 to 6
- head_guess: float32 [256, 256, 128], P('ga', 'ba'), may hold values from -6 to 6
Outputs:
- conductivity: float32 [256, 256, 128], P('ga', 'ba')
- pressure: float32 [256, 256, 128], P('ga', 'ba')
The draws below stay inside these ranges and needn't reach their ends.
Inputs may be any that keep to these rules, and one draw needn't show every extreme that they name: amplitude is even in the frequencies: its entry at (ky, kx, kz) equals its entry at ((-ky) mod 512, (-kx) mod 512, (-kz) mod 256).
All inputs are finite; a program needn't handle non-finite values.
Results may differ from the reference program's by a relative error of at most 0.00029.
Values sent between devices are 32-bit elements; how exact they have to be, the bound alone decides.
No kernel may reach another device: no remote copies, remote signals or barrier semaphores. Data moves between devices by JAX's collectives and lax.ppermute only.
A program may use at most 64 MiB of HBM per device.

```python
import math
import jax
import jax.numpy as jnp

AX = 256
AY = 256
AZ = 128
SWEEPS = 2
EX = 512
EY = 512
EZ = 256


def mirrored(values):
    for axis_number in range(3):
        values = jnp.roll(jnp.flip(values, axis_number), 1, axis_number)
    return values


def draw_amplitude(key, part):
    key = jax.random.fold_in(key, 5)
    shape = (EY, EX, EZ)
    base = jnp.exp(jax.random.uniform(key, shape, jnp.float32, math.log(0.2), math.log(2.0)))
    return 0.5 * (base + mirrored(base))


def block_levels(rng, dims, split, low, top_value):
    factor_of, own = 1.0, jax.random.fold_in(rng, 6)
    for axis_at, blocks in split:
        steps = jnp.exp(jax.random.uniform(jax.random.fold_in(own, axis_at), (blocks,), jnp.float32, low / len(split), top_value / len(split)))
        factor_of = factor_of * jnp.repeat(steps, dims[axis_at] // blocks).reshape([-1 if axis == axis_at else 1 for axis in range(len(dims))])
    return factor_of


def bell_draw(key, extent, width, bound, split=(), kind=jnp.bfloat16):
    gain = block_levels(key, extent, split, -0.22, 0.18) if split else 1.0
    entries = jax.random.normal(key, extent, jnp.float32) * width * gain
    return jnp.minimum(jnp.maximum(entries, -bound), bound).astype(kind)


def setup_inputs(seed: int = 0) -> dict:
    streams_of = jax.random.split(jax.random.key(seed), 5)
    white_noise = bell_draw(streams_of[0], (EZ, EY, EX), 1.0, 6.0, ((0, 32), (1, 8)), jnp.float32)
    amplitude = draw_amplitude(jax.random.fold_in(streams_of[4], 71), 0)
    recharge = bell_draw(streams_of[2], (AX, AY, AZ), 1.0, 6.0, ((0, 8), (1, 32)), jnp.float32)
    head_guess = bell_draw(streams_of[3], (AX, AY, AZ), 1.0, 6.0, ((0, 8), (1, 32)), jnp.float32)
    return dict(white_noise=white_noise, amplitude=amplitude, recharge=recharge, head_guess=head_guess)


def neighbours(padded):
    return [padded[2:, 1:-1, 1:-1], padded[:-2, 1:-1, 1:-1],
            padded[1:-1, 2:, 1:-1], padded[1:-1, :-2, 1:-1],
            padded[1:-1, 1:-1, 2:], padded[1:-1, 1:-1, :-2]]


def reference(white_noise, amplitude, recharge, head_guess):
    spectrum = jnp.fft.fftn(white_noise)
    amplitude_cube = jnp.transpose(amplitude, (2, 0, 1))
    inverse = jnp.fft.ifftn(spectrum * amplitude_cube)
    log_field = jnp.transpose(jnp.real(inverse)[:AZ, :AY, :AX], (2, 1, 0))
    conductivity = jnp.exp(log_field)
    face_terms = [0.5 * (conductivity + side) for side in neighbours(jnp.pad(conductivity, 1))]
    diagonal = face_terms[0]
    for term in face_terms[1:]:
        diagonal = diagonal + term
    pressure = head_guess
    for sweep_index in range(SWEEPS):
        sides = neighbours(jnp.pad(pressure, 1))
        pushed = face_terms[0] * sides[0]
        for term, side in zip(face_terms[1:], sides[1:]):
            pushed = pushed + term * side
        pressure = (recharge + pushed) / diagonal
    return conductivity, pressure
```

```python
import functools
import math

import jax
import jax.numpy as jnp
import ml_dtypes
import numpy as np
from jax import lax
from jax.experimental import pallas as pl
from jax.experimental.pallas import tpu as pltpu
from jax.sharding import PartitionSpec as P

AX, AY, AZ = 256, 256, 128
EX, EY, EZ = 512, 512, 256
GA, BA = 8, 32
DEVS = GA * BA
PACKED_GA = 4
XROWS = 40
CHUNK = XROWS + 32
VMEM = 48 * 2**20
f32, bf16 = jnp.float32, jnp.bfloat16


def split_np(table):
    high = table.astype(np.float32).astype(ml_dtypes.bfloat16)
    low = (table - high.astype(np.float64)).astype(np.float32).astype(ml_dtypes.bfloat16)
    return np.stack([high, low])


def trig(rows, cols, period):
    angles = (np.outer(rows, cols) % period) * (2.0 * math.pi / period)
    return np.cos(angles), np.sin(angles)


def kx_of():
    ids = np.zeros(DEVS, np.int64)
    for b in range(BA):
        for g in range(GA):
            if b:
                kx = 64 * g + b
            elif g < PACKED_GA:
                kx = 64 * g + 32
            else:
                kx = -1 if g == PACKED_GA else 64 * g
            ids[b * GA + g] = kx
    return ids


@functools.cache
def tables():
    kx = kx_of()
    packed = kx < 0
    alternating = 1.0 - 2.0 * (np.arange(EX) % 2)
    cos, sin = trig(np.maximum(kx, 0), np.arange(EX), EX)
    wide_re, wide_im = cos.copy(), -sin
    wide_re[packed], wide_im[packed] = alternating, 1.0
    x_fwd = np.concatenate([wide_re, wide_im])

    y_fwd = np.stack(trig(np.arange(EY), np.arange(EY), EY))

    half, quarter, block = np.meshgrid(np.arange(2), np.arange(4), np.arange(BA), indexing="ij")
    z_order = (8 * block + 2 * quarter + half).reshape(-1)
    z_fwd = np.concatenate(trig(z_order, np.arange(EZ), EZ), 1)
    z_inv = np.concatenate(trig(np.arange(EZ), np.arange(AZ), EZ), 1)

    cos, sin = trig(np.arange(AY), np.arange(EY), EY)
    y_inv = np.concatenate(
        [np.stack([cos, sin], 1).reshape(2 * AY, EY), np.stack([-sin, cos], 1).reshape(2 * AY, EY)], 1
    )

    xs = np.clip((32 * np.arange(GA)[:, None] - 4 + np.arange(XROWS)).reshape(-1), 0, AX - 1)
    cos, sin = trig(xs, np.maximum(kx, 0), EX)
    back_re, back_im = 2.0 * cos, -2.0 * sin
    back_re[:, packed] = alternating[xs][:, None]
    back_im[:, packed] = 1.0
    x_inv = np.stack([back_re, back_im], 2).reshape(xs.size, 2 * DEVS) / (EX * EY * EZ)
    return tuple(split_np(t) for t in (x_fwd, y_fwd, z_fwd, z_inv, y_inv, x_inv))


def split(value):
    high = value.astype(bf16)
    return high, (value - high.astype(f32)).astype(bf16)


def dot3(a, b, rhs_dim=0):
    dims = (((1,), (rhs_dim,)), ((), ()))
    mul = functools.partial(lax.dot_general, dimension_numbers=dims, preferred_element_type=f32)
    return mul(a[0], b[0]) + (mul(a[0], b[1]) + mul(a[1], b[0]))


def enter_kernel(where, noise, table, amp, head, rech, sent, amp_sent, amp_dc, below, above):
    ga = where[0]
    for part in range(2):
        rows = split(noise[256 * part : 256 * part + 256, :])
        for c in range(2):
            own = slice(256 * c, 256 * c + 256)
            result = dot3((table[0, own, :], table[1, own, :]), rows, 1)
            for q in range(2):
                sent[pl.ds(4 * c + 2 * part + q, DEVS, stride=8), :] = result[:, 128 * q : 128 * q + 128]
    for half in range(2):
        lanes = slice(128 * half, 128 * half + 128)
        first = amp[:, 0, lanes]
        amp_dc[:, lanes] = first
        middle = amp[:, 32, lanes]
        amp_sent[0:16, lanes] = jnp.where(ga < PACKED_GA, middle, first)
        for b in range(1, BA):
            amp_sent[16 * b : 16 * b + 16, lanes] = amp[:, b, lanes]
    for out, near in ((below, (0, 1, 0)), (above, (6, 7, 7))):
        for i, (ref, y) in enumerate(zip((head, head, rech), near)):
            out[32 * i : 32 * i + 32, :] = ref[pl.ds(y, 32, stride=8), :]


def middle_kernel(where, got, amp, amp_dc, y_fwd, z_fwd, z_inv, y_inv, sent, rows, lines):
    low_half = lax.broadcasted_iota(jnp.int32, (BA, 128), 1) < 64
    for c in range(2):
        for q in range(4):
            for p in range(4):
                even = got[pl.ds(16 * p + 4 * c + q, BA, stride=64), :]
                odd = got[pl.ds(16 * p + 8 + 4 * c + q, BA, stride=64), :]
                first = jnp.where(low_half, even, pltpu.roll(odd, 64, 1))
                second = jnp.where(low_half, pltpu.roll(even, 64, 1), odd)
                for half, value in enumerate((first, second)):
                    at = slice(256 * c + 128 * half + 32 * q, 256 * c + 128 * half + 32 * q + 32)
                    high, low = split(value)
                    rows[0, at, 128 * p : 128 * p + 128] = high
                    rows[1, at, 128 * p : 128 * p + 128] = low

    def spectral(amp_ref, keep):
        for part in range(2):
            ky = slice(256 * part, 256 * part + 256)
            data = (rows[0], rows[1])
            by_cos = dot3((y_fwd[0, 0, ky, :], y_fwd[1, 0, ky, :]), data, 1)
            by_sin = dot3((y_fwd[0, 1, ky, :], y_fwd[1, 1, ky, :]), data, 1)
            real = by_cos[:, :256] + by_sin[:, 256:]
            imag = by_cos[:, 256:] - by_sin[:, :256]
            forward = (z_fwd[0], z_fwd[1])
            real, imag = dot3(split(real), forward), dot3(split(imag), forward)
            scale = amp_ref[ky, :]
            new_real = (real[:, :256] + imag[:, 256:]) * scale
            new_imag = (imag[:, :256] - real[:, 256:]) * scale
            back = (z_inv[0], z_inv[1])
            real, imag = dot3(split(new_real), back), dot3(split(new_imag), back)
            for c, value in enumerate((real[:, :128] - imag[:, 128:], imag[:, :128] + real[:, 128:])):
                high, low = split(value)
                at = slice(512 * c + 256 * part, 512 * c + 256 * part + 256)
                lines[0, at, :] = high
                lines[1, at, :] = low

    spectral(amp, None)
    sent[...] = dot3((y_inv[0], y_inv[1]), (lines[0], lines[1]))

    @pl.when(where[1] == 1)
    def _():
        spectral(amp_dc, None)
        other = dot3((y_inv[0], y_inv[1]), (lines[0], lines[1]))
        odd_row = lax.broadcasted_iota(jnp.int32, (2 * AY, AZ), 0) % 2 == 1
        sent[...] = jnp.where(odd_row, other, sent[...])


def field_kernel(where, got, table, head, rech, lo_halo, hi_halo, sent):
    ga = where[0]
    log_field = dot3((table[0], table[1]), split(got[...]))
    row = lax.broadcasted_iota(jnp.int32, (XROWS, AZ), 0)
    corner = lax.broadcasted_iota(jnp.int32, (8, AZ), 0)

    def pack(far, near):
        edges = jnp.where(
            corner == 0, lo_halo[32 + near : 33 + near, :], hi_halo[near : near + 1, :]
        )
        return (head[8 * far : 8 * far + 8, :], head[8 * near : 8 * near + 8, :],
                rech[8 * near : 8 * near + 8, :], edges)

    up, down = pack(30, 31), pack(1, 0)
    for g in range(GA):
        x = row + (32 * g - 4)
        inside = (x >= 0) & (x < AX)
        value = jnp.exp(log_field[XROWS * g : XROWS * g + XROWS, :])
        sent[CHUNK * g : CHUNK * g + XROWS, :] = jnp.where(inside, value, 0.0)
        for i in range(4):
            at = CHUNK * g + XROWS + 8 * i
            sent[at : at + 8, :] = jnp.where(ga + 1 == g, up[i], down[i])


def sweep_kernel(where, got, lo_cond, hi_cond, head, rech, lo_halo, hi_halo, cond_out, press_out,
                 head_ext, rech_ext, staged):
    ga, ba = where[0], where[2]
    head_ext[...] = jnp.zeros_like(head_ext)
    rech_ext[...] = jnp.zeros_like(rech_ext)
    for y in range(8):
        at = XROWS * (y + 2)
        head_ext[at + 4 : at + 36, :] = head[pl.ds(y, 32, stride=8), :]
        rech_ext[at + 4 : at + 36, :] = rech[pl.ds(y, 32, stride=8), :]
    for halo, (first, second, only) in ((lo_halo, (0, 1, 1)), (hi_halo, (10, 11, 10))):
        for ref, y, i in ((head_ext, first, 0), (head_ext, second, 1), (rech_ext, only, 2)):
            ref[XROWS * y + 4 : XROWS * y + 36, :] = halo[32 * i : 32 * i + 32, :]
    for side, peer, present, far, near in (
        (0, jnp.maximum(ga - 1, 0), ga > 0, 2, 3), (1, jnp.minimum(ga + 1, GA - 1), ga < GA - 1, 37, 36)
    ):
        block = got[pl.ds(pl.multiple_of(peer * CHUNK + XROWS, 8), 32), :]
        block = jnp.where(present, block, 0.0)
        for y in range(8):
            at = XROWS * (y + 2)
            head_ext[at + far : at + far + 1, :] = block[y : y + 1, :]
            head_ext[at + near : at + near + 1, :] = block[8 + y : 9 + y, :]
            rech_ext[at + near : at + near + 1, :] = block[16 + y : 17 + y, :]
        head_ext[XROWS + near : XROWS + near + 1, :] = block[24:25, :]
        head_ext[10 * XROWS + near : 10 * XROWS + near + 1, :] = block[25:26, :]

    lane = lax.broadcasted_iota(jnp.int32, (XROWS, AZ), 1)
    row = lax.broadcasted_iota(jnp.int32, (XROWS, AZ), 0)
    x = row + (32 * ga - 4)
    inside_x = (x >= 0) & (x < AX)

    def in_plane(value):
        total = pltpu.roll(value, 1, 0) + pltpu.roll(value, XROWS - 1, 0)
        total = total + jnp.where(lane > 0, pltpu.roll(value, 1, 1), 0.0)
        return total + jnp.where(lane < AZ - 1, pltpu.roll(value, AZ - 1, 1), 0.0)

    cond = [lo_cond[0:XROWS, :], lo_cond[CHUNK : CHUNK + XROWS, :]]
    cond += [got[CHUNK * y : CHUNK * y + XROWS, :] for y in range(8)]
    cond += [hi_cond[0:XROWS, :], hi_cond[CHUNK : CHUNK + XROWS, :]]
    planes = [head_ext[XROWS * y : XROWS * y + XROWS, :] for y in range(12)]
    weight = {y: 6.0 * cond[y] + (in_plane(cond[y]) + (cond[y - 1] + cond[y + 1])) for y in range(1, 11)}
    source = {y: 2.0 * rech_ext[XROWS * y : XROWS * y + XROWS, :] for y in range(1, 11)}
    for sweep in range(2):
        flow = {y: cond[y] * planes[y] for y in range(sweep, 12 - sweep)}
        new = dict()
        for y in range(sweep + 1, 11 - sweep):
            heads = in_plane(planes[y]) + (planes[y - 1] + planes[y + 1])
            flows = in_plane(flow[y]) + (flow[y - 1] + flow[y + 1])
            new[y] = (source[y] + (cond[y] * heads + flows)) / weight[y]
            if sweep == 0:
                inside = inside_x
                if y == 1:
                    inside = inside & (ba > 0)
                if y == 10:
                    inside = inside & (ba < BA - 1)
                new[y] = jnp.where(inside, new[y], 0.0)
        planes = new
    for y in range(8):
        cond_out[pl.ds(y, 32, stride=8), :] = got[CHUNK * y + 4 : CHUNK * y + 36, :]
        staged[...] = planes[y + 2]
        press_out[pl.ds(y, 32, stride=8), :] = staged[4:36, :]


def kernel_call(kernel, outs, inputs, scratch=()):
    vmem = pl.BlockSpec(memory_space=pltpu.VMEM)
    smem = pl.BlockSpec(memory_space=pltpu.SMEM)
    return pl.pallas_call(
        kernel,
        out_shape=[jax.ShapeDtypeStruct(shape, f32) for shape in outs],
        in_specs=[smem] + [vmem] * (len(inputs) - 1),
        out_specs=[vmem] * len(outs),
        scratch_shapes=list(scratch),
        compiler_params=pltpu.CompilerParams(vmem_limit_bytes=VMEM),
    )(*inputs)


def body(noise, amplitude, recharge, head_guess):
    x_fwd, y_fwd, z_fwd, z_inv, y_inv, x_inv = (jnp.asarray(t) for t in tables())
    ga, ba = lax.axis_index("ga"), lax.axis_index("ba")
    packed = ((ga == PACKED_GA) & (ba == 0)).astype(jnp.int32)
    where = jnp.stack([ga.astype(jnp.int32), packed, ba.astype(jnp.int32)])
    noise = noise.reshape(512, EX)
    recharge = recharge.reshape(256, AZ)
    head = head_guess.reshape(256, AZ)
    sent, amp_sent, amp_dc, below, above = kernel_call(
        enter_kernel, [(8 * DEVS, 128), (512, EZ), (16, EZ), (96, AZ), (96, AZ)],
        [where, noise, x_fwd, amplitude, head, recharge],
    )
    up = [(i, i + 1) for i in range(BA - 1)]
    down = [(j, i) for i, j in up]
    hi_halo = lax.ppermute(below, "ba", down)
    lo_halo = lax.ppermute(above, "ba", up)
    amp_dc = lax.ppermute(amp_dc, "ga", [(0, PACKED_GA)])
    amp_dc = lax.all_gather(amp_dc, "ba", axis=0, tiled=True)
    amp_got = lax.all_to_all(amp_sent, "ba", 0, 0, tiled=True)
    got = lax.all_to_all(sent, ("ba", "ga"), 0, 0, tiled=True)
    (sent,) = kernel_call(
        middle_kernel, [(2 * AY, AZ)],
        [where, got, amp_got, amp_dc, y_fwd, z_fwd, z_inv, y_inv],
        [pltpu.VMEM((2, 512, 512), bf16), pltpu.VMEM((2, 1024, AZ), bf16)],
    )
    got = lax.all_to_all(sent, ("ba", "ga"), 0, 0, tiled=True)
    (sent,) = kernel_call(
        field_kernel, [(CHUNK * GA, AZ)], [where, got, x_inv, head, recharge, lo_halo, hi_halo]
    )
    got = lax.all_to_all(sent, "ga", 0, 0, tiled=True)
    lo_cond = lax.ppermute(got[6 * CHUNK :], "ba", up)
    hi_cond = lax.ppermute(got[: 2 * CHUNK], "ba", down)
    ext = pltpu.VMEM((12 * XROWS, AZ), f32)
    conductivity, pressure = kernel_call(
        sweep_kernel, [(256, AZ), (256, AZ)],
        [where, got, lo_cond, hi_cond, head, recharge, lo_halo, hi_halo],
        [ext, ext, pltpu.VMEM((XROWS, AZ), f32)],
    )
    return conductivity.reshape(32, 8, AZ), pressure.reshape(32, 8, AZ)


def solution(mesh):
    placed = (P("ba", "ga", None), P("ba", "ga", None), P("ga", "ba", None), P("ga", "ba", None))
    return jax.shard_map(
        body,
        mesh=mesh,
        in_specs=placed,
        out_specs=(P("ga", "ba", None), P("ga", "ba", None)),
        check_vma=False,
    )
```

```python
import functools
import math

import jax
import jax.numpy as jnp
import ml_dtypes
import numpy as np
from jax import lax
from jax.experimental import pallas as pl
from jax.experimental.pallas import tpu as pltpu
from jax.sharding import PartitionSpec as P

AX, AY, AZ = 256, 256, 128
EX, EY, EZ = 512, 512, 256
GA, BA = 8, 32
DEVS = GA * BA
PACKED_GA = 4
XROWS = 40
CHUNK = XROWS + 32
VMEM = 48 * 2**20
f32, bf16 = jnp.float32, jnp.bfloat16


def split_np(table):
    high = table.astype(np.float32).astype(ml_dtypes.bfloat16)
    low = (table - high.astype(np.float64)).astype(np.float32).astype(ml_dtypes.bfloat16)
    return np.stack([high, low])


def trig(rows, cols, period):
    angles = (np.outer(rows, cols) % period) * (2.0 * math.pi / period)
    return np.cos(angles), np.sin(angles)


def kx_of():
    ids = np.zeros(DEVS, np.int64)
    for b in range(BA):
        for g in range(GA):
            if b:
                kx = 64 * g + b
            elif g < PACKED_GA:
                kx = 64 * g + 32
            else:
                kx = -1 if g == PACKED_GA else 64 * g
            ids[b * GA + g] = kx
    return ids


@functools.cache
def tables():
    kx = kx_of()
    packed = kx < 0
    alternating = 1.0 - 2.0 * (np.arange(EX) % 2)
    cos, sin = trig(np.maximum(kx, 0), np.arange(EX), EX)
    wide_re, wide_im = cos.copy(), -sin
    wide_re[packed], wide_im[packed] = alternating, 1.0
    x_fwd = np.concatenate([wide_re, wide_im])

    y_fwd = np.stack(trig(np.arange(EY), np.arange(EY), EY))

    half, quarter, block = np.meshgrid(np.arange(2), np.arange(4), np.arange(BA), indexing="ij")
    z_order = (8 * block + 2 * quarter + half).reshape(-1)
    z_fwd = np.concatenate(trig(z_order, np.arange(EZ), EZ), 1)
    z_inv = np.concatenate(trig(np.arange(EZ), np.arange(AZ), EZ), 1)

    cos, sin = trig(np.arange(AY), np.arange(EY), EY)
    y_inv = np.concatenate(
        [np.stack([cos, sin], 1).reshape(2 * AY, EY), np.stack([-sin, cos], 1).reshape(2 * AY, EY)], 1
    )

    xs = np.clip((32 * np.arange(GA)[:, None] - 4 + np.arange(XROWS)).reshape(-1), 0, AX - 1)
    cos, sin = trig(xs, np.maximum(kx, 0), EX)
    back_re, back_im = 2.0 * cos, -2.0 * sin
    back_re[:, packed] = alternating[xs][:, None]
    back_im[:, packed] = 1.0
    x_inv = np.stack([back_re, back_im], 2).reshape(xs.size, 2 * DEVS) / (EX * EY * EZ)
    return tuple(split_np(t) for t in (x_fwd, y_fwd, z_fwd, z_inv, y_inv, x_inv))


def split(value):
    high = value.astype(bf16)
    return high, (value - high.astype(f32)).astype(bf16)


def dot3(a, b, rhs_dim=0):
    dims = (((1,), (rhs_dim,)), ((), ()))
    mul = functools.partial(lax.dot_general, dimension_numbers=dims, preferred_element_type=f32)
    return mul(a[0], b[0]) + (mul(a[0], b[1]) + mul(a[1], b[0]))


def fetch(pairs, sems):
    copies = [pltpu.make_async_copy(src, dst, sems.at[i]) for i, (src, dst) in enumerate(pairs)]
    for copy in copies:
        copy.start()
    return copies


def enter_kernel(noise, table, sent, noise_in, table_in, rows_out, sems):
    pairs = [(table, table_in), (noise.at[0:256, :], noise_in.at[0:256, :]),
             (noise.at[256:512, :], noise_in.at[256:512, :])]
    copies = fetch(pairs, sems)
    copies[0].wait()
    for part in range(2):
        copies[1 + part].wait()
        rows = split(noise_in[256 * part : 256 * part + 256, :])
        for c in range(2):
            own = slice(256 * c, 256 * c + 256)
            result = dot3((table_in[0, own, :], table_in[1, own, :]), rows, 1)
            for q in range(2):
                at = pl.ds(4 * c + 2 * part + q, DEVS, stride=8)
                rows_out[at, :] = result[:, 128 * q : 128 * q + 128]
    pltpu.sync_copy(rows_out, sent)


def edges_kernel(where, amp, head, rech, amp_sent, amp_first, below, above, amp_in, head_in, rech_in, sems):
    ga = where[0]
    copies = fetch([(amp.at[:, 0:40, :], amp_in), (head, head_in), (rech, rech_in)], sems)
    for copy in copies:
        copy.wait()
    for half in range(2):
        lanes = slice(128 * half, 128 * half + 128)
        first = amp_in[:, 0, lanes]
        amp_first[:, lanes] = first
        amp_sent[0:16, lanes] = jnp.where(ga < PACKED_GA, amp_in[:, 32, lanes], first)
        for b in range(1, BA):
            amp_sent[16 * b : 16 * b + 16, lanes] = amp_in[:, b, lanes]
    for out, near in ((below, (0, 1, 0)), (above, (6, 7, 7))):
        for i, (ref, y) in enumerate(zip((head_in, head_in, rech_in), near)):
            out[32 * i : 32 * i + 32, :] = ref[pl.ds(y, 32, stride=8), :]


def mirror_of(value):
    ones = []
    for size in value.shape:
        i = lax.broadcasted_iota(jnp.int32, (size, size), 0)
        j = lax.broadcasted_iota(jnp.int32, (size, size), 1)
        ones.append((((i + j) == 0) | ((i + j) == size)).astype(bf16))
    total = None
    for _ in range(3):
        part = value.astype(bf16)
        value = value - part.astype(f32)
        part = jnp.dot(ones[0], part, preferred_element_type=f32).astype(bf16)
        part = jnp.dot(part, ones[1], preferred_element_type=f32)
        total = part if total is None else total + part
    return total


def middle_kernel(where, got, amp, amp_row0, amp_row256, y_fwd, z_fwd, z_inv, y_inv, sent,
                  got_in, amp_in, y_fwd_in, z_fwd_in, z_inv_in, y_inv_in, row0_in, row256_in,
                  rows, lines, amps, sems):
    packed = where[1] == 1
    pairs = [(got, got_in), (y_fwd, y_fwd_in), (z_fwd, z_fwd_in), (amp, amp_in), (z_inv, z_inv_in),
             (y_inv, y_inv_in), (amp_row0, row0_in), (amp_row256, row256_in)]
    copies = fetch(pairs, sems)
    copies[0].wait()
    low_half = lax.broadcasted_iota(jnp.int32, (BA, 128), 1) < 64
    for c in range(2):
        for q in range(4):
            for p in range(4):
                even = got_in[pl.ds(16 * p + 4 * c + q, BA, stride=64), :]
                odd = got_in[pl.ds(16 * p + 8 + 4 * c + q, BA, stride=64), :]
                first = jnp.where(low_half, even, pltpu.roll(odd, 64, 1))
                second = jnp.where(low_half, pltpu.roll(even, 64, 1), odd)
                for half, value in enumerate((first, second)):
                    at = slice(256 * c + 128 * half + 32 * q, 256 * c + 128 * half + 32 * q + 32)
                    high, low = split(value)
                    rows[0, at, 128 * p : 128 * p + 128] = high
                    rows[1, at, 128 * p : 128 * p + 128] = low
    for copy in copies[1:]:
        copy.wait()

    @pl.when(packed)
    def _():
        held = amp_in[...]
        mirror = mirror_of(held)
        ky = lax.broadcasted_iota(jnp.int32, (EY, EZ), 0)
        amps[...] = jnp.where(ky == 0, row0_in[0:1, :], jnp.where(ky < 256, mirror, held))
        amp_in[...] = jnp.where(ky == 256, row256_in[0:1, :], jnp.where(ky < 256, held, mirror))

    for part in range(2):
        ky = slice(256 * part, 256 * part + 256)
        data = (rows[0], rows[1])
        by_cos = dot3((y_fwd_in[0, 0, ky, :], y_fwd_in[1, 0, ky, :]), data, 1)
        by_sin = dot3((y_fwd_in[0, 1, ky, :], y_fwd_in[1, 1, ky, :]), data, 1)
        real = by_cos[:, :256] + by_sin[:, 256:]
        imag = by_cos[:, 256:] - by_sin[:, :256]
        forward = (z_fwd_in[0], z_fwd_in[1])
        real, imag = dot3(split(real), forward), dot3(split(imag), forward)
        real, imag = real[:, :256] + imag[:, 256:], imag[:, :256] - real[:, 256:]

        def back(amp_ref, lanes):
            table = (z_inv_in[0], z_inv_in[1])
            scale = amp_ref[ky, :]
            re, im = dot3(split(real * scale), table), dot3(split(imag * scale), table)
            for c, value in enumerate((re[:, :128] - im[:, 128:], im[:, :128] + re[:, 128:])):
                high, low = split(value)
                at = slice(512 * c + 256 * part, 512 * c + 256 * part + 256)
                lines[0, at, lanes] = high
                lines[1, at, lanes] = low

        back(amp_in, slice(0, 128))

        @pl.when(packed)
        def _():
            back(amps, slice(128, 256))

        @pl.when(jnp.logical_not(packed))
        def _():
            for i in range(2):
                for c in range(2):
                    at = slice(512 * c + 256 * part, 512 * c + 256 * part + 256)
                    lines[i, at, 128:256] = jnp.zeros((256, 128), bf16)

    result = dot3((y_inv_in[0], y_inv_in[1]), (lines[0], lines[1]))
    odd_row = lax.broadcasted_iota(jnp.int32, (2 * AY, AZ), 0) % 2 == 1
    sent[...] = jnp.where(odd_row & packed, result[:, 128:], result[:, :128])


def field_kernel(where, got, table, head, rech, lo_halo, hi_halo, sent):
    ga = where[0]
    log_field = dot3((table[0], table[1]), split(got[...]))
    row = lax.broadcasted_iota(jnp.int32, (XROWS, AZ), 0)
    corner = lax.broadcasted_iota(jnp.int32, (8, AZ), 0)

    def pack(far, near):
        edges = jnp.where(
            corner == 0, lo_halo[32 + near : 33 + near, :], hi_halo[near : near + 1, :]
        )
        return (head[8 * far : 8 * far + 8, :], head[8 * near : 8 * near + 8, :],
                rech[8 * near : 8 * near + 8, :], edges)

    up, down = pack(30, 31), pack(1, 0)
    for g in range(GA):
        x = row + (32 * g - 4)
        inside = (x >= 0) & (x < AX)
        value = jnp.exp(log_field[XROWS * g : XROWS * g + XROWS, :])
        sent[CHUNK * g : CHUNK * g + XROWS, :] = jnp.where(inside, value, 0.0)
        for i in range(4):
            at = CHUNK * g + XROWS + 8 * i
            sent[at : at + 8, :] = jnp.where(ga + 1 == g, up[i], down[i])


def sweep_kernel(where, got, lo_cond, hi_cond, head, rech, lo_halo, hi_halo, cond_out, press_out,
                 head_ext, rech_ext, staged):
    ga, ba = where[0], where[2]
    head_ext[...] = jnp.zeros_like(head_ext)
    rech_ext[...] = jnp.zeros_like(rech_ext)
    for y in range(8):
        at = XROWS * (y + 2)
        head_ext[at + 4 : at + 36, :] = head[pl.ds(y, 32, stride=8), :]
        rech_ext[at + 4 : at + 36, :] = rech[pl.ds(y, 32, stride=8), :]
    for halo, (first, second, only) in ((lo_halo, (0, 1, 1)), (hi_halo, (10, 11, 10))):
        for ref, y, i in ((head_ext, first, 0), (head_ext, second, 1), (rech_ext, only, 2)):
            ref[XROWS * y + 4 : XROWS * y + 36, :] = halo[32 * i : 32 * i + 32, :]
    for side, peer, present, far, near in (
        (0, jnp.maximum(ga - 1, 0), ga > 0, 2, 3), (1, jnp.minimum(ga + 1, GA - 1), ga < GA - 1, 37, 36)
    ):
        block = got[pl.ds(pl.multiple_of(peer * CHUNK + XROWS, 8), 32), :]
        block = jnp.where(present, block, 0.0)
        for y in range(8):
            at = XROWS * (y + 2)
            head_ext[at + far : at + far + 1, :] = block[y : y + 1, :]
            head_ext[at + near : at + near + 1, :] = block[8 + y : 9 + y, :]
            rech_ext[at + near : at + near + 1, :] = block[16 + y : 17 + y, :]
        head_ext[XROWS + near : XROWS + near + 1, :] = block[24:25, :]
        head_ext[10 * XROWS + near : 10 * XROWS + near + 1, :] = block[25:26, :]

    lane = lax.broadcasted_iota(jnp.int32, (XROWS, AZ), 1)
    row = lax.broadcasted_iota(jnp.int32, (XROWS, AZ), 0)
    x = row + (32 * ga - 4)
    inside_x = (x >= 0) & (x < AX)

    def in_plane(value):
        total = pltpu.roll(value, 1, 0) + pltpu.roll(value, XROWS - 1, 0)
        total = total + jnp.where(lane > 0, pltpu.roll(value, 1, 1), 0.0)
        return total + jnp.where(lane < AZ - 1, pltpu.roll(value, AZ - 1, 1), 0.0)

    cond = [lo_cond[0:XROWS, :], lo_cond[CHUNK : CHUNK + XROWS, :]]
    cond += [got[CHUNK * y : CHUNK * y + XROWS, :] for y in range(8)]
    cond += [hi_cond[0:XROWS, :], hi_cond[CHUNK : CHUNK + XROWS, :]]
    planes = [head_ext[XROWS * y : XROWS * y + XROWS, :] for y in range(12)]
    weight = {y: 6.0 * cond[y] + (in_plane(cond[y]) + (cond[y - 1] + cond[y + 1])) for y in range(1, 11)}
    source = {y: 2.0 * rech_ext[XROWS * y : XROWS * y + XROWS, :] for y in range(1, 11)}
    for sweep in range(2):
        flow = {y: cond[y] * planes[y] for y in range(sweep, 12 - sweep)}
        new = dict()
        for y in range(sweep + 1, 11 - sweep):
            heads = in_plane(planes[y]) + (planes[y - 1] + planes[y + 1])
            flows = in_plane(flow[y]) + (flow[y - 1] + flow[y + 1])
            new[y] = (source[y] + (cond[y] * heads + flows)) / weight[y]
            if sweep == 0:
                inside = inside_x
                if y == 1:
                    inside = inside & (ba > 0)
                if y == 10:
                    inside = inside & (ba < BA - 1)
                new[y] = jnp.where(inside, new[y], 0.0)
        planes = new
    for y in range(8):
        cond_out[pl.ds(y, 32, stride=8), :] = got[CHUNK * y + 4 : CHUNK * y + 36, :]
        staged[...] = planes[y + 2]
        press_out[pl.ds(y, 32, stride=8), :] = staged[4:36, :]


def kernel_call(kernel, outs, inputs, scratch=(), held=(), outs_held=()):
    vmem = pl.BlockSpec(memory_space=pltpu.VMEM)
    smem = pl.BlockSpec(memory_space=pltpu.SMEM)
    there = pl.BlockSpec(memory_space=pl.ANY)

    def spec(i, value):
        if value.dtype == jnp.int32:
            return smem
        return there if i in held else vmem

    return pl.pallas_call(
        kernel,
        out_shape=[jax.ShapeDtypeStruct(shape, f32) for shape in outs],
        in_specs=[spec(i, value) for i, value in enumerate(inputs)],
        out_specs=[there if i in outs_held else vmem for i in range(len(outs))],
        scratch_shapes=list(scratch),
        compiler_params=pltpu.CompilerParams(vmem_limit_bytes=VMEM),
    )(*inputs)


def body(noise, amplitude, recharge, head_guess):
    x_fwd, y_fwd, z_fwd, z_inv, y_inv, x_inv = (jnp.asarray(t) for t in tables())
    ga, ba = lax.axis_index("ga"), lax.axis_index("ba")
    packed = ((ga == PACKED_GA) & (ba == 0)).astype(jnp.int32)
    where = jnp.stack([ga.astype(jnp.int32), packed, ba.astype(jnp.int32)])
    recharge = recharge.reshape(256, AZ)
    head = head_guess.reshape(256, AZ)
    memory, sems = pltpu.VMEM, pltpu.SemaphoreType.DMA
    (sent,) = kernel_call(
        enter_kernel, [(8 * DEVS, 128)], [noise.reshape(512, EX), x_fwd],
        [memory((512, EX), f32), memory(x_fwd.shape, bf16), memory((8 * DEVS, 128), f32), sems((3,))],
        held=(0, 1), outs_held=(0,),
    )
    got = lax.all_to_all(sent, ("ba", "ga"), 0, 0, tiled=True)
    amp_sent, amp_first, below, above = kernel_call(
        edges_kernel, [(512, EZ), (16, EZ), (96, AZ), (96, AZ)], [where, amplitude, head, recharge],
        [memory((16, 40, EZ), f32), memory((256, AZ), f32), memory((256, AZ), f32), sems((3,))],
        held=(1, 2, 3),
    )
    up = [(i, i + 1) for i in range(BA - 1)]
    down = [(j, i) for i, j in up]
    hi_halo = lax.ppermute(below, "ba", down)
    lo_halo = lax.ppermute(above, "ba", up)
    amp_zero = lax.ppermute(amp_first, "ga", [(0, PACKED_GA)])
    amp_row = lax.ppermute(amp_first, "ba", [(BA // 2, 0)])
    swap = (ga == PACKED_GA) & (ba >= BA // 2)
    amp_sent = amp_sent.at[:16].set(jnp.where(swap, amp_zero, amp_sent[:16]))
    amp_got = lax.all_to_all(amp_sent, "ba", 0, 0, tiled=True)
    inputs = [where, got, amp_got, amp_zero, amp_row, y_fwd, z_fwd, z_inv, y_inv]
    (sent,) = kernel_call(
        middle_kernel, [(2 * AY, AZ)], inputs,
        [memory(value.shape, value.dtype) for value in (got, amp_got, y_fwd, z_fwd, z_inv, y_inv, amp_zero, amp_row)]
        + [memory((2, 512, 512), bf16), memory((2, 1024, 2 * AZ), bf16), memory((EY, EZ), f32), sems((8,))],
        held=range(1, 9),
    )
    got = lax.all_to_all(sent, ("ba", "ga"), 0, 0, tiled=True)
    (sent,) = kernel_call(
        field_kernel, [(CHUNK * GA, AZ)], [where, got, x_inv, head, recharge, lo_halo, hi_halo]
    )
    got = lax.all_to_all(sent, "ga", 0, 0, tiled=True)
    lo_cond = lax.ppermute(got[6 * CHUNK :], "ba", up)
    hi_cond = lax.ppermute(got[: 2 * CHUNK], "ba", down)
    ext = pltpu.VMEM((12 * XROWS, AZ), f32)
    conductivity, pressure = kernel_call(
        sweep_kernel, [(256, AZ), (256, AZ)],
        [where, got, lo_cond, hi_cond, head, recharge, lo_halo, hi_halo],
        [ext, ext, pltpu.VMEM((XROWS, AZ), f32)],
    )
    return conductivity.reshape(32, 8, AZ), pressure.reshape(32, 8, AZ)


def solution(mesh):
    placed = (P("ba", "ga", None), P("ba", "ga", None), P("ga", "ba", None), P("ga", "ba", None))
    return jax.shard_map(
        body,
        mesh=mesh,
        in_specs=placed,
        out_specs=(P("ga", "ba", None), P("ga", "ba", None)),
        check_vma=False,
    )
```

```python
import functools
import math

import jax
import jax.numpy as jnp
import ml_dtypes
import numpy as np
from jax import lax
from jax.experimental import pallas as pl
from jax.experimental.pallas import tpu as pltpu
from jax.sharding import PartitionSpec as P

AX, AY, AZ = 256, 256, 128
EX, EY, EZ = 512, 512, 256
GA, BA = 8, 32
DEVS = GA * BA
PACKED_GA = 4
XROWS = 40
CHUNK = 2 * XROWS
VMEM = 60 * 2**20
f32, bf16 = jnp.float32, jnp.bfloat16


def split_np(table):
    high = table.astype(np.float32).astype(ml_dtypes.bfloat16)
    low = (table - high.astype(np.float64)).astype(np.float32).astype(ml_dtypes.bfloat16)
    return np.stack([high, low])


def trig(rows, cols, period):
    angles = (np.outer(rows, cols) % period) * (2.0 * math.pi / period)
    return np.cos(angles), np.sin(angles)


def kx_of():
    ids = np.zeros(DEVS, np.int64)
    for b in range(BA):
        for g in range(GA):
            if b:
                kx = 64 * g + b
            elif g < PACKED_GA:
                kx = 64 * g + 32
            else:
                kx = -1 if g == PACKED_GA else 64 * g
            ids[b * GA + g] = kx
    return ids


@functools.cache
def tables():
    kx = kx_of()
    packed = kx < 0
    alternating = 1.0 - 2.0 * (np.arange(EX) % 2)
    cos, sin = trig(np.maximum(kx, 0), np.arange(EX), EX)
    wide_re, wide_im = cos.copy(), -sin
    wide_re[packed], wide_im[packed] = alternating, 1.0
    x_fwd = np.concatenate([wide_re, wide_im])

    y_fwd = np.stack(trig(np.arange(EY), np.arange(EY), EY))

    half, quarter, block = np.meshgrid(np.arange(2), np.arange(4), np.arange(BA), indexing="ij")
    z_order = (8 * block + 2 * quarter + half).reshape(-1)
    z_fwd = np.concatenate(trig(z_order, np.arange(EZ), EZ), 1)
    z_inv = np.concatenate(trig(np.arange(EZ), np.arange(AZ), EZ), 1)

    cos, sin = trig(np.arange(AY), np.arange(EY), EY)
    y_inv = np.concatenate(
        [np.concatenate([cos, sin]), np.concatenate([-sin, cos])], 1
    )

    xs = np.clip((32 * np.arange(GA)[:, None] - 4 + np.arange(XROWS)).reshape(-1), 0, AX - 1)
    cos, sin = trig(xs, np.maximum(kx, 0), EX)
    back_re, back_im = 2.0 * cos, -2.0 * sin
    back_re[:, packed] = alternating[xs][:, None]
    back_im[:, packed] = 1.0
    x_inv = np.concatenate([back_re, back_im], 1) / (EX * EY * EZ)
    return tuple(split_np(t) for t in (x_fwd, y_fwd, z_fwd, z_inv, y_inv, x_inv))


def split(value):
    high = value.astype(bf16)
    return high, (value - high.astype(f32)).astype(bf16)


def dot3(a, b, rhs_dim=0):
    dims = (((1,), (rhs_dim,)), ((), ()))
    mul = functools.partial(lax.dot_general, dimension_numbers=dims, preferred_element_type=f32)
    return mul(a[0], b[0]) + (mul(a[0], b[1]) + mul(a[1], b[0]))


def fetch(pairs, sems):
    copies = [pltpu.make_async_copy(src, dst, sems.at[i]) for i, (src, dst) in enumerate(pairs)]
    for copy in copies:
        copy.start()
    return copies


def enter_kernel(noise, table, sent, noise_in, table_in, rows_out, sems):
    pairs = [(table, table_in), (noise.at[0:256, :], noise_in.at[0:256, :]),
             (noise.at[256:512, :], noise_in.at[256:512, :])]
    copies = fetch(pairs, sems)
    copies[0].wait()
    for part in range(2):
        copies[1 + part].wait()
        rows = split(noise_in[256 * part : 256 * part + 256, :])
        for c in range(2):
            own = slice(256 * c, 256 * c + 256)
            result = dot3((table_in[0, own, :], table_in[1, own, :]), rows, 1)
            for q in range(2):
                at = pl.ds(4 * c + 2 * part + q, DEVS, stride=8)
                rows_out[at, :] = result[:, 128 * q : 128 * q + 128]
    pltpu.sync_copy(rows_out, sent)


def edges_kernel(where, amp, head, rech, amp_sent, amp_first, below, above, amp_in, head_in, rech_in, sems):
    ga = where[0]
    copies = fetch([(amp.at[:, 0:40, :], amp_in), (head, head_in), (rech, rech_in)], sems)
    for copy in copies:
        copy.wait()
    for half in range(2):
        lanes = slice(128 * half, 128 * half + 128)
        first = amp_in[:, 0, lanes]
        amp_first[:, lanes] = first
        amp_sent[0:16, lanes] = jnp.where(ga < PACKED_GA, amp_in[:, 32, lanes], first)
        for b in range(1, BA):
            amp_sent[16 * b : 16 * b + 16, lanes] = amp_in[:, b, lanes]
    for out, near in ((below, (0, 1, 0)), (above, (6, 7, 7))):
        for i, (ref, y) in enumerate(zip((head_in, head_in, rech_in), near)):
            out[32 * i : 32 * i + 32, :] = ref[pl.ds(y, 32, stride=8), :]


def mirror_of(value):
    ones = []
    for size in value.shape:
        i = lax.broadcasted_iota(jnp.int32, (size, size), 0)
        j = lax.broadcasted_iota(jnp.int32, (size, size), 1)
        ones.append((((i + j) == 0) | ((i + j) == size)).astype(bf16))
    total = None
    for _ in range(3):
        part = value.astype(bf16)
        value = value - part.astype(f32)
        part = jnp.dot(ones[0], part, preferred_element_type=f32).astype(bf16)
        part = jnp.dot(part, ones[1], preferred_element_type=f32)
        total = part if total is None else total + part
    return total


def middle_kernel(where, got, amp, amp_row0, amp_row256, y_fwd, z_fwd, z_inv, y_inv, up, down, sent,
                  got_in, amp_in, y_fwd_in, z_fwd_in, z_inv_in, y_inv_in, row0_in, row256_in,
                  rows, lines, amps, sems):
    packed = where[1] == 1
    pairs = [(got, got_in), (y_fwd, y_fwd_in), (z_fwd, z_fwd_in), (amp, amp_in), (z_inv, z_inv_in),
             (y_inv, y_inv_in), (amp_row0, row0_in), (amp_row256, row256_in)]
    copies = fetch(pairs, sems)
    copies[0].wait()
    low_half = lax.broadcasted_iota(jnp.int32, (BA, 128), 1) < 64
    for c in range(2):
        for q in range(4):
            for p in range(4):
                even = got_in[pl.ds(16 * p + 4 * c + q, BA, stride=64), :]
                odd = got_in[pl.ds(16 * p + 8 + 4 * c + q, BA, stride=64), :]
                first = jnp.where(low_half, even, pltpu.roll(odd, 64, 1))
                second = jnp.where(low_half, pltpu.roll(even, 64, 1), odd)
                for half, value in enumerate((first, second)):
                    at = slice(256 * c + 128 * half + 32 * q, 256 * c + 128 * half + 32 * q + 32)
                    high, low = split(value)
                    rows[0, at, 128 * p : 128 * p + 128] = high
                    rows[1, at, 128 * p : 128 * p + 128] = low
    copies[3].wait()
    copies[6].wait()
    copies[7].wait()

    @pl.when(packed)
    def _():
        held = amp_in[...]
        mirror = mirror_of(held)
        ky = lax.broadcasted_iota(jnp.int32, (EY, EZ), 0)
        amps[...] = jnp.where(ky == 0, row0_in[0:1, :], jnp.where(ky < 256, mirror, held))
        amp_in[...] = jnp.where(ky == 256, row256_in[0:1, :], jnp.where(ky < 256, held, mirror))

    for part in range(2):
        ky = slice(256 * part, 256 * part + 256)
        data = (rows[0], rows[1])
        if part == 0:
            copies[1].wait()
        by_cos = dot3((y_fwd_in[0, 0, ky, :], y_fwd_in[1, 0, ky, :]), data, 1)
        by_sin = dot3((y_fwd_in[0, 1, ky, :], y_fwd_in[1, 1, ky, :]), data, 1)
        real = by_cos[:, :256] + by_sin[:, 256:]
        imag = by_cos[:, 256:] - by_sin[:, :256]
        if part == 0:
            copies[2].wait()
            copies[4].wait()
        forward = (z_fwd_in[0], z_fwd_in[1])
        real, imag = dot3(split(real), forward), dot3(split(imag), forward)
        real, imag = real[:, :256] + imag[:, 256:], imag[:, :256] - real[:, 256:]

        def back(amp_ref, lanes):
            table = (z_inv_in[0], z_inv_in[1])
            scale = amp_ref[ky, :]
            re, im = dot3(split(real * scale), table), dot3(split(imag * scale), table)
            for c, value in enumerate((re[:, :128] - im[:, 128:], im[:, :128] + re[:, 128:])):
                high, low = split(value)
                at = slice(512 * c + 256 * part, 512 * c + 256 * part + 256)
                lines[0, at, lanes] = high
                lines[1, at, lanes] = low

        back(amp_in, slice(0, 128))

        @pl.when(packed)
        def _():
            back(amps, slice(128, 256))

        @pl.when(jnp.logical_not(packed))
        def _():
            for i in range(2):
                for c in range(2):
                    at = slice(512 * c + 256 * part, 512 * c + 256 * part + 256)
                    lines[i, at, 128:256] = jnp.zeros((256, 128), bf16)

    copies[5].wait()
    result = dot3((y_inv_in[0], y_inv_in[1]), (lines[0], lines[1]))
    forward_halo = lax.broadcasted_iota(jnp.int32, (AY, AZ), 0) % GA < GA // 2
    for c in range(2):
        own = result[AY * c : AY * c + AY, :AZ]
        if c == 1:
            own = jnp.where(packed, result[AY:, AZ:], own)
        after = jnp.concatenate([own[GA:], own[:GA]], 0)
        before = jnp.concatenate([own[AY - GA :], own[: AY - GA]], 0)
        sent[pl.ds(c, AY, stride=4), :] = own
        sent[pl.ds(2 + c, AY, stride=4), :] = jnp.where(forward_halo, after, before)


def pack_kernel(head, rech, lo_halo, hi_halo, up, down):
    corner = lax.broadcasted_iota(jnp.int32, (8, AZ), 0)
    for out, far, near in ((up, 30, 31), (down, 1, 0)):
        out[0:8, :] = head[8 * far : 8 * far + 8, :]
        out[8:16, :] = head[8 * near : 8 * near + 8, :]
        out[16:24, :] = rech[8 * near : 8 * near + 8, :]
        before, after = lo_halo[32 + near : 33 + near, :], hi_halo[near : near + 1, :]
        out[24:32, :] = jnp.where(corner == 0, before, after)


def field_kernel(where, got, table, lo_x, hi_x, sent):
    ga, ba = where[0], where[2]
    own = jnp.concatenate([got[pl.ds(c, DEVS, stride=4), :] for c in range(2)], 0)
    halo = jnp.concatenate([got[pl.ds(2 + c, DEVS, stride=4), :] for c in range(2)], 0)
    log_field = dot3((table[0], table[1]), split(jnp.concatenate([own, halo], 1)))
    row = lax.broadcasted_iota(jnp.int32, (XROWS, AZ), 0)
    halo_inside = jnp.where(ga < GA // 2, ba < BA - 1, ba > 0)
    for g in range(GA):
        x = row + (32 * g - 4)
        inside = (x >= 0) & (x < AX)
        value = jnp.exp(log_field[XROWS * g : XROWS * g + XROWS, :])
        sent[CHUNK * g : CHUNK * g + XROWS, :] = jnp.where(inside, value[:, :AZ], 0.0)
        beside = jnp.where(inside & halo_inside, value[:, AZ:], 0.0)
        sent[CHUNK * g + XROWS : CHUNK * g + CHUNK, :] = beside


def sweep_kernel(where, got, head, rech, lo_halo, hi_halo, lo_x, hi_x, cond_out, press_out,
                 head_ext, rech_ext, staged):
    ga, ba = where[0], where[2]
    head_ext[...] = jnp.zeros_like(head_ext)
    rech_ext[...] = jnp.zeros_like(rech_ext)
    for y in range(8):
        at = XROWS * (y + 2)
        head_ext[at + 4 : at + 36, :] = head[pl.ds(y, 32, stride=8), :]
        rech_ext[at + 4 : at + 36, :] = rech[pl.ds(y, 32, stride=8), :]
    for halo, (first, second, only) in ((lo_halo, (0, 1, 1)), (hi_halo, (10, 11, 10))):
        for ref, y, i in ((head_ext, first, 0), (head_ext, second, 1), (rech_ext, only, 2)):
            ref[XROWS * y + 4 : XROWS * y + 36, :] = halo[32 * i : 32 * i + 32, :]
    for block, far, near in ((lo_x, 2, 3), (hi_x, 37, 36)):
        for y in range(8):
            at = XROWS * (y + 2)
            head_ext[at + far : at + far + 1, :] = block[y : y + 1, :]
            head_ext[at + near : at + near + 1, :] = block[8 + y : 9 + y, :]
            rech_ext[at + near : at + near + 1, :] = block[16 + y : 17 + y, :]
        head_ext[XROWS + near : XROWS + near + 1, :] = block[24:25, :]
        head_ext[10 * XROWS + near : 10 * XROWS + near + 1, :] = block[25:26, :]

    lane = lax.broadcasted_iota(jnp.int32, (XROWS, AZ), 1)
    row = lax.broadcasted_iota(jnp.int32, (XROWS, AZ), 0)
    x = row + (32 * ga - 4)
    inside_x = (x >= 0) & (x < AX)

    def in_plane(value):
        total = pltpu.roll(value, 1, 0) + pltpu.roll(value, XROWS - 1, 0)
        total = total + jnp.where(lane > 0, pltpu.roll(value, 1, 1), 0.0)
        return total + jnp.where(lane < AZ - 1, pltpu.roll(value, AZ - 1, 1), 0.0)

    beside = {y: got[CHUNK * y + XROWS : CHUNK * y + CHUNK, :] for y in (0, 1, 6, 7)}
    cond = [beside[6], beside[7]]
    cond += [got[CHUNK * y : CHUNK * y + XROWS, :] for y in range(8)]
    cond += [beside[0], beside[1]]
    planes = [head_ext[XROWS * y : XROWS * y + XROWS, :] for y in range(12)]
    weight = {y: 6.0 * cond[y] + (in_plane(cond[y]) + (cond[y - 1] + cond[y + 1])) for y in range(1, 11)}
    source = {y: 2.0 * rech_ext[XROWS * y : XROWS * y + XROWS, :] for y in range(1, 11)}
    for sweep in range(2):
        flow = {y: cond[y] * planes[y] for y in range(sweep, 12 - sweep)}
        new = dict()
        for y in range(sweep + 1, 11 - sweep):
            heads = in_plane(planes[y]) + (planes[y - 1] + planes[y + 1])
            flows = in_plane(flow[y]) + (flow[y - 1] + flow[y + 1])
            new[y] = (source[y] + (cond[y] * heads + flows)) / weight[y]
            if sweep == 0:
                inside = inside_x
                if y == 1:
                    inside = inside & (ba > 0)
                if y == 10:
                    inside = inside & (ba < BA - 1)
                new[y] = jnp.where(inside, new[y], 0.0)
        planes = new
    for y in range(8):
        cond_out[pl.ds(y, 32, stride=8), :] = got[CHUNK * y + 4 : CHUNK * y + 36, :]
        staged[...] = planes[y + 2]
        press_out[pl.ds(y, 32, stride=8), :] = staged[4:36, :]


def kernel_call(kernel, outs, inputs, scratch=(), held=(), outs_held=()):
    vmem = pl.BlockSpec(memory_space=pltpu.VMEM)
    smem = pl.BlockSpec(memory_space=pltpu.SMEM)
    there = pl.BlockSpec(memory_space=pl.ANY)

    def spec(i, value):
        if value.dtype == jnp.int32:
            return smem
        return there if i in held else vmem

    return pl.pallas_call(
        kernel,
        out_shape=[jax.ShapeDtypeStruct(shape, f32) for shape in outs],
        in_specs=[spec(i, value) for i, value in enumerate(inputs)],
        out_specs=[there if i in outs_held else vmem for i in range(len(outs))],
        scratch_shapes=list(scratch),
        compiler_params=pltpu.CompilerParams(vmem_limit_bytes=VMEM),
    )(*inputs)


def body(noise, amplitude, recharge, head_guess):
    x_fwd, y_fwd, z_fwd, z_inv, y_inv, x_inv = (jnp.asarray(t) for t in tables())
    ga, ba = lax.axis_index("ga"), lax.axis_index("ba")
    packed = ((ga == PACKED_GA) & (ba == 0)).astype(jnp.int32)
    where = jnp.stack([ga.astype(jnp.int32), packed, ba.astype(jnp.int32)])
    recharge = recharge.reshape(256, AZ)
    head = head_guess.reshape(256, AZ)
    memory, sems = pltpu.VMEM, pltpu.SemaphoreType.DMA
    (sent,) = kernel_call(
        enter_kernel, [(8 * DEVS, 128)], [noise.reshape(512, EX), x_fwd],
        [memory((512, EX), f32), memory(x_fwd.shape, bf16), memory((8 * DEVS, 128), f32), sems((3,))],
        held=(0, 1), outs_held=(0,),
    )
    got = lax.all_to_all(sent, ("ba", "ga"), 0, 0, tiled=True)
    amp_sent, amp_first, below, above = kernel_call(
        edges_kernel, [(512, EZ), (16, EZ), (96, AZ), (96, AZ)], [where, amplitude, head, recharge],
        [memory((16, 40, EZ), f32), memory((256, AZ), f32), memory((256, AZ), f32), sems((3,))],
        held=(1, 2, 3),
    )
    up = [(i, i + 1) for i in range(BA - 1)]
    down = [(j, i) for i, j in up]
    hi_halo = lax.ppermute(below, "ba", down)
    lo_halo = lax.ppermute(above, "ba", up)
    amp_zero = lax.ppermute(amp_first, "ga", [(0, PACKED_GA)])
    amp_row = lax.ppermute(amp_first, "ba", [(BA // 2, 0)])
    swap = (ga == PACKED_GA) & (ba >= BA // 2)
    amp_sent = amp_sent.at[:16].set(jnp.where(swap, amp_zero, amp_sent[:16]))
    amp_got = lax.all_to_all(amp_sent, "ba", 0, 0, tiled=True)
    to_up, to_down = kernel_call(pack_kernel, [(32, AZ), (32, AZ)], [head, recharge, lo_halo, hi_halo])
    inputs = [where, got, amp_got, amp_zero, amp_row, y_fwd, z_fwd, z_inv, y_inv, to_up, to_down]
    (sent,) = kernel_call(
        middle_kernel, [(4 * AY, AZ)], inputs,
        [memory(value.shape, value.dtype) for value in (got, amp_got, y_fwd, z_fwd, z_inv, y_inv, amp_zero, amp_row)]
        + [memory((2, 512, 512), bf16), memory((2, 1024, 2 * AZ), bf16), memory((EY, EZ), f32), sems((8,))],
        held=range(1, 11),
    )
    got = lax.all_to_all(sent, ("ba", "ga"), 0, 0, tiled=True)
    lo_x = lax.ppermute(to_up, "ga", [(i, i + 1) for i in range(GA - 1)])
    hi_x = lax.ppermute(to_down, "ga", [(i + 1, i) for i in range(GA - 1)])
    (sent,) = kernel_call(field_kernel, [(CHUNK * GA, AZ)], [where, got, x_inv, lo_x, hi_x], held=(3, 4))
    got = lax.all_to_all(sent, "ga", 0, 0, tiled=True)
    ext = pltpu.VMEM((12 * XROWS, AZ), f32)
    conductivity, pressure = kernel_call(
        sweep_kernel, [(256, AZ), (256, AZ)],
        [where, got, head, recharge, lo_halo, hi_halo, lo_x, hi_x],
        [ext, ext, pltpu.VMEM((XROWS, AZ), f32)],
    )
    return conductivity.reshape(32, 8, AZ), pressure.reshape(32, 8, AZ)


def solution(mesh):
    placed = (P("ba", "ga", None), P("ba", "ga", None), P("ga", "ba", None), P("ga", "ba", None))
    return jax.shard_map(
        body,
        mesh=mesh,
        in_specs=placed,
        out_specs=(P("ga", "ba", None), P("ga", "ba", None)),
        check_vma=False,
    )
```

```python
import functools
import math

import jax
import jax.numpy as jnp
import ml_dtypes
import numpy as np
from jax import lax
from jax.experimental import pallas as pl
from jax.experimental.pallas import tpu as pltpu
from jax.sharding import PartitionSpec as P

AX, AY, AZ = 256, 256, 128
EX, EY, EZ = 512, 512, 256
GA, BA = 8, 32
DEVS = GA * BA
PACKED_GA = 4
XROWS = 40
CHUNK = 2 * XROWS
VMEM = 60 * 2**20
f32, bf16 = jnp.float32, jnp.bfloat16


def split_np(table):
    high = table.astype(np.float32).astype(ml_dtypes.bfloat16)
    low = (table - high.astype(np.float64)).astype(np.float32).astype(ml_dtypes.bfloat16)
    return np.stack([high, low])


def trig(rows, cols, period):
    angles = (np.outer(rows, cols) % period) * (2.0 * math.pi / period)
    return np.cos(angles), np.sin(angles)


def kx_of():
    ids = np.zeros(DEVS, np.int64)
    for b in range(BA):
        for g in range(GA):
            if b:
                kx = 64 * g + b
            elif g < PACKED_GA:
                kx = 64 * g + 32
            else:
                kx = -1 if g == PACKED_GA else 64 * g
            ids[b * GA + g] = kx
    return ids


@functools.cache
def tables():
    kx = kx_of()
    packed = kx < 0
    alternating = 1.0 - 2.0 * (np.arange(EX) % 2)
    cos, sin = trig(np.maximum(kx, 0), np.arange(EX), EX)
    wide_re, wide_im = cos.copy(), -sin
    wide_re[packed], wide_im[packed] = alternating, 1.0
    x_fwd = np.concatenate([wide_re, wide_im])

    y_fwd = np.stack(trig(np.arange(EY), np.arange(EY), EY))

    half, quarter, block = np.meshgrid(np.arange(2), np.arange(4), np.arange(BA), indexing="ij")
    z_order = (8 * block + 2 * quarter + half).reshape(-1)
    z_fwd = np.concatenate(trig(z_order, np.arange(EZ), EZ), 1)
    z_inv = np.concatenate(trig(np.arange(EZ), np.arange(AZ), EZ), 1)

    xs = np.clip((32 * np.arange(GA)[:, None] - 4 + np.arange(XROWS)).reshape(-1), 0, AX - 1)
    cos, sin = trig(xs, np.maximum(kx, 0), EX)
    back_re, back_im = 2.0 * cos, -2.0 * sin
    back_re[:, packed] = alternating[xs][:, None]
    back_im[:, packed] = 1.0
    x_inv = np.concatenate([back_re, back_im], 1) / (EX * EY * EZ)
    return tuple(split_np(t) for t in (x_fwd, y_fwd, z_fwd, z_inv, x_inv))


def split(value):
    high = value.astype(bf16)
    return high, (value - high.astype(f32)).astype(bf16)


def dot3(a, b, rhs_dim=0):
    dims = (((1,), (rhs_dim,)), ((), ()))
    mul = functools.partial(lax.dot_general, dimension_numbers=dims, preferred_element_type=f32)
    return mul(a[0], b[0]) + (mul(a[0], b[1]) + mul(a[1], b[0]))


def fetch(pairs, sems):
    copies = [pltpu.make_async_copy(src, dst, sems.at[i]) for i, (src, dst) in enumerate(pairs)]
    for copy in copies:
        copy.start()
    return copies


def enter_kernel(noise, table, sent, noise_in, table_in, rows_out, sems):
    pairs = [(table, table_in), (noise.at[0:256, :], noise_in.at[0:256, :]),
             (noise.at[256:512, :], noise_in.at[256:512, :])]
    copies = fetch(pairs, sems)
    copies[0].wait()
    for part in range(2):
        copies[1 + part].wait()
        rows = split(noise_in[256 * part : 256 * part + 256, :])
        for c in range(2):
            own = slice(256 * c, 256 * c + 256)
            result = dot3((table_in[0, own, :], table_in[1, own, :]), rows, 1)
            for q in range(2):
                at = pl.ds(4 * c + 2 * part + q, DEVS, stride=8)
                rows_out[at, :] = result[:, 128 * q : 128 * q + 128]
    pltpu.sync_copy(rows_out, sent)


def edges_kernel(amp, amp_first, amp_zero, head, rech, amp_sent, up, down, amp_in, sems):
    ga, ba = lax.axis_index("ga"), lax.axis_index("ba")
    (copy,) = fetch([(amp.at[:, 0:40, :], amp_in)], sems)
    for out, far, near in ((up, 30, 31), (down, 1, 0)):
        out[0:8, :] = head[8 * far : 8 * far + 8, :]
        out[8:16, :] = head[8 * near : 8 * near + 8, :]
        out[16:24, :] = rech[8 * near : 8 * near + 8, :]
    copy.wait()
    zero = (ga == PACKED_GA) & (ba >= BA // 2)
    for half in range(2):
        lanes = slice(128 * half, 128 * half + 128)
        first = jnp.where(zero, amp_zero[:, lanes], amp_first[:, lanes])
        amp_sent[0:16, lanes] = jnp.where(ga < PACKED_GA, amp_in[:, 32, lanes], first)
        for b in range(1, BA):
            amp_sent[16 * b : 16 * b + 16, lanes] = amp_in[:, b, lanes]


def mirror_of(value):
    ones = []
    for size in value.shape:
        i = lax.broadcasted_iota(jnp.int32, (size, size), 0)
        j = lax.broadcasted_iota(jnp.int32, (size, size), 1)
        ones.append((((i + j) == 0) | ((i + j) == size)).astype(bf16))
    total = None
    for _ in range(3):
        part = value.astype(bf16)
        value = value - part.astype(f32)
        part = jnp.dot(ones[0], part, preferred_element_type=f32).astype(bf16)
        part = jnp.dot(part, ones[1], preferred_element_type=f32)
        total = part if total is None else total + part
    return total


def middle_kernel(got, amp_near, amp_far, amp_row0, amp_row256, y_fwd, z_fwd, z_inv, below, above, sent,
                  got_in, amp_in, y_fwd_in, z_fwd_in, z_inv_in, row0_in, row256_in,
                  rows, lines, amps, sems):
    ga, ba = lax.axis_index("ga"), lax.axis_index("ba")
    packed = (ga == PACKED_GA) & (ba == 0)
    side = lax.rem(ba, 2)
    pairs = [(got, got_in), (y_fwd, y_fwd_in), (z_fwd, z_fwd_in), (amp_near.at[:, side], amp_in.at[:, side]),
             (amp_far, amp_in.at[:, 1 - side]), (z_inv, z_inv_in), (amp_row0, row0_in), (amp_row256, row256_in)]
    copies = fetch(pairs, sems)
    copies[0].wait()
    low_half = lax.broadcasted_iota(jnp.int32, (BA, 128), 1) < 64
    for c in range(2):
        for q in range(4):
            for p in range(4):
                even = got_in[pl.ds(16 * p + 4 * c + q, BA, stride=64), :]
                odd = got_in[pl.ds(16 * p + 8 + 4 * c + q, BA, stride=64), :]
                first = jnp.where(low_half, even, pltpu.roll(odd, 64, 1))
                second = jnp.where(low_half, pltpu.roll(even, 64, 1), odd)
                for half, value in enumerate((first, second)):
                    at = slice(256 * c + 128 * half + 32 * q, 256 * c + 128 * half + 32 * q + 32)
                    high, low = split(value)
                    rows[0, at, 128 * p : 128 * p + 128] = high
                    rows[1, at, 128 * p : 128 * p + 128] = low
    for i in (3, 4, 6, 7):
        copies[i].wait()

    @pl.when(packed)
    def _():
        held = amp_in[...].reshape(EY, EZ)
        mirror = mirror_of(held)
        ky = lax.broadcasted_iota(jnp.int32, (EY, EZ), 0)
        amps[...] = jnp.where(ky == 0, row0_in[0:1, :], jnp.where(ky < 256, mirror, held))
        new = jnp.where(ky == 256, row256_in[0:1, :], jnp.where(ky < 256, held, mirror))
        amp_in[...] = new.reshape(amp_in.shape)

    for part in range(2):
        ky = slice(256 * part, 256 * part + 256)
        data = (rows[0], rows[1])
        if part == 0:
            copies[1].wait()
        by_cos = dot3((y_fwd_in[0, 0, ky, :], y_fwd_in[1, 0, ky, :]), data, 1)
        by_sin = dot3((y_fwd_in[0, 1, ky, :], y_fwd_in[1, 1, ky, :]), data, 1)
        real = by_cos[:, :256] + by_sin[:, 256:]
        imag = by_cos[:, 256:] - by_sin[:, :256]
        if part == 0:
            copies[2].wait()
            copies[5].wait()
        forward = (z_fwd_in[0], z_fwd_in[1])
        real, imag = dot3(split(real), forward), dot3(split(imag), forward)
        real, imag = real[:, :256] + imag[:, 256:], imag[:, :256] - real[:, 256:]

        def back(scale, at):
            table = (z_inv_in[0], z_inv_in[1])
            re, im = dot3(split(real * scale), table), dot3(split(imag * scale), table)
            for c, value in enumerate((re[:, :128] - im[:, 128:], im[:, :128] + re[:, 128:])):
                lanes = slice(128 * c, 128 * c + 128)
                lines[at, 0, ky, lanes], lines[at, 1, ky, lanes] = split(value)

        back(amp_in[8 * part : 8 * part + 8].reshape(256, EZ), 0)

        @pl.when(packed)
        def _():
            back(amps[ky, :], 1)

    def inverse(at):
        data = (lines[at, 0], lines[at, 1])
        near = slice(0, AY)
        by_cos = dot3((y_fwd_in[0, 0, near, :], y_fwd_in[1, 0, near, :]), data)
        by_sin = dot3((y_fwd_in[0, 1, near, :], y_fwd_in[1, 1, near, :]), data)
        return by_cos[:, :AZ] - by_sin[:, AZ:], by_cos[:, AZ:] + by_sin[:, :AZ]

    def store(c, own):
        forward_halo = lax.broadcasted_iota(jnp.int32, (AY, AZ), 0) % GA < GA // 2
        after = jnp.concatenate([own[GA:], own[:GA]], 0)
        before = jnp.concatenate([own[AY - GA :], own[: AY - GA]], 0)
        sent[pl.ds(c, AY, stride=4), :] = own
        sent[pl.ds(2 + c, AY, stride=4), :] = jnp.where(forward_halo, after, before)

    real, imag = inverse(0)
    store(0, real)
    store(1, imag)

    @pl.when(packed)
    def _():
        store(1, inverse(1)[1])


def pack_kernel(head, rech, lo_x, hi_x, below, above):
    corner = lax.broadcasted_iota(jnp.int32, (8, AZ), 0)
    for out, near, far in ((below, 0, 1), (above, 7, 6)):
        for i, (ref, y) in enumerate(((head, near), (head, far), (rech, near))):
            out[32 * i : 32 * i + 32, :] = ref[pl.ds(y, 32, stride=8), :]
        out[96:104, :] = jnp.where(corner == 0, lo_x[8 + near : 9 + near, :], hi_x[8 + near : 9 + near, :])


def field_kernel(got, table, lo_halo, hi_halo, sent):
    ga, ba = lax.axis_index("ga"), lax.axis_index("ba")
    own = jnp.concatenate([got[pl.ds(c, DEVS, stride=4), :] for c in range(2)], 0)
    halo = jnp.concatenate([got[pl.ds(2 + c, DEVS, stride=4), :] for c in range(2)], 0)
    log_field = dot3((table[0], table[1]), split(jnp.concatenate([own, halo], 1)))
    row = lax.broadcasted_iota(jnp.int32, (XROWS, AZ), 0)
    halo_inside = jnp.where(ga < GA // 2, ba < BA - 1, ba > 0)
    for g in range(GA):
        x = row + (32 * g - 4)
        inside = (x >= 0) & (x < AX)
        value = jnp.exp(log_field[XROWS * g : XROWS * g + XROWS, :])
        sent[CHUNK * g : CHUNK * g + XROWS, :] = jnp.where(inside, value[:, :AZ], 0.0)
        beside = jnp.where(inside & halo_inside, value[:, AZ:], 0.0)
        sent[CHUNK * g + XROWS : CHUNK * g + CHUNK, :] = beside


def sweep_kernel(got, head, rech, lo_halo, hi_halo, lo_x, hi_x, cond_out, press_out,
                 head_ext, rech_ext, staged):
    ga, ba = lax.axis_index("ga"), lax.axis_index("ba")
    head_ext[...] = jnp.zeros_like(head_ext)
    rech_ext[...] = jnp.zeros_like(rech_ext)
    for y in range(8):
        at = XROWS * (y + 2)
        head_ext[at + 4 : at + 36, :] = head[pl.ds(y, 32, stride=8), :]
        rech_ext[at + 4 : at + 36, :] = rech[pl.ds(y, 32, stride=8), :]
    for halo, (first, second, only) in ((lo_halo, (1, 0, 1)), (hi_halo, (10, 11, 10))):
        for ref, y, i in ((head_ext, first, 0), (head_ext, second, 1), (rech_ext, only, 2)):
            ref[XROWS * y + 4 : XROWS * y + 36, :] = halo[32 * i : 32 * i + 32, :]
    for block, far, near in ((lo_x, 2, 3), (hi_x, 37, 36)):
        for y in range(8):
            at = XROWS * (y + 2)
            head_ext[at + far : at + far + 1, :] = block[y : y + 1, :]
            head_ext[at + near : at + near + 1, :] = block[8 + y : 9 + y, :]
            rech_ext[at + near : at + near + 1, :] = block[16 + y : 17 + y, :]
    for halo, y in ((lo_halo, 1), (hi_halo, 10)):
        for i, near in enumerate((3, 36)):
            head_ext[XROWS * y + near : XROWS * y + near + 1, :] = halo[96 + i : 97 + i, :]

    lane = lax.broadcasted_iota(jnp.int32, (XROWS, AZ), 1)
    row = lax.broadcasted_iota(jnp.int32, (XROWS, AZ), 0)
    x = row + (32 * ga - 4)
    inside_x = (x >= 0) & (x < AX)

    def in_plane(value):
        total = pltpu.roll(value, 1, 0) + pltpu.roll(value, XROWS - 1, 0)
        total = total + jnp.where(lane > 0, pltpu.roll(value, 1, 1), 0.0)
        return total + jnp.where(lane < AZ - 1, pltpu.roll(value, AZ - 1, 1), 0.0)

    beside = {y: got[CHUNK * y + XROWS : CHUNK * y + CHUNK, :] for y in (0, 1, 6, 7)}
    cond = [beside[6], beside[7]]
    cond += [got[CHUNK * y : CHUNK * y + XROWS, :] for y in range(8)]
    cond += [beside[0], beside[1]]
    planes = [head_ext[XROWS * y : XROWS * y + XROWS, :] for y in range(12)]
    weight = {y: 6.0 * cond[y] + (in_plane(cond[y]) + (cond[y - 1] + cond[y + 1])) for y in range(1, 11)}
    source = {y: 2.0 * rech_ext[XROWS * y : XROWS * y + XROWS, :] for y in range(1, 11)}
    for sweep in range(2):
        flow = {y: cond[y] * planes[y] for y in range(sweep, 12 - sweep)}
        new = dict()
        for y in range(sweep + 1, 11 - sweep):
            heads = in_plane(planes[y]) + (planes[y - 1] + planes[y + 1])
            flows = in_plane(flow[y]) + (flow[y - 1] + flow[y + 1])
            new[y] = (source[y] + (cond[y] * heads + flows)) / weight[y]
            if sweep == 0:
                inside = inside_x
                if y == 1:
                    inside = inside & (ba > 0)
                if y == 10:
                    inside = inside & (ba < BA - 1)
                new[y] = jnp.where(inside, new[y], 0.0)
        planes = new
    for y in range(8):
        cond_out[pl.ds(y, 32, stride=8), :] = got[CHUNK * y + 4 : CHUNK * y + 36, :]
        staged[...] = planes[y + 2]
        press_out[pl.ds(y, 32, stride=8), :] = staged[4:36, :]


def kernel_call(kernel, outs, inputs, scratch=(), held=(), outs_held=()):
    vmem = pl.BlockSpec(memory_space=pltpu.VMEM)
    there = pl.BlockSpec(memory_space=pl.ANY)
    return pl.pallas_call(
        kernel,
        out_shape=[jax.ShapeDtypeStruct(shape, f32) for shape in outs],
        in_specs=[there if i in held else vmem for i in range(len(inputs))],
        out_specs=[there if i in outs_held else vmem for i in range(len(outs))],
        scratch_shapes=list(scratch),
        compiler_params=pltpu.CompilerParams(vmem_limit_bytes=VMEM),
    )(*inputs)


def steps(axis):
    up = [(i, i + 1) for i in range(lax.axis_size(axis) - 1)]
    return up, [(j, i) for i, j in up]


def body(noise, amplitude, recharge, head_guess):
    x_fwd, y_fwd, z_fwd, z_inv, x_inv = (jnp.asarray(t) for t in tables())
    recharge = recharge.reshape(256, AZ)
    head = head_guess.reshape(256, AZ)
    memory, sems = pltpu.VMEM, pltpu.SemaphoreType.DMA
    (sent,) = kernel_call(
        enter_kernel, [(8 * DEVS, 128)], [noise.reshape(512, EX), x_fwd],
        [memory((512, EX), f32), memory(x_fwd.shape, bf16), memory((8 * DEVS, 128), f32), sems((3,))],
        held=(0, 1), outs_held=(0,),
    )
    got = lax.all_to_all(sent, ("ba", "ga"), 0, 0, tiled=True)
    amp_first = amplitude[:, 0, :]
    amp_zero = lax.ppermute(amp_first, "ga", [(0, PACKED_GA)])
    amp_row = lax.ppermute(amp_first, "ba", [(BA // 2, 0)])
    amp_sent, to_up, to_down = kernel_call(
        edges_kernel, [(512, EZ), (24, AZ), (24, AZ)], [amplitude, amp_first, amp_zero, head, recharge],
        [memory((16, 40, EZ), f32), sems((1,))], held=(0,),
    )
    halves = [list(range(side, BA, 2)) for side in range(2)]
    amp_near = lax.all_to_all(amp_sent, "ba", 0, 0, tiled=True, axis_index_groups=halves)
    amp_near = amp_near.reshape(BA // 2, 2, 16, EZ)
    give = jnp.where(lax.axis_index("ba") % 2 == 0, amp_near[:, 1], amp_near[:, 0])
    amp_far = lax.ppermute(give, "ba", [(i, i ^ 1) for i in range(BA)])
    up, down = steps("ga")
    lo_x = lax.ppermute(to_up, "ga", up)
    hi_x = lax.ppermute(to_down, "ga", down)
    below, above = kernel_call(pack_kernel, [(104, AZ), (104, AZ)], [head, recharge, lo_x, hi_x])
    inputs = [got, amp_near, amp_far, amp_zero, amp_row, y_fwd, z_fwd, z_inv, below, above]
    (sent,) = kernel_call(
        middle_kernel, [(4 * AY, AZ)], inputs,
        [memory(value.shape, value.dtype) for value in (got, amp_near, y_fwd, z_fwd, z_inv, amp_zero, amp_row)]
        + [memory((2, 512, 512), bf16), memory((2, 2, EY, 2 * AZ), bf16), memory((EY, EZ), f32), sems((8,))],
        held=range(10),
    )
    got = lax.all_to_all(sent, ("ba", "ga"), 0, 0, tiled=True)
    up, down = steps("ba")
    hi_halo = lax.ppermute(below, "ba", down)
    lo_halo = lax.ppermute(above, "ba", up)
    (sent,) = kernel_call(field_kernel, [(CHUNK * GA, AZ)], [got, x_inv, lo_halo, hi_halo], held=(2, 3))
    got = lax.all_to_all(sent, "ga", 0, 0, tiled=True)
    ext = pltpu.VMEM((12 * XROWS, AZ), f32)
    conductivity, pressure = kernel_call(
        sweep_kernel, [(256, AZ), (256, AZ)],
        [got, head, recharge, lo_halo, hi_halo, lo_x, hi_x],
        [ext, ext, pltpu.VMEM((XROWS, AZ), f32)],
    )
    return conductivity.reshape(32, 8, AZ), pressure.reshape(32, 8, AZ)


def solution(mesh):
    placed = (P("ba", "ga", None), P("ba", "ga", None), P("ga", "ba", None), P("ga", "ba", None))
    return jax.shard_map(
        body,
        mesh=mesh,
        in_specs=placed,
        out_specs=(P("ga", "ba", None), P("ga", "ba", None)),
        check_vma=False,
    )
```

```python
import functools
import math

import jax
import jax.numpy as jnp
import ml_dtypes
import numpy as np
from jax import lax
from jax.experimental import pallas as pl
from jax.experimental.pallas import tpu as pltpu
from jax.sharding import PartitionSpec as P

AX, AY, AZ = 256, 256, 128
EX, EY, EZ = 512, 512, 256
GA, BA = 8, 32
DEVS = GA * BA
PACKED_GA = 4
XROWS = 40
CHUNK = 2 * XROWS
VMEM = 60 * 2**20
VMEM_END = 16 * 2**20
f32, bf16 = jnp.float32, jnp.bfloat16


def split_np(table):
    high = table.astype(np.float32).astype(ml_dtypes.bfloat16)
    low = (table - high.astype(np.float64)).astype(np.float32).astype(ml_dtypes.bfloat16)
    return np.stack([high, low])


def trig(rows, cols, period):
    angles = (np.outer(rows, cols) % period) * (2.0 * math.pi / period)
    return np.cos(angles), np.sin(angles)


def kx_of():
    ids = np.zeros(DEVS, np.int64)
    for b in range(BA):
        for g in range(GA):
            if b:
                kx = 64 * g + b
            elif g < PACKED_GA:
                kx = 64 * g + 32
            else:
                kx = -1 if g == PACKED_GA else 64 * g
            ids[b * GA + g] = kx
    return ids


@functools.cache
def tables():
    kx = kx_of()
    packed = kx < 0
    alternating = 1.0 - 2.0 * (np.arange(EX) % 2)
    cos, sin = trig(np.maximum(kx, 0), np.arange(EX), EX)
    wide_re, wide_im = cos.copy(), -sin
    wide_re[packed], wide_im[packed] = alternating, 1.0
    x_fwd = np.concatenate([wide_re, wide_im])

    y_fwd = np.stack(trig(np.arange(EY), np.arange(EY), EY))

    half, quarter, block = np.meshgrid(np.arange(2), np.arange(4), np.arange(BA), indexing="ij")
    z_order = (8 * block + 2 * quarter + half).reshape(-1)
    z_fwd = np.concatenate(trig(z_order, np.arange(EZ), EZ), 1)
    z_inv = np.concatenate(trig(np.arange(EZ), np.arange(AZ), EZ), 1)

    xs = np.clip((32 * np.arange(GA)[:, None] - 4 + np.arange(XROWS)).reshape(-1), 0, AX - 1)
    cos, sin = trig(xs, np.maximum(kx, 0), EX)
    back_re, back_im = 2.0 * cos, -2.0 * sin
    back_re[:, packed] = alternating[xs][:, None]
    back_im[:, packed] = 1.0
    x_inv = np.concatenate([back_re, back_im], 1) / (EX * EY * EZ)
    return tuple(split_np(t) for t in (x_fwd, y_fwd, z_fwd, z_inv, x_inv))


def split(value):
    high = value.astype(bf16)
    return high, (value - high.astype(f32)).astype(bf16)


def dot3(a, b, rhs_dim=0):
    dims = (((1,), (rhs_dim,)), ((), ()))
    mul = functools.partial(lax.dot_general, dimension_numbers=dims, preferred_element_type=f32)
    return mul(a[0], b[0]) + (mul(a[0], b[1]) + mul(a[1], b[0]))


def fetch(pairs, sems):
    copies = [pltpu.make_async_copy(src, dst, sems.at[i]) for i, (src, dst) in enumerate(pairs)]
    for copy in copies:
        copy.start()
    return copies


def enter_kernel(noise, table, after, sent, noise_in, table_in, rows_out, sems):
    pairs = [(table, table_in), (noise.at[0:256, :], noise_in.at[0:256, :]),
             (noise.at[256:512, :], noise_in.at[256:512, :])]
    copies = fetch(pairs, sems)
    copies[0].wait()
    for part in range(2):
        copies[1 + part].wait()
        rows = split(noise_in[256 * part : 256 * part + 256, :])
        for c in range(2):
            own = slice(256 * c, 256 * c + 256)
            result = dot3((table_in[0, own, :], table_in[1, own, :]), rows, 1)
            for q in range(2):
                at = pl.ds(4 * c + 2 * part + q, DEVS, stride=8)
                rows_out[at, :] = result[:, 128 * q : 128 * q + 128]
    pltpu.sync_copy(rows_out, sent)


def edges_kernel(amp, amp_first, amp_zero, head, rech, amp_sent, below, above, amp_in, sems):
    ga, ba = lax.axis_index("ga"), lax.axis_index("ba")
    (copy,) = fetch([(amp.at[:, 0:40, :], amp_in)], sems)
    for out, near, far in ((below, 0, 1), (above, 7, 6)):
        for i, (ref, y) in enumerate(((head, near), (head, far), (rech, near))):
            out[32 * i : 32 * i + 32, :] = ref[pl.ds(y, 32, stride=8), :]
    copy.wait()
    zero = (ga == PACKED_GA) & (ba >= BA // 2)
    for half in range(2):
        lanes = slice(128 * half, 128 * half + 128)
        first = jnp.where(zero, amp_zero[:, lanes], amp_first[:, lanes])
        amp_sent[0:16, lanes] = jnp.where(ga < PACKED_GA, amp_in[:, 32, lanes], first)
        for b in range(1, BA):
            amp_sent[16 * b : 16 * b + 16, lanes] = amp_in[:, b, lanes]


def gate_kernel(amp_sent, got, lo_halo, hi_halo, same):
    pass


def mirror_of(value):
    ones = []
    for size in value.shape:
        i = lax.broadcasted_iota(jnp.int32, (size, size), 0)
        j = lax.broadcasted_iota(jnp.int32, (size, size), 1)
        ones.append((((i + j) == 0) | ((i + j) == size)).astype(bf16))
    total = None
    for _ in range(3):
        part = value.astype(bf16)
        value = value - part.astype(f32)
        part = jnp.dot(ones[0], part, preferred_element_type=f32).astype(bf16)
        part = jnp.dot(part, ones[1], preferred_element_type=f32)
        total = part if total is None else total + part
    return total


def forward_kernel(got, y_fwd, z_fwd, spectrum, got_in, y_fwd_in, z_fwd_in, rows, held, sems):
    copies = fetch([(got, got_in), (y_fwd, y_fwd_in), (z_fwd, z_fwd_in)], sems)
    copies[0].wait()
    low_half = lax.broadcasted_iota(jnp.int32, (BA, 128), 1) < 64
    for c in range(2):
        for q in range(4):
            for p in range(4):
                even = got_in[pl.ds(16 * p + 4 * c + q, BA, stride=64), :]
                odd = got_in[pl.ds(16 * p + 8 + 4 * c + q, BA, stride=64), :]
                first = jnp.where(low_half, even, pltpu.roll(odd, 64, 1))
                second = jnp.where(low_half, pltpu.roll(even, 64, 1), odd)
                for half, value in enumerate((first, second)):
                    at = slice(256 * c + 128 * half + 32 * q, 256 * c + 128 * half + 32 * q + 32)
                    high, low = split(value)
                    rows[0, at, 128 * p : 128 * p + 128] = high
                    rows[1, at, 128 * p : 128 * p + 128] = low
    leaving = []
    for part in range(2):
        ky = slice(256 * part, 256 * part + 256)
        data = (rows[0], rows[1])
        if part == 0:
            copies[1].wait()
        by_cos = dot3((y_fwd_in[0, 0, ky, :], y_fwd_in[1, 0, ky, :]), data, 1)
        by_sin = dot3((y_fwd_in[0, 1, ky, :], y_fwd_in[1, 1, ky, :]), data, 1)
        real = by_cos[:, :256] + by_sin[:, 256:]
        imag = by_cos[:, 256:] - by_sin[:, :256]
        if part == 0:
            copies[2].wait()
        forward = (z_fwd_in[0], z_fwd_in[1])
        real, imag = dot3(split(real), forward), dot3(split(imag), forward)
        real, imag = real[:, :256] + imag[:, 256:], imag[:, :256] - real[:, 256:]

        held[0, ky, :] = real
        held[1, ky, :] = imag
        leaving += fetch([(held.at[:, ky, :], spectrum.at[:, ky, :])], sems.at[pl.ds(3 + part, 1)])
    for copy in leaving:
        copy.wait()


def inverse_kernel(spectrum, amp, amp_row0, amp_row256, z_inv, y_fwd, up, down, sent,
                   spectrum_in, amp_in, y_fwd_in, z_inv_in, row0_in, row256_in, lines, amps, sems):
    ga, ba = lax.axis_index("ga"), lax.axis_index("ba")
    packed = (ga == PACKED_GA) & (ba == 0)
    pairs = [(amp, amp_in), (amp_row0, row0_in), (amp_row256, row256_in), (spectrum, spectrum_in), (z_inv, z_inv_in),
             (y_fwd.at[:, :, 0:256, :], y_fwd_in)]
    copies = fetch(pairs, sems)
    for i in range(3):
        copies[i].wait()

    @pl.when(packed)
    def _():
        held = amp_in[...]
        mirror = mirror_of(held)
        ky = lax.broadcasted_iota(jnp.int32, (EY, EZ), 0)
        amps[...] = jnp.where(ky == 0, row0_in[0:1, :], jnp.where(ky < 256, mirror, held))
        amp_in[...] = jnp.where(ky == 256, row256_in[0:1, :], jnp.where(ky < 256, held, mirror))

    copies[3].wait()
    copies[4].wait()
    for part in range(2):
        ky = slice(256 * part, 256 * part + 256)
        real, imag = spectrum_in[0, ky, :], spectrum_in[1, ky, :]

        def back(scale, at):
            table = (z_inv_in[0], z_inv_in[1])
            re, im = dot3(split(real * scale), table), dot3(split(imag * scale), table)
            for c, value in enumerate((re[:, :128] - im[:, 128:], im[:, :128] + re[:, 128:])):
                lanes = slice(128 * c, 128 * c + 128)
                lines[at, 0, ky, lanes], lines[at, 1, ky, lanes] = split(value)

        back(amp_in[ky, :], 0)

        @pl.when(packed)
        def _():
            back(amps[ky, :], 1)

    def inverse(at):
        data = (lines[at, 0], lines[at, 1])
        by_cos = dot3((y_fwd_in[0, 0], y_fwd_in[1, 0]), data)
        by_sin = dot3((y_fwd_in[0, 1], y_fwd_in[1, 1]), data)
        return by_cos[:, :AZ] - by_sin[:, AZ:], by_cos[:, AZ:] + by_sin[:, :AZ]

    def store(c, own):
        forward_halo = lax.broadcasted_iota(jnp.int32, (AY, AZ), 0) % GA < GA // 2
        after = jnp.concatenate([own[GA:], own[:GA]], 0)
        before = jnp.concatenate([own[AY - GA :], own[: AY - GA]], 0)
        sent[pl.ds(c, AY, stride=4), :] = own
        sent[pl.ds(2 + c, AY, stride=4), :] = jnp.where(forward_halo, after, before)

    copies[5].wait()
    real, imag = inverse(0)
    store(0, real)
    store(1, imag)

    @pl.when(packed)
    def _():
        store(1, inverse(1)[1])


def pack_kernel(head, rech, lo_halo, hi_halo, up, down):
    corner = lax.broadcasted_iota(jnp.int32, (8, AZ), 0)
    for out, far, near in ((up, 30, 31), (down, 1, 0)):
        out[0:8, :] = head[8 * far : 8 * far + 8, :]
        out[8:16, :] = head[8 * near : 8 * near + 8, :]
        out[16:24, :] = rech[8 * near : 8 * near + 8, :]
        out[24:32, :] = jnp.where(corner == 0, lo_halo[near : near + 1, :], hi_halo[near : near + 1, :])


def field_kernel(got, table, lo_x, hi_x, sent, table_in, sems):
    (copy,) = fetch([(table, table_in)], sems)
    ga, ba = lax.axis_index("ga"), lax.axis_index("ba")
    own = jnp.concatenate([got[pl.ds(c, DEVS, stride=4), :] for c in range(2)], 0)
    halo = jnp.concatenate([got[pl.ds(2 + c, DEVS, stride=4), :] for c in range(2)], 0)
    copy.wait()
    log_field = dot3((table_in[0], table_in[1]), split(jnp.concatenate([own, halo], 1)))
    row = lax.broadcasted_iota(jnp.int32, (XROWS, AZ), 0)
    halo_inside = jnp.where(ga < GA // 2, ba < BA - 1, ba > 0)
    for g in range(GA):
        x = row + (32 * g - 4)
        inside = (x >= 0) & (x < AX)
        value = jnp.exp(log_field[XROWS * g : XROWS * g + XROWS, :])
        sent[CHUNK * g : CHUNK * g + XROWS, :] = jnp.where(inside, value[:, :AZ], 0.0)
        beside = jnp.where(inside & halo_inside, value[:, AZ:], 0.0)
        sent[CHUNK * g + XROWS : CHUNK * g + CHUNK, :] = beside


def sweep_kernel(got, head, rech, lo_halo, hi_halo, lo_x, hi_x, cond_out, press_out,
                 head_ext, rech_ext, staged):
    ga, ba = lax.axis_index("ga"), lax.axis_index("ba")
    head_ext[...] = jnp.zeros_like(head_ext)
    rech_ext[...] = jnp.zeros_like(rech_ext)
    for y in range(8):
        at = XROWS * (y + 2)
        head_ext[at + 4 : at + 36, :] = head[pl.ds(y, 32, stride=8), :]
        rech_ext[at + 4 : at + 36, :] = rech[pl.ds(y, 32, stride=8), :]
    for halo, (first, second, only) in ((lo_halo, (1, 0, 1)), (hi_halo, (10, 11, 10))):
        for ref, y, i in ((head_ext, first, 0), (head_ext, second, 1), (rech_ext, only, 2)):
            ref[XROWS * y + 4 : XROWS * y + 36, :] = halo[32 * i : 32 * i + 32, :]
    for block, far, near in ((lo_x, 2, 3), (hi_x, 37, 36)):
        for y in range(8):
            at = XROWS * (y + 2)
            head_ext[at + far : at + far + 1, :] = block[y : y + 1, :]
            head_ext[at + near : at + near + 1, :] = block[8 + y : 9 + y, :]
            rech_ext[at + near : at + near + 1, :] = block[16 + y : 17 + y, :]
        head_ext[XROWS + near : XROWS + near + 1, :] = block[24:25, :]
        head_ext[10 * XROWS + near : 10 * XROWS + near + 1, :] = block[25:26, :]

    lane = lax.broadcasted_iota(jnp.int32, (XROWS, AZ), 1)
    row = lax.broadcasted_iota(jnp.int32, (XROWS, AZ), 0)
    x = row + (32 * ga - 4)
    inside_x = (x >= 0) & (x < AX)

    def in_plane(value):
        total = pltpu.roll(value, 1, 0) + pltpu.roll(value, XROWS - 1, 0)
        total = total + jnp.where(lane > 0, pltpu.roll(value, 1, 1), 0.0)
        return total + jnp.where(lane < AZ - 1, pltpu.roll(value, AZ - 1, 1), 0.0)

    beside = {y: got[CHUNK * y + XROWS : CHUNK * y + CHUNK, :] for y in (0, 1, 6, 7)}
    cond = [beside[6], beside[7]]
    cond += [got[CHUNK * y : CHUNK * y + XROWS, :] for y in range(8)]
    cond += [beside[0], beside[1]]
    planes = [head_ext[XROWS * y : XROWS * y + XROWS, :] for y in range(12)]
    weight = {y: 6.0 * cond[y] + (in_plane(cond[y]) + (cond[y - 1] + cond[y + 1])) for y in range(1, 11)}
    source = {y: 2.0 * rech_ext[XROWS * y : XROWS * y + XROWS, :] for y in range(1, 11)}
    for sweep in range(2):
        flow = {y: cond[y] * planes[y] for y in range(sweep, 12 - sweep)}
        new = dict()
        for y in range(sweep + 1, 11 - sweep):
            heads = in_plane(planes[y]) + (planes[y - 1] + planes[y + 1])
            flows = in_plane(flow[y]) + (flow[y - 1] + flow[y + 1])
            new[y] = (source[y] + (cond[y] * heads + flows)) / weight[y]
            if sweep == 0:
                inside = inside_x
                if y == 1:
                    inside = inside & (ba > 0)
                if y == 10:
                    inside = inside & (ba < BA - 1)
                new[y] = jnp.where(inside, new[y], 0.0)
        planes = new
    for y in range(8):
        cond_out[pl.ds(y, 32, stride=8), :] = got[CHUNK * y + 4 : CHUNK * y + 36, :]
        staged[...] = planes[y + 2]
        press_out[pl.ds(y, 32, stride=8), :] = staged[4:36, :]


def kernel_call(kernel, outs, inputs, scratch=(), held=(), outs_held=(), vmem=VMEM, flops=0, aliases=None):
    whole = pl.BlockSpec(memory_space=pltpu.VMEM)
    there = pl.BlockSpec(memory_space=pl.ANY)
    return pl.pallas_call(
        kernel,
        out_shape=[jax.ShapeDtypeStruct(shape, f32) for shape in outs],
        in_specs=[there if i in held else whole for i in range(len(inputs))],
        out_specs=[there if i in outs_held else whole for i in range(len(outs))],
        scratch_shapes=list(scratch),
        input_output_aliases=aliases or {},
        compiler_params=pltpu.CompilerParams(vmem_limit_bytes=vmem),
        cost_estimate=pl.CostEstimate(flops=flops, bytes_accessed=6 * 2**20, transcendentals=0) if flops else None,
    )(*inputs)


def steps(axis):
    up = [(i, i + 1) for i in range(lax.axis_size(axis) - 1)]
    return up, [(j, i) for i, j in up]


def body(noise, amplitude, recharge, head_guess):
    x_fwd, y_fwd, z_fwd, z_inv, x_inv = (jnp.asarray(t) for t in tables())
    recharge = recharge.reshape(256, AZ)
    head = head_guess.reshape(256, AZ)
    memory, sems = pltpu.VMEM, pltpu.SemaphoreType.DMA
    amp_first = amplitude[:, 0, :]
    amp_zero = lax.ppermute(amp_first, "ga", [(0, PACKED_GA)])
    amp_row = lax.ppermute(amp_first, "ba", [(BA // 2, 0)])
    (sent,) = kernel_call(
        enter_kernel, [(8 * DEVS, 128)], [noise.reshape(512, EX), x_fwd, amp_zero],
        [memory((512, EX), f32), memory(x_fwd.shape, bf16), memory((8 * DEVS, 128), f32), sems((3,))],
        held=(0, 1, 2), outs_held=(0,), flops=10**9,
    )
    got = lax.all_to_all(sent, ("ba", "ga"), 0, 0, tiled=True)
    amp_sent, below, above = kernel_call(
        edges_kernel, [(512, EZ), (96, AZ), (96, AZ)], [amplitude, amp_first, amp_zero, head, recharge],
        [memory((16, 40, EZ), f32), sems((1,))], held=(0,),
    )
    up, down = steps("ba")
    hi_halo = lax.ppermute(below, "ba", down)
    lo_halo = lax.ppermute(above, "ba", up)
    (amp_sent,) = kernel_call(
        gate_kernel, [(512, EZ)], [amp_sent, got, lo_halo, hi_halo], held=range(4), outs_held=(0,), aliases={0: 0}
    )
    amp = lax.all_to_all(amp_sent, "ba", 0, 0, tiled=True)
    (spectrum,) = kernel_call(
        forward_kernel, [(2, EY, EZ)], [got, y_fwd, z_fwd],
        [memory(value.shape, value.dtype) for value in (got, y_fwd, z_fwd)]
        + [memory((2, 512, 512), bf16), memory((2, EY, EZ), f32), sems((5,))],
        held=range(3), outs_held=(0,), flops=3 * 10**9,
    )
    to_up, to_down = kernel_call(pack_kernel, [(32, AZ), (32, AZ)], [head, recharge, lo_halo, hi_halo])
    plane = (EY, EZ)
    (sent,) = kernel_call(
        inverse_kernel, [(4 * AY, AZ)],
        [spectrum, amp, amp_zero, amp_row, z_inv, y_fwd, to_up, to_down],
        [memory((2, EY, EZ), f32), memory(plane, f32), memory((2, 2, AY, EY), bf16), memory(z_inv.shape, bf16)]
        + [memory((16, EZ), f32)] * 2 + [memory((2, 2, EY, 2 * AZ), bf16), memory(plane, f32), sems((6,))],
        held=range(8),
    )
    got = lax.all_to_all(sent, ("ba", "ga"), 0, 0, tiled=True)
    up, down = steps("ga")
    lo_x = lax.ppermute(to_up, "ga", up)
    hi_x = lax.ppermute(to_down, "ga", down)
    (sent,) = kernel_call(
        field_kernel, [(CHUNK * GA, AZ)], [got, x_inv, lo_x, hi_x],
        [memory(x_inv.shape, bf16), sems((1,))], held=(1, 2, 3), vmem=VMEM_END,
    )
    got = lax.all_to_all(sent, "ga", 0, 0, tiled=True)
    ext = pltpu.VMEM((12 * XROWS, AZ), f32)
    conductivity, pressure = kernel_call(
        sweep_kernel, [(256, AZ), (256, AZ)],
        [got, head, recharge, lo_halo, hi_halo, lo_x, hi_x],
        [ext, ext, pltpu.VMEM((XROWS, AZ), f32)], vmem=VMEM_END,
    )
    return conductivity.reshape(32, 8, AZ), pressure.reshape(32, 8, AZ)


def solution(mesh):
    placed = (P("ba", "ga", None), P("ba", "ga", None), P("ga", "ba", None), P("ga", "ba", None))
    return jax.shard_map(
        body,
        mesh=mesh,
        in_specs=placed,
        out_specs=(P("ga", "ba", None), P("ga", "ba", None)),
        check_vma=False,
    )
```

```python
import functools
import math

import jax
import jax.numpy as jnp
import ml_dtypes
import numpy as np
from jax import lax
from jax.experimental import pallas as pl
from jax.experimental.pallas import tpu as pltpu
from jax.sharding import PartitionSpec as P

AX, AY, AZ = 256, 256, 128
EX, EY, EZ = 512, 512, 256
GA, BA = 8, 32
DEVS = GA * BA
PACKED_GA = 4
XROWS = 40
CHUNK = 2 * XROWS
VMEM = 60 * 2**20
VMEM_END = 16 * 2**20
f32, bf16 = jnp.float32, jnp.bfloat16


def split_np(table):
    high = table.astype(np.float32).astype(ml_dtypes.bfloat16)
    low = (table - high.astype(np.float64)).astype(np.float32).astype(ml_dtypes.bfloat16)
    return np.stack([high, low])


def trig(rows, cols, period):
    angles = (np.outer(rows, cols) % period) * (2.0 * math.pi / period)
    return np.cos(angles), np.sin(angles)


def kx_of():
    ids = np.zeros(DEVS, np.int64)
    for b in range(BA):
        for g in range(GA):
            if b:
                kx = 64 * g + b
            elif g < PACKED_GA:
                kx = 64 * g + 32
            else:
                kx = -1 if g == PACKED_GA else 64 * g
            ids[b * GA + g] = kx
    return ids


@functools.cache
def tables():
    kx = kx_of()
    packed = kx < 0
    alternating = 1.0 - 2.0 * (np.arange(EX) % 2)
    cos, sin = trig(np.maximum(kx, 0), np.arange(EX), EX)
    wide_re, wide_im = cos.copy(), -sin
    wide_re[packed], wide_im[packed] = alternating, 1.0
    x_fwd = np.concatenate([wide_re, wide_im])

    y_fwd = np.stack(trig(np.arange(EY), np.arange(EY), EY))

    half, quarter, block = np.meshgrid(np.arange(2), np.arange(4), np.arange(BA), indexing="ij")
    z_order = (8 * block + 2 * quarter + half).reshape(-1)
    z_fwd = np.concatenate(trig(z_order, np.arange(EZ), EZ), 1)
    z_inv = np.concatenate(trig(np.arange(EZ), np.arange(AZ), EZ), 1)

    xs = np.clip((32 * np.arange(GA)[:, None] - 4 + np.arange(XROWS)).reshape(-1), 0, AX - 1)
    cos, sin = trig(xs, np.maximum(kx, 0), EX)
    back_re, back_im = 2.0 * cos, -2.0 * sin
    back_re[:, packed] = alternating[xs][:, None]
    back_im[:, packed] = 1.0
    x_inv = np.concatenate([back_re, back_im], 1) / (EX * EY * EZ)
    return tuple(split_np(t) for t in (x_fwd, y_fwd, z_fwd, z_inv, x_inv))


def split(value):
    high = value.astype(bf16)
    return high, (value - high.astype(f32)).astype(bf16)


def dot3(a, b, rhs_dim=0):
    dims = (((1,), (rhs_dim,)), ((), ()))
    mul = functools.partial(lax.dot_general, dimension_numbers=dims, preferred_element_type=f32)
    return mul(a[0], b[0]) + (mul(a[0], b[1]) + mul(a[1], b[0]))


def fetch(pairs, sems):
    copies = [pltpu.make_async_copy(src, dst, sems.at[i]) for i, (src, dst) in enumerate(pairs)]
    for copy in copies:
        copy.start()
    return copies


def enter_kernel(noise, table, sent, noise_in, table_in, out, sems):
    pairs = [(table, table_in), (noise.at[0:256, :], noise_in.at[0:256, :]),
             (noise.at[256:512, :], noise_in.at[256:512, :])]
    copies = fetch(pairs, sems)
    copies[0].wait()
    for part in range(2):
        copies[1 + part].wait()
        rows = split(noise_in[256 * part : 256 * part + 256, :])
        for c in range(2):
            own = slice(256 * c, 256 * c + 256)
            result = dot3((table_in[0, own, :], table_in[1, own, :]), rows, 1)
            for q in range(2):
                at = pl.ds(4 * c + 2 * part + q, DEVS, stride=8)
                out[at, :] = result[:, 128 * q : 128 * q + 128]
    pltpu.sync_copy(out, sent)


def edges_kernel(amp, head, rech, keep, give, first, below, above, amp_in, sems):
    ga, ba = lax.axis_index("ga"), lax.axis_index("ba")
    (copy,) = fetch([(amp.at[:, 0:40, :], amp_in)], sems)
    for out, near, far in ((below, 0, 1), (above, 7, 6)):
        for i, (ref, y) in enumerate(((head, near), (head, far), (rech, near))):
            out[32 * i : 32 * i + 32, :] = ref[pl.ds(y, 32, stride=8), :]
    copy.wait()
    even = lax.rem(ba, 2) == 0
    for half in range(2):
        lanes = slice(128 * half, 128 * half + 128)
        for b in range(0, BA, 2):
            near, far = amp_in[:, b, lanes], amp_in[:, b + 1, lanes]
            if b == 0:
                first[:, lanes] = near
                near = jnp.where(ga < PACKED_GA, amp_in[:, 32, lanes], near)
            keep[b // 2, 0, :, lanes] = jnp.where(even, near, far)
            give[b // 2, :, lanes] = jnp.where(even, far, near)


def join_kernel(keep, other, zero_near, zero_far, got, lo_halo, hi_halo, sent, sems):
    ga, ba = lax.axis_index("ga"), lax.axis_index("ba")
    (copy,) = fetch([(other, sent.at[:, 1])], sems)
    copy.wait()

    @pl.when((ga == PACKED_GA) & (ba >= BA // 2) & (lax.rem(ba, 2) == 0))
    def _():
        for copy in fetch([(zero_near, sent.at[0, 0]), (zero_far, sent.at[0, 1])], sems):
            copy.wait()


def mirror_of(value):
    ones = []
    for size in value.shape:
        i = lax.broadcasted_iota(jnp.int32, (size, size), 0)
        j = lax.broadcasted_iota(jnp.int32, (size, size), 1)
        ones.append((((i + j) == 0) | ((i + j) == size)).astype(bf16))
    total = None
    for _ in range(3):
        part = value.astype(bf16)
        value = value - part.astype(f32)
        part = jnp.dot(ones[0], part, preferred_element_type=f32).astype(bf16)
        part = jnp.dot(part, ones[1], preferred_element_type=f32)
        total = part if total is None else total + part
    return total


def forward_kernel(got, y_fwd, z_fwd, head, rech, lo_halo, hi_halo, spectrum, up, down,
                   got_in, y_fwd_in, z_fwd_in, rows, held, edge, sems):
    pairs = [(got, got_in), (y_fwd, y_fwd_in), (z_fwd, z_fwd_in), (head.at[0:16, :], edge.at[0:16, :]),
             (head.at[240:256, :], edge.at[16:32, :]), (rech.at[0:8, :], edge.at[32:40, :]),
             (rech.at[248:256, :], edge.at[40:48, :])]
    pairs += [(halo.at[x : x + 8, :], edge.at[48 + 16 * i + x // 3 : 56 + 16 * i + x // 3, :])
              for i, halo in enumerate((lo_halo, hi_halo)) for x in (0, 24)]
    copies = fetch(pairs, sems)
    copies[0].wait()
    low_half = lax.broadcasted_iota(jnp.int32, (BA, 128), 1) < 64
    for c in range(2):
        for q in range(4):
            for p in range(4):
                even = got_in[pl.ds(16 * p + 4 * c + q, BA, stride=64), :]
                odd = got_in[pl.ds(16 * p + 8 + 4 * c + q, BA, stride=64), :]
                first = jnp.where(low_half, even, pltpu.roll(odd, 64, 1))
                second = jnp.where(low_half, pltpu.roll(even, 64, 1), odd)
                for half, value in enumerate((first, second)):
                    at = slice(256 * c + 128 * half + 32 * q, 256 * c + 128 * half + 32 * q + 32)
                    high, low = split(value)
                    rows[0, at, 128 * p : 128 * p + 128] = high
                    rows[1, at, 128 * p : 128 * p + 128] = low
    leaving = []
    for part in range(2):
        ky = slice(256 * part, 256 * part + 256)
        data = (rows[0], rows[1])
        if part == 0:
            copies[1].wait()
        by_cos = dot3((y_fwd_in[0, 0, ky, :], y_fwd_in[1, 0, ky, :]), data, 1)
        by_sin = dot3((y_fwd_in[0, 1, ky, :], y_fwd_in[1, 1, ky, :]), data, 1)
        real = by_cos[:, :256] + by_sin[:, 256:]
        imag = by_cos[:, 256:] - by_sin[:, :256]
        if part == 0:
            copies[2].wait()
        forward = (z_fwd_in[0], z_fwd_in[1])
        real, imag = dot3(split(real), forward), dot3(split(imag), forward)
        real, imag = real[:, :256] + imag[:, 256:], imag[:, :256] - real[:, 256:]

        held[0, ky, :] = real
        held[1, ky, :] = imag
        leaving += fetch([(held.at[:, ky, :], spectrum.at[:, ky, :])], sems.at[pl.ds(11 + part, 1)])
    for copy in copies[3:]:
        copy.wait()
    corner = lax.broadcasted_iota(jnp.int32, (8, AZ), 0)
    for out, far, near, rech_at, x in ((up, 16, 24, 40, 15), (down, 8, 0, 32, 0)):
        out[0:8, :] = edge[far : far + 8, :]
        out[8:16, :] = edge[near : near + 8, :]
        out[16:24, :] = edge[rech_at : rech_at + 8, :]
        out[24:32, :] = jnp.where(corner == 0, edge[48 + x : 49 + x, :], edge[64 + x : 65 + x, :])
    for copy in leaving:
        copy.wait()


def inverse_kernel(spectrum, amp, amp_row0, amp_row256, z_inv, y_fwd, sent,
                   spectrum_in, amp_in, y_fwd_in, z_inv_in, row0_in, row256_in, lines, amps, sems):
    ga, ba = lax.axis_index("ga"), lax.axis_index("ba")
    packed = (ga == PACKED_GA) & (ba == 0)
    side = lax.rem(ba, 2)
    pairs = [(amp.at[:, 0], amp_in.at[:, side]), (amp.at[:, 1], amp_in.at[:, 1 - side]),
             (amp_row0, row0_in), (amp_row256, row256_in), (spectrum, spectrum_in), (z_inv, z_inv_in),
             (y_fwd.at[:, :, 0:256, :], y_fwd_in)]
    copies = fetch(pairs, sems)
    for i in range(4):
        copies[i].wait()

    @pl.when(packed)
    def _():
        held = amp_in[...].reshape(EY, EZ)
        mirror = mirror_of(held)
        ky = lax.broadcasted_iota(jnp.int32, (EY, EZ), 0)
        amps[...] = jnp.where(ky == 0, row0_in[0:1, :], jnp.where(ky < 256, mirror, held))
        new = jnp.where(ky == 256, row256_in[0:1, :], jnp.where(ky < 256, held, mirror))
        amp_in[...] = new.reshape(amp_in.shape)

    copies[4].wait()
    copies[5].wait()
    for part in range(2):
        ky = slice(256 * part, 256 * part + 256)
        real, imag = spectrum_in[0, ky, :], spectrum_in[1, ky, :]

        def back(scale, at):
            table = (z_inv_in[0], z_inv_in[1])
            re, im = dot3(split(real * scale), table), dot3(split(imag * scale), table)
            for c, value in enumerate((re[:, :128] - im[:, 128:], im[:, :128] + re[:, 128:])):
                lanes = slice(128 * c, 128 * c + 128)
                lines[at, 0, ky, lanes], lines[at, 1, ky, lanes] = split(value)

        back(amp_in[8 * part : 8 * part + 8].reshape(256, EZ), 0)

        @pl.when(packed)
        def _():
            back(amps[ky, :], 1)

    def inverse(at):
        data = (lines[at, 0], lines[at, 1])
        by_cos = dot3((y_fwd_in[0, 0], y_fwd_in[1, 0]), data)
        by_sin = dot3((y_fwd_in[0, 1], y_fwd_in[1, 1]), data)
        return by_cos[:, :AZ] - by_sin[:, AZ:], by_cos[:, AZ:] + by_sin[:, :AZ]

    def store(c, own):
        forward_halo = lax.broadcasted_iota(jnp.int32, (AY, AZ), 0) % GA < GA // 2
        after = jnp.concatenate([own[GA:], own[:GA]], 0)
        before = jnp.concatenate([own[AY - GA :], own[: AY - GA]], 0)
        sent[pl.ds(c, AY, stride=4), :] = own
        sent[pl.ds(2 + c, AY, stride=4), :] = jnp.where(forward_halo, after, before)

    copies[6].wait()
    real, imag = inverse(0)
    store(0, real)
    store(1, imag)

    @pl.when(packed)
    def _():
        store(1, inverse(1)[1])


def field_kernel(got, table, lo_x, hi_x, sent, table_in, sems):
    (copy,) = fetch([(table, table_in)], sems)
    ga, ba = lax.axis_index("ga"), lax.axis_index("ba")
    own = jnp.concatenate([got[pl.ds(c, DEVS, stride=4), :] for c in range(2)], 0)
    halo = jnp.concatenate([got[pl.ds(2 + c, DEVS, stride=4), :] for c in range(2)], 0)
    copy.wait()
    log_field = dot3((table_in[0], table_in[1]), split(jnp.concatenate([own, halo], 1)))
    row = lax.broadcasted_iota(jnp.int32, (XROWS, AZ), 0)
    halo_inside = jnp.where(ga < GA // 2, ba < BA - 1, ba > 0)
    for g in range(GA):
        x = row + (32 * g - 4)
        inside = (x >= 0) & (x < AX)
        value = jnp.exp(log_field[XROWS * g : XROWS * g + XROWS, :])
        sent[CHUNK * g : CHUNK * g + XROWS, :] = jnp.where(inside, value[:, :AZ], 0.0)
        beside = jnp.where(inside & halo_inside, value[:, AZ:], 0.0)
        sent[CHUNK * g + XROWS : CHUNK * g + CHUNK, :] = beside


def sweep_kernel(got, head, rech, lo_halo, hi_halo, lo_x, hi_x, cond_out, press_out,
                 head_ext, rech_ext, staged):
    ga, ba = lax.axis_index("ga"), lax.axis_index("ba")
    head_ext[...] = jnp.zeros_like(head_ext)
    rech_ext[...] = jnp.zeros_like(rech_ext)
    for y in range(8):
        at = XROWS * (y + 2)
        head_ext[at + 4 : at + 36, :] = head[pl.ds(y, 32, stride=8), :]
        rech_ext[at + 4 : at + 36, :] = rech[pl.ds(y, 32, stride=8), :]
    for halo, (first, second, only) in ((lo_halo, (1, 0, 1)), (hi_halo, (10, 11, 10))):
        for ref, y, i in ((head_ext, first, 0), (head_ext, second, 1), (rech_ext, only, 2)):
            ref[XROWS * y + 4 : XROWS * y + 36, :] = halo[32 * i : 32 * i + 32, :]
    for block, far, near in ((lo_x, 2, 3), (hi_x, 37, 36)):
        for y in range(8):
            at = XROWS * (y + 2)
            head_ext[at + far : at + far + 1, :] = block[y : y + 1, :]
            head_ext[at + near : at + near + 1, :] = block[8 + y : 9 + y, :]
            rech_ext[at + near : at + near + 1, :] = block[16 + y : 17 + y, :]
        head_ext[XROWS + near : XROWS + near + 1, :] = block[24:25, :]
        head_ext[10 * XROWS + near : 10 * XROWS + near + 1, :] = block[25:26, :]

    lane = lax.broadcasted_iota(jnp.int32, (XROWS, AZ), 1)
    row = lax.broadcasted_iota(jnp.int32, (XROWS, AZ), 0)
    x = row + (32 * ga - 4)
    inside_x = (x >= 0) & (x < AX)

    def in_plane(value):
        total = pltpu.roll(value, 1, 0) + pltpu.roll(value, XROWS - 1, 0)
        total = total + jnp.where(lane > 0, pltpu.roll(value, 1, 1), 0.0)
        return total + jnp.where(lane < AZ - 1, pltpu.roll(value, AZ - 1, 1), 0.0)

    beside = {y: got[CHUNK * y + XROWS : CHUNK * y + CHUNK, :] for y in (0, 1, 6, 7)}
    cond = [beside[6], beside[7]]
    cond += [got[CHUNK * y : CHUNK * y + XROWS, :] for y in range(8)]
    cond += [beside[0], beside[1]]
    planes = [head_ext[XROWS * y : XROWS * y + XROWS, :] for y in range(12)]
    weight = {y: 6.0 * cond[y] + (in_plane(cond[y]) + (cond[y - 1] + cond[y + 1])) for y in range(1, 11)}
    source = {y: 2.0 * rech_ext[XROWS * y : XROWS * y + XROWS, :] for y in range(1, 11)}
    for sweep in range(2):
        flow = {y: cond[y] * planes[y] for y in range(sweep, 12 - sweep)}
        new = dict()
        for y in range(sweep + 1, 11 - sweep):
            heads = in_plane(planes[y]) + (planes[y - 1] + planes[y + 1])
            flows = in_plane(flow[y]) + (flow[y - 1] + flow[y + 1])
            new[y] = (source[y] + (cond[y] * heads + flows)) / weight[y]
            if sweep == 0:
                inside = inside_x
                if y == 1:
                    inside = inside & (ba > 0)
                if y == 10:
                    inside = inside & (ba < BA - 1)
                new[y] = jnp.where(inside, new[y], 0.0)
        planes = new
    for y in range(8):
        cond_out[pl.ds(y, 32, stride=8), :] = got[CHUNK * y + 4 : CHUNK * y + 36, :]
        staged[...] = planes[y + 2]
        press_out[pl.ds(y, 32, stride=8), :] = staged[4:36, :]


def kernel_call(kernel, outs, inputs, scratch=(), held=(), outs_held=(), vmem=VMEM, flops=0, aliases=None):
    whole = pl.BlockSpec(memory_space=pltpu.VMEM)
    there = pl.BlockSpec(memory_space=pl.ANY)
    return pl.pallas_call(
        kernel,
        out_shape=[jax.ShapeDtypeStruct(shape, f32) for shape in outs],
        in_specs=[there if i in held else whole for i in range(len(inputs))],
        out_specs=[there if i in outs_held else whole for i in range(len(outs))],
        scratch_shapes=list(scratch),
        input_output_aliases=aliases or {},
        compiler_params=pltpu.CompilerParams(vmem_limit_bytes=vmem),
        cost_estimate=pl.CostEstimate(flops=flops, bytes_accessed=6 * 2**20, transcendentals=0) if flops else None,
    )(*inputs)


def steps(axis):
    up = [(i, i + 1) for i in range(lax.axis_size(axis) - 1)]
    return up, [(j, i) for i, j in up]


def body(noise, amplitude, recharge, head_guess):
    x_fwd, y_fwd, z_fwd, z_inv, x_inv = (jnp.asarray(t) for t in tables())
    recharge = recharge.reshape(256, AZ)
    head = head_guess.reshape(256, AZ)
    memory, sems = pltpu.VMEM, pltpu.SemaphoreType.DMA
    (sent,) = kernel_call(
        enter_kernel, [(8 * DEVS, 128)], [noise.reshape(512, EX), x_fwd],
        [memory((512, EX), f32), memory(x_fwd.shape, bf16), memory((8 * DEVS, 128), f32), sems((3,))],
        held=(0, 1), outs_held=(0,), flops=10**9,
    )
    got = lax.all_to_all(sent, ("ba", "ga"), 0, 0, tiled=True)
    half, plane = (BA // 2, 16, EZ), (BA // 2, 2, 16, EZ)
    keep, give, amp_first, below, above = kernel_call(
        edges_kernel, [plane, half, (16, EZ), (96, AZ), (96, AZ)], [amplitude, head, recharge],
        [memory((16, 40, EZ), f32), sems((1,))], held=(0,),
    )
    other = lax.ppermute(give, "ba", [(i, i ^ 1) for i in range(BA)])
    zero_near = lax.ppermute(amp_first, "ga", [(0, PACKED_GA)])
    pairs = [(b + 1, PACKED_GA * BA + b) for b in range(BA // 2, BA, 2)]
    zero_far = lax.ppermute(amp_first, ("ga", "ba"), pairs)
    amp_row = lax.ppermute(amp_first, "ba", [(BA // 2, 0)])
    up, down = steps("ba")
    hi_halo = lax.ppermute(below, "ba", down)
    lo_halo = lax.ppermute(above, "ba", up)
    (amp_sent,) = kernel_call(
        join_kernel, [plane], [keep, other, zero_near, zero_far, got, lo_halo, hi_halo],
        [sems((2,))], held=(0, 4, 5, 6), outs_held=(0,), vmem=4 * 2**20, aliases={0: 0},
    )
    halves = [list(range(side, BA, 2)) for side in range(2)]
    amp = lax.all_to_all(amp_sent.reshape(EY, EZ), "ba", 0, 0, tiled=True, axis_index_groups=halves)
    spectrum, to_up, to_down = kernel_call(
        forward_kernel, [(2, EY, EZ), (32, AZ), (32, AZ)], [got, y_fwd, z_fwd, head, recharge, lo_halo, hi_halo],
        [memory(value.shape, value.dtype) for value in (got, y_fwd, z_fwd)]
        + [memory((2, 512, 512), bf16), memory((2, EY, EZ), f32), memory((80, AZ), f32), sems((13,))],
        held=range(7), outs_held=(0,), flops=3 * 10**9,
    )
    (sent,) = kernel_call(
        inverse_kernel, [(4 * AY, AZ)],
        [spectrum, amp.reshape(plane), zero_near, amp_row, z_inv, y_fwd],
        [memory((2, EY, EZ), f32), memory(plane, f32), memory((2, 2, AY, EY), bf16), memory(z_inv.shape, bf16)]
        + [memory((16, EZ), f32)] * 2 + [memory((2, 2, EY, 2 * AZ), bf16), memory((EY, EZ), f32), sems((7,))],
        held=range(6),
    )
    got = lax.all_to_all(sent, ("ba", "ga"), 0, 0, tiled=True)
    up, down = steps("ga")
    lo_x = lax.ppermute(to_up, "ga", up)
    hi_x = lax.ppermute(to_down, "ga", down)
    (sent,) = kernel_call(
        field_kernel, [(CHUNK * GA, AZ)], [got, x_inv, lo_x, hi_x],
        [memory(x_inv.shape, bf16), sems((1,))], held=(1, 2, 3), vmem=VMEM_END,
    )
    got = lax.all_to_all(sent, "ga", 0, 0, tiled=True)
    ext = pltpu.VMEM((12 * XROWS, AZ), f32)
    conductivity, pressure = kernel_call(
        sweep_kernel, [(256, AZ), (256, AZ)],
        [got, head, recharge, lo_halo, hi_halo, lo_x, hi_x],
        [ext, ext, pltpu.VMEM((XROWS, AZ), f32)], vmem=VMEM_END,
    )
    return conductivity.reshape(32, 8, AZ), pressure.reshape(32, 8, AZ)


def solution(mesh):
    placed = (P("ba", "ga", None), P("ba", "ga", None), P("ga", "ba", None), P("ga", "ba", None))
    return jax.shard_map(
        body,
        mesh=mesh,
        in_specs=placed,
        out_specs=(P("ga", "ba", None), P("ga", "ba", None)),
        check_vma=False,
    )
```

```python
import functools
import math

import jax
import jax.numpy as jnp
import ml_dtypes
import numpy as np
from jax import lax
from jax.experimental import pallas as pl
from jax.experimental.pallas import tpu as pltpu
from jax.sharding import PartitionSpec as P

AX, AY, AZ = 256, 256, 128
EX, EY, EZ = 512, 512, 256
GA, BA = 8, 32
DEVS = GA * BA
PACKED_GA = 4
XROWS = 40
CHUNK = XROWS + 24
VMEM = 60 * 2**20
VMEM_END = 16 * 2**20
f32, bf16 = jnp.float32, jnp.bfloat16


def split_np(table):
    high = table.astype(np.float32).astype(ml_dtypes.bfloat16)
    low = (table - high.astype(np.float64)).astype(np.float32).astype(ml_dtypes.bfloat16)
    return np.stack([high, low])


def trig(rows, cols, period):
    angles = (np.outer(rows, cols) % period) * (2.0 * math.pi / period)
    return np.cos(angles), np.sin(angles)


def kx_of():
    ids = np.zeros(DEVS, np.int64)
    for b in range(BA):
        for g in range(GA):
            if b:
                kx = 64 * g + b
            elif g < PACKED_GA:
                kx = 64 * g + 32
            else:
                kx = -1 if g == PACKED_GA else 64 * g
            ids[b * GA + g] = kx
    return ids


@functools.cache
def tables():
    kx = kx_of()
    packed = kx < 0
    alternating = 1.0 - 2.0 * (np.arange(EX) % 2)
    cos, sin = trig(np.maximum(kx, 0), np.arange(EX), EX)
    wide_re, wide_im = cos.copy(), -sin
    wide_re[packed], wide_im[packed] = alternating, 1.0
    x_fwd = np.concatenate([wide_re, wide_im])

    y_fwd = np.stack(trig(np.arange(EY), np.arange(EY), EY))

    half, quarter, block = np.meshgrid(np.arange(2), np.arange(4), np.arange(BA), indexing="ij")
    z_order = (8 * block + 2 * quarter + half).reshape(-1)
    z_fwd = np.concatenate(trig(z_order, np.arange(EZ), EZ), 1)
    z_inv = np.concatenate(trig(np.arange(EZ), np.arange(AZ), EZ), 1)

    xs = np.clip((32 * np.arange(GA)[:, None] - 4 + np.arange(XROWS)).reshape(-1), 0, AX - 1)
    cos, sin = trig(xs, np.maximum(kx, 0), EX)
    back_re, back_im = 2.0 * cos, -2.0 * sin
    back_re[:, packed] = alternating[xs][:, None]
    back_im[:, packed] = 1.0
    x_inv = np.concatenate([back_re, back_im], 1) / (EX * EY * EZ)
    return tuple(split_np(t) for t in (x_fwd, y_fwd, z_fwd, z_inv, x_inv))


def split(value):
    high = value.astype(bf16)
    return high, (value - high.astype(f32)).astype(bf16)


def dot3(a, b, rhs_dim=0):
    dims = (((1,), (rhs_dim,)), ((), ()))
    mul = functools.partial(lax.dot_general, dimension_numbers=dims, preferred_element_type=f32)
    return mul(a[0], b[0]) + (mul(a[0], b[1]) + mul(a[1], b[0]))


def fetch(pairs, sems):
    copies = [pltpu.make_async_copy(src, dst, sems.at[i]) for i, (src, dst) in enumerate(pairs)]
    for copy in copies:
        copy.start()
    return copies


def enter_kernel(noise, table, sent, noise_in, table_in, out, sems):
    pairs = [(table, table_in), (noise.at[0:256, :], noise_in.at[0:256, :]),
             (noise.at[256:512, :], noise_in.at[256:512, :])]
    copies = fetch(pairs, sems)
    copies[0].wait()
    for part in range(2):
        copies[1 + part].wait()
        rows = split(noise_in[256 * part : 256 * part + 256, :])
        for c in range(2):
            own = slice(256 * c, 256 * c + 256)
            result = dot3((table_in[0, own, :], table_in[1, own, :]), rows, 1)
            for q in range(2):
                at = pl.ds(4 * c + 2 * part + q, DEVS, stride=8)
                out[at, :] = result[:, 128 * q : 128 * q + 128]
    pltpu.sync_copy(out, sent)


def edges_kernel(amp, head, rech, keep, give, first, below, above, amp_in, sems):
    ga, ba = lax.axis_index("ga"), lax.axis_index("ba")
    (copy,) = fetch([(amp.at[:, 0:40, :], amp_in)], sems)
    for out, near, far in ((below, 0, 1), (above, 7, 6)):
        for i, (ref, y) in enumerate(((head, near), (head, far), (rech, near))):
            out[32 * i : 32 * i + 32, :] = ref[pl.ds(y, 32, stride=8), :]
    copy.wait()
    even = lax.rem(ba, 2) == 0
    for half in range(2):
        lanes = slice(128 * half, 128 * half + 128)
        for b in range(0, BA, 2):
            near, far = amp_in[:, b, lanes], amp_in[:, b + 1, lanes]
            if b == 0:
                first[:, lanes] = near
                near = jnp.where(ga < PACKED_GA, amp_in[:, 32, lanes], near)
            keep[b // 2, 0, :, lanes] = jnp.where(even, near, far)
            give[b // 2, :, lanes] = jnp.where(even, far, near)


def join_kernel(keep, other, zero_near, zero_far, got, lo_halo, hi_halo, sent, sems):
    ga, ba = lax.axis_index("ga"), lax.axis_index("ba")
    (copy,) = fetch([(other, sent.at[:, 1])], sems)
    copy.wait()

    @pl.when((ga == PACKED_GA) & (ba >= BA // 2) & (lax.rem(ba, 2) == 0))
    def _():
        for copy in fetch([(zero_near, sent.at[0, 0]), (zero_far, sent.at[0, 1])], sems):
            copy.wait()


def mirror_of(value):
    ones = []
    for size in value.shape:
        i = lax.broadcasted_iota(jnp.int32, (size, size), 0)
        j = lax.broadcasted_iota(jnp.int32, (size, size), 1)
        ones.append((((i + j) == 0) | ((i + j) == size)).astype(bf16))
    total = None
    for _ in range(3):
        part = value.astype(bf16)
        value = value - part.astype(f32)
        part = jnp.dot(ones[0], part, preferred_element_type=f32).astype(bf16)
        part = jnp.dot(part, ones[1], preferred_element_type=f32)
        total = part if total is None else total + part
    return total


def forward_kernel(got, y_fwd, z_fwd, head, rech, lo_halo, hi_halo, spectrum, up, down,
                   got_in, y_fwd_in, z_fwd_in, rows, held, edge, sems):
    pairs = [(got, got_in), (y_fwd, y_fwd_in), (z_fwd, z_fwd_in), (head.at[0:16, :], edge.at[0:16, :]),
             (head.at[240:256, :], edge.at[16:32, :]), (rech.at[0:8, :], edge.at[32:40, :]),
             (rech.at[248:256, :], edge.at[40:48, :])]
    pairs += [(halo.at[x : x + 8, :], edge.at[48 + 16 * i + x // 3 : 56 + 16 * i + x // 3, :])
              for i, halo in enumerate((lo_halo, hi_halo)) for x in (0, 24)]
    copies = fetch(pairs, sems)
    copies[0].wait()
    low_half = lax.broadcasted_iota(jnp.int32, (BA, 128), 1) < 64
    for c in range(2):
        for q in range(4):
            for p in range(4):
                even = got_in[pl.ds(16 * p + 4 * c + q, BA, stride=64), :]
                odd = got_in[pl.ds(16 * p + 8 + 4 * c + q, BA, stride=64), :]
                first = jnp.where(low_half, even, pltpu.roll(odd, 64, 1))
                second = jnp.where(low_half, pltpu.roll(even, 64, 1), odd)
                for half, value in enumerate((first, second)):
                    at = slice(256 * c + 128 * half + 32 * q, 256 * c + 128 * half + 32 * q + 32)
                    high, low = split(value)
                    rows[0, at, 128 * p : 128 * p + 128] = high
                    rows[1, at, 128 * p : 128 * p + 128] = low
    leaving = []
    for part in range(2):
        ky = slice(256 * part, 256 * part + 256)
        data = (rows[0], rows[1])
        if part == 0:
            copies[1].wait()
        by_cos = dot3((y_fwd_in[0, 0, ky, :], y_fwd_in[1, 0, ky, :]), data, 1)
        by_sin = dot3((y_fwd_in[0, 1, ky, :], y_fwd_in[1, 1, ky, :]), data, 1)
        real = by_cos[:, :256] + by_sin[:, 256:]
        imag = by_cos[:, 256:] - by_sin[:, :256]
        if part == 0:
            copies[2].wait()
        forward = (z_fwd_in[0], z_fwd_in[1])
        real, imag = dot3(split(real), forward), dot3(split(imag), forward)
        real, imag = real[:, :256] + imag[:, 256:], imag[:, :256] - real[:, 256:]

        held[0, ky, :] = real
        held[1, ky, :] = imag
        leaving += fetch([(held.at[:, ky, :], spectrum.at[:, ky, :])], sems.at[pl.ds(11 + part, 1)])
    for copy in copies[3:]:
        copy.wait()
    corner = lax.broadcasted_iota(jnp.int32, (8, AZ), 0)
    for out, far, near, rech_at, x in ((up, 16, 24, 40, 15), (down, 8, 0, 32, 0)):
        out[0:8, :] = edge[far : far + 8, :]
        out[8:16, :] = edge[near : near + 8, :]
        out[16:24, :] = edge[rech_at : rech_at + 8, :]
        out[24:32, :] = jnp.where(corner == 0, edge[48 + x : 49 + x, :], edge[64 + x : 65 + x, :])
    for copy in leaving:
        copy.wait()


def inverse_kernel(spectrum, amp, amp_row0, amp_row256, z_inv, y_fwd, sent,
                   spectrum_in, amp_in, y_fwd_in, z_inv_in, row0_in, row256_in, lines, amps, sems):
    ga, ba = lax.axis_index("ga"), lax.axis_index("ba")
    packed = (ga == PACKED_GA) & (ba == 0)
    side = lax.rem(ba, 2)
    pairs = [(amp.at[:, 0], amp_in.at[:, side]), (amp.at[:, 1], amp_in.at[:, 1 - side]),
             (amp_row0, row0_in), (amp_row256, row256_in), (spectrum, spectrum_in), (z_inv, z_inv_in),
             (y_fwd.at[:, :, 0:256, :], y_fwd_in)]
    copies = fetch(pairs, sems)
    for i in range(4):
        copies[i].wait()

    @pl.when(packed)
    def _():
        held = amp_in[...].reshape(EY, EZ)
        mirror = mirror_of(held)
        ky = lax.broadcasted_iota(jnp.int32, (EY, EZ), 0)
        amps[...] = jnp.where(ky == 0, row0_in[0:1, :], jnp.where(ky < 256, mirror, held))
        new = jnp.where(ky == 256, row256_in[0:1, :], jnp.where(ky < 256, held, mirror))
        amp_in[...] = new.reshape(amp_in.shape)

    copies[4].wait()
    copies[5].wait()
    for part in range(2):
        ky = slice(256 * part, 256 * part + 256)
        real, imag = spectrum_in[0, ky, :], spectrum_in[1, ky, :]

        def back(scale, at):
            table = (z_inv_in[0], z_inv_in[1])
            re, im = dot3(split(real * scale), table), dot3(split(imag * scale), table)
            for c, value in enumerate((re[:, :128] - im[:, 128:], im[:, :128] + re[:, 128:])):
                lanes = slice(128 * c, 128 * c + 128)
                lines[at, 0, ky, lanes], lines[at, 1, ky, lanes] = split(value)

        back(amp_in[8 * part : 8 * part + 8].reshape(256, EZ), 0)

        @pl.when(packed)
        def _():
            back(amps[ky, :], 1)

    def inverse(at):
        data = (lines[at, 0], lines[at, 1])
        by_cos = dot3((y_fwd_in[0, 0], y_fwd_in[1, 0]), data)
        by_sin = dot3((y_fwd_in[0, 1], y_fwd_in[1, 1]), data)
        return by_cos[:, :AZ] - by_sin[:, AZ:], by_cos[:, AZ:] + by_sin[:, :AZ]

    copies[6].wait()
    real, imag = inverse(0)

    def store(real, imag):
        lane = lax.broadcasted_iota(jnp.int32, (AY, AZ), 1)
        peer = lax.broadcasted_iota(jnp.int32, (AY, AZ), 0) % GA
        first = jnp.where(lane < 64, real, pltpu.roll(imag, 64, 1))
        second = jnp.where(lane < 64, pltpu.roll(real, 64, 1), imag)
        halo = pltpu.roll(first, AY - 8, 0)
        for g, shift in ((1, 7), (2, 7), (3, 6), (4, -6), (5, -7), (6, -7), (7, -8)):
            moved = pltpu.roll(second if g % 2 else first, (AY - shift) % AY, 0)
            halo = jnp.where(peer == g, moved, halo)
        for i, rows in enumerate((real, imag, halo)):
            sent[pl.ds(i, AY, stride=3), :] = rows

    store(real, imag)

    @pl.when(packed)
    def _():
        store(real, inverse(1)[1])


def field_kernel(got, table, lo_x, hi_x, sent, table_in, sems):
    (copy,) = fetch([(table, table_in)], sems)
    ga, ba = lax.axis_index("ga"), lax.axis_index("ba")
    own = jnp.concatenate([got[pl.ds(c, DEVS, stride=3), :] for c in range(2)], 0)
    halo = got[pl.ds(2, DEVS, stride=3), :]
    halo = jnp.concatenate([halo, pltpu.roll(halo, 64, 1)], 0)
    copy.wait()
    log_field = dot3((table_in[0], table_in[1]), split(jnp.concatenate([own, halo], 1)))
    row = lax.broadcasted_iota(jnp.int32, (XROWS, AZ), 0)
    low_half = lax.broadcasted_iota(jnp.int32, (24, AZ), 1) < 64
    in_half = lax.broadcasted_iota(jnp.int32, (XROWS, AZ), 1) < 64
    halo_inside = jnp.where(ga < GA // 2, ba < BA - 1, ba > 0)
    for g in range(GA):
        x = row + (32 * g - 4)
        inside = (x >= 0) & (x < AX)
        value = log_field[XROWS * g : XROWS * g + XROWS, :]
        sent[CHUNK * g : CHUNK * g + XROWS, :] = jnp.where(inside, jnp.exp(value[:, :AZ]), 0.0)
        beside = jnp.where(inside & halo_inside & in_half, jnp.exp(value[:, AZ:]), 0.0)
        late = jnp.concatenate([beside[24:], beside[32:]], 0)
        sent[CHUNK * g + XROWS : CHUNK * g + CHUNK, :] = jnp.where(low_half, beside[:24], pltpu.roll(late, 64, 1))


def sweep_kernel(got, head, rech, lo_halo, hi_halo, lo_x, hi_x, cond_out, press_out,
                 head_ext, rech_ext, staged):
    ga, ba = lax.axis_index("ga"), lax.axis_index("ba")
    head_ext[...] = jnp.zeros_like(head_ext)
    rech_ext[...] = jnp.zeros_like(rech_ext)
    for y in range(8):
        at = XROWS * (y + 2)
        head_ext[at + 4 : at + 36, :] = head[pl.ds(y, 32, stride=8), :]
        rech_ext[at + 4 : at + 36, :] = rech[pl.ds(y, 32, stride=8), :]
    for halo, (first, second, only) in ((lo_halo, (1, 0, 1)), (hi_halo, (10, 11, 10))):
        for ref, y, i in ((head_ext, first, 0), (head_ext, second, 1), (rech_ext, only, 2)):
            ref[XROWS * y + 4 : XROWS * y + 36, :] = halo[32 * i : 32 * i + 32, :]
    for block, far, near in ((lo_x, 2, 3), (hi_x, 37, 36)):
        for y in range(8):
            at = XROWS * (y + 2)
            head_ext[at + far : at + far + 1, :] = block[y : y + 1, :]
            head_ext[at + near : at + near + 1, :] = block[8 + y : 9 + y, :]
            rech_ext[at + near : at + near + 1, :] = block[16 + y : 17 + y, :]
        head_ext[XROWS + near : XROWS + near + 1, :] = block[24:25, :]
        head_ext[10 * XROWS + near : 10 * XROWS + near + 1, :] = block[25:26, :]

    lane = lax.broadcasted_iota(jnp.int32, (XROWS, AZ), 1)
    row = lax.broadcasted_iota(jnp.int32, (XROWS, AZ), 0)
    x = row + (32 * ga - 4)
    inside_x = (x >= 0) & (x < AX)

    def in_plane(value):
        total = pltpu.roll(value, 1, 0) + pltpu.roll(value, XROWS - 1, 0)
        total = total + jnp.where(lane > 0, pltpu.roll(value, 1, 1), 0.0)
        return total + jnp.where(lane < AZ - 1, pltpu.roll(value, AZ - 1, 1), 0.0)

    low_half = lax.broadcasted_iota(jnp.int32, (24, AZ), 1) < 64

    def beside(i):
        first, second = (got[CHUNK * g + XROWS : CHUNK * g + CHUNK, :] for g in (2 * i, 2 * i + 1))
        early = jnp.where(low_half, first, pltpu.roll(second, 64, 1))
        late = jnp.where(low_half, pltpu.roll(first, 64, 1), second)
        return jnp.concatenate([early, late[:16]], 0)

    cond = [beside(2), beside(3)]
    cond += [got[CHUNK * y : CHUNK * y + XROWS, :] for y in range(8)]
    cond += [beside(0), beside(1)]
    planes = [head_ext[XROWS * y : XROWS * y + XROWS, :] for y in range(12)]
    weight = {y: 6.0 * cond[y] + (in_plane(cond[y]) + (cond[y - 1] + cond[y + 1])) for y in range(1, 11)}
    source = {y: 2.0 * rech_ext[XROWS * y : XROWS * y + XROWS, :] for y in range(1, 11)}
    for sweep in range(2):
        flow = {y: cond[y] * planes[y] for y in range(sweep, 12 - sweep)}
        new = dict()
        for y in range(sweep + 1, 11 - sweep):
            heads = in_plane(planes[y]) + (planes[y - 1] + planes[y + 1])
            flows = in_plane(flow[y]) + (flow[y - 1] + flow[y + 1])
            new[y] = (source[y] + (cond[y] * heads + flows)) / weight[y]
            if sweep == 0:
                inside = inside_x
                if y == 1:
                    inside = inside & (ba > 0)
                if y == 10:
                    inside = inside & (ba < BA - 1)
                new[y] = jnp.where(inside, new[y], 0.0)
        planes = new
    for y in range(8):
        cond_out[pl.ds(y, 32, stride=8), :] = got[CHUNK * y + 4 : CHUNK * y + 36, :]
        staged[...] = planes[y + 2]
        press_out[pl.ds(y, 32, stride=8), :] = staged[4:36, :]


def kernel_call(kernel, outs, inputs, scratch=(), held=(), outs_held=(), vmem=VMEM, flops=0, aliases=None):
    whole = pl.BlockSpec(memory_space=pltpu.VMEM)
    there = pl.BlockSpec(memory_space=pl.ANY)
    return pl.pallas_call(
        kernel,
        out_shape=[jax.ShapeDtypeStruct(shape, f32) for shape in outs],
        in_specs=[there if i in held else whole for i in range(len(inputs))],
        out_specs=[there if i in outs_held else whole for i in range(len(outs))],
        scratch_shapes=list(scratch),
        input_output_aliases=aliases or {},
        compiler_params=pltpu.CompilerParams(vmem_limit_bytes=vmem),
        cost_estimate=pl.CostEstimate(flops=flops, bytes_accessed=6 * 2**20, transcendentals=0) if flops else None,
    )(*inputs)


def steps(axis):
    up = [(i, i + 1) for i in range(lax.axis_size(axis) - 1)]
    return up, [(j, i) for i, j in up]


def body(noise, amplitude, recharge, head_guess):
    x_fwd, y_fwd, z_fwd, z_inv, x_inv = (jnp.asarray(t) for t in tables())
    recharge = recharge.reshape(256, AZ)
    head = head_guess.reshape(256, AZ)
    memory, sems = pltpu.VMEM, pltpu.SemaphoreType.DMA
    (sent,) = kernel_call(
        enter_kernel, [(8 * DEVS, 128)], [noise.reshape(512, EX), x_fwd],
        [memory((512, EX), f32), memory(x_fwd.shape, bf16), memory((8 * DEVS, 128), f32), sems((3,))],
        held=(0, 1), outs_held=(0,), flops=10**9,
    )
    got = lax.all_to_all(sent, ("ba", "ga"), 0, 0, tiled=True)
    half, plane = (BA // 2, 16, EZ), (BA // 2, 2, 16, EZ)
    keep, give, amp_first, below, above = kernel_call(
        edges_kernel, [plane, half, (16, EZ), (96, AZ), (96, AZ)], [amplitude, head, recharge],
        [memory((16, 40, EZ), f32), sems((1,))], held=(0,),
    )
    other = lax.ppermute(give, "ba", [(i, i ^ 1) for i in range(BA)])
    zero_near = lax.ppermute(amp_first, "ga", [(0, PACKED_GA)])
    pairs = [(b + 1, PACKED_GA * BA + b) for b in range(BA // 2, BA, 2)]
    zero_far = lax.ppermute(amp_first, ("ga", "ba"), pairs)
    amp_row = lax.ppermute(amp_first, "ba", [(BA // 2, 0)])
    up, down = steps("ba")
    hi_halo = lax.ppermute(below, "ba", down)
    lo_halo = lax.ppermute(above, "ba", up)
    (amp_sent,) = kernel_call(
        join_kernel, [plane], [keep, other, zero_near, zero_far, got, lo_halo, hi_halo],
        [sems((2,))], held=(0, 4, 5, 6), outs_held=(0,), vmem=4 * 2**20, aliases={0: 0},
    )
    halves = [list(range(side, BA, 2)) for side in range(2)]
    amp = lax.all_to_all(amp_sent.reshape(EY, EZ), "ba", 0, 0, tiled=True, axis_index_groups=halves)
    spectrum, to_up, to_down = kernel_call(
        forward_kernel, [(2, EY, EZ), (32, AZ), (32, AZ)], [got, y_fwd, z_fwd, head, recharge, lo_halo, hi_halo],
        [memory(value.shape, value.dtype) for value in (got, y_fwd, z_fwd)]
        + [memory((2, 512, 512), bf16), memory((2, EY, EZ), f32), memory((80, AZ), f32), sems((13,))],
        held=range(7), outs_held=(0,), flops=3 * 10**9,
    )
    (sent,) = kernel_call(
        inverse_kernel, [(3 * AY, AZ)],
        [spectrum, amp.reshape(plane), zero_near, amp_row, z_inv, y_fwd],
        [memory((2, EY, EZ), f32), memory(plane, f32), memory((2, 2, AY, EY), bf16), memory(z_inv.shape, bf16)]
        + [memory((16, EZ), f32)] * 2 + [memory((2, 2, EY, 2 * AZ), bf16), memory((EY, EZ), f32), sems((7,))],
        held=range(6),
    )
    sent = sent.reshape(DEVS, 1, 3 * AZ)
    got = lax.all_to_all(sent, ("ba", "ga"), 0, 0, tiled=True).reshape(3 * DEVS, AZ)
    up, down = steps("ga")
    lo_x = lax.ppermute(to_up, "ga", up)
    hi_x = lax.ppermute(to_down, "ga", down)
    (sent,) = kernel_call(
        field_kernel, [(CHUNK * GA, AZ)], [got, x_inv, lo_x, hi_x],
        [memory(x_inv.shape, bf16), sems((1,))], held=(1, 2, 3), vmem=VMEM_END,
    )
    got = lax.all_to_all(sent, "ga", 0, 0, tiled=True)
    ext = pltpu.VMEM((12 * XROWS, AZ), f32)
    conductivity, pressure = kernel_call(
        sweep_kernel, [(256, AZ), (256, AZ)],
        [got, head, recharge, lo_halo, hi_halo, lo_x, hi_x],
        [ext, ext, pltpu.VMEM((XROWS, AZ), f32)], vmem=VMEM_END,
    )
    return conductivity.reshape(32, 8, AZ), pressure.reshape(32, 8, AZ)


def solution(mesh):
    placed = (P("ba", "ga", None), P("ba", "ga", None), P("ga", "ba", None), P("ga", "ba", None))
    return jax.shard_map(
        body,
        mesh=mesh,
        in_specs=placed,
        out_specs=(P("ga", "ba", None), P("ga", "ba", None)),
        check_vma=False,
    )
```

```python
import functools
import math

import jax
import jax.numpy as jnp
import ml_dtypes
import numpy as np
from jax import lax
from jax.experimental import pallas as pl
from jax.experimental.pallas import tpu as pltpu
from jax.sharding import PartitionSpec as P

AX, AY, AZ = 256, 256, 128
EX, EY, EZ = 512, 512, 256
GA, BA = 8, 32
DEVS = GA * BA
PACKED_GA = 4
XROWS = 40
CHUNK = XROWS + 24
VMEM = 60 * 2**20
VMEM_END = 16 * 2**20
f32, bf16 = jnp.float32, jnp.bfloat16


def split_np(table):
    high = table.astype(np.float32).astype(ml_dtypes.bfloat16)
    low = (table - high.astype(np.float64)).astype(np.float32).astype(ml_dtypes.bfloat16)
    return np.stack([high, low])


def trig(rows, cols, period):
    angles = (np.outer(rows, cols) % period) * (2.0 * math.pi / period)
    return np.cos(angles), np.sin(angles)


def kx_of():
    ids = np.zeros(DEVS, np.int64)
    for b in range(BA):
        for g in range(GA):
            if b:
                kx = 64 * g + b
            elif g < PACKED_GA:
                kx = 64 * g + 32
            else:
                kx = -1 if g == PACKED_GA else 64 * g
            ids[b * GA + g] = kx
    return ids


@functools.cache
def tables():
    kx = kx_of()
    packed = kx < 0
    alternating = 1.0 - 2.0 * (np.arange(EX) % 2)
    cos, sin = trig(np.maximum(kx, 0), np.arange(EX), EX)
    wide_re, wide_im = cos.copy(), -sin
    wide_re[packed], wide_im[packed] = alternating, 1.0
    x_fwd = np.stack([wide_re, wide_im]).reshape(2, BA // 2, 2, GA, EX).transpose(0, 2, 1, 3, 4)
    x_fwd = x_fwd.reshape(2 * DEVS, EX)[:, : EX // 2]

    y_fwd = np.stack(trig(np.arange(EY), np.arange(EY), EY))

    half, quarter, block = np.meshgrid(np.arange(2), np.arange(4), np.arange(BA), indexing="ij")
    z_order = (8 * block + 2 * quarter + half).reshape(-1)
    z_fwd = np.concatenate(trig(z_order, np.arange(EZ), EZ), 1)
    z_inv = np.concatenate(trig(np.arange(EZ), np.arange(AZ), EZ), 1)

    xs = np.clip((32 * np.arange(GA)[:, None] - 4 + np.arange(XROWS)).reshape(-1), 0, AX - 1)
    cos, sin = trig(xs, np.maximum(kx, 0), EX)
    back_re, back_im = 2.0 * cos, -2.0 * sin
    back_re[:, packed] = alternating[xs][:, None]
    back_im[:, packed] = 1.0
    x_inv = np.concatenate([back_re, back_im], 1) / (EX * EY * EZ)
    return tuple(split_np(t) for t in (x_fwd, y_fwd, z_fwd, z_inv, x_inv))


def split(value):
    high = value.astype(bf16)
    return high, (value - high.astype(f32)).astype(bf16)


def dot3(a, b, rhs_dim=0):
    dims = (((1,), (rhs_dim,)), ((), ()))
    mul = functools.partial(lax.dot_general, dimension_numbers=dims, preferred_element_type=f32)
    return mul(a[0], b[0]) + (mul(a[0], b[1]) + mul(a[1], b[0]))


def fetch(pairs, sems):
    copies = [pltpu.make_async_copy(src, dst, sems.at[i]) for i, (src, dst) in enumerate(pairs)]
    for copy in copies:
        copy.start()
    return copies


def enter_kernel(noise, table, sent, noise_in, table_in, out, sems):
    pairs = [(table, table_in), (noise.at[0:256, :], noise_in.at[0:256, :]),
             (noise.at[256:512, :], noise_in.at[256:512, :])]
    copies = fetch(pairs, sems)
    copies[0].wait()
    for part in range(2):
        copies[1 + part].wait()
        rows = slice(256 * part, 256 * part + 256)
        early, late = noise_in[rows, 0:256], noise_in[rows, 256:512]
        for parity, value in enumerate((early + late, early - late)):
            folded = split(value)
            for c in range(2):
                own = slice(256 * c + 128 * parity, 256 * c + 128 * parity + 128)
                result = dot3((table_in[0, own, :], table_in[1, own, :]), folded, 1)
                for pair in range(BA // 2):
                    for q in range(2):
                        first = 8 * GA * (2 * pair + parity) + 4 * c + 2 * part + q
                        tile = result[GA * pair : GA * pair + GA, 128 * q : 128 * q + 128]
                        out[pl.ds(first, GA, stride=8), :] = tile
    pltpu.sync_copy(out, sent)


def edges_kernel(amp, head, rech, keep, give, first, below, above, amp_in, sems):
    ga, ba = lax.axis_index("ga"), lax.axis_index("ba")
    (copy,) = fetch([(amp.at[:, 0:40, :], amp_in)], sems)
    for out, near, far in ((below, 0, 1), (above, 7, 6)):
        for i, (ref, y) in enumerate(((head, near), (head, far), (rech, near))):
            out[32 * i : 32 * i + 32, :] = ref[pl.ds(y, 32, stride=8), :]
    copy.wait()
    even = lax.rem(ba, 2) == 0
    for half in range(2):
        lanes = slice(128 * half, 128 * half + 128)
        for b in range(0, BA, 2):
            near, far = amp_in[:, b, lanes], amp_in[:, b + 1, lanes]
            if b == 0:
                first[:, lanes] = near
                near = jnp.where(ga < PACKED_GA, amp_in[:, 32, lanes], near)
            keep[b // 2, 0, :, lanes] = jnp.where(even, near, far)
            give[b // 2, :, lanes] = jnp.where(even, far, near)


def join_kernel(keep, other, zero_near, zero_far, got, lo_halo, hi_halo, sent, sems):
    ga, ba = lax.axis_index("ga"), lax.axis_index("ba")
    (copy,) = fetch([(other, sent.at[:, 1])], sems)
    copy.wait()

    @pl.when((ga == PACKED_GA) & (ba >= BA // 2) & (lax.rem(ba, 2) == 0))
    def _():
        for copy in fetch([(zero_near, sent.at[0, 0]), (zero_far, sent.at[0, 1])], sems):
            copy.wait()


def mirror_of(value):
    ones = []
    for size in value.shape:
        i = lax.broadcasted_iota(jnp.int32, (size, size), 0)
        j = lax.broadcasted_iota(jnp.int32, (size, size), 1)
        ones.append((((i + j) == 0) | ((i + j) == size)).astype(bf16))
    total = None
    for _ in range(3):
        part = value.astype(bf16)
        value = value - part.astype(f32)
        part = jnp.dot(ones[0], part, preferred_element_type=f32).astype(bf16)
        part = jnp.dot(part, ones[1], preferred_element_type=f32)
        total = part if total is None else total + part
    return total


def forward_kernel(got, y_fwd, z_fwd, head, rech, lo_halo, hi_halo, spectrum, up, down,
                   got_in, y_fwd_in, z_fwd_in, rows, held, edge, sems):
    pairs = [(got, got_in), (y_fwd, y_fwd_in), (z_fwd, z_fwd_in), (head.at[0:16, :], edge.at[0:16, :]),
             (head.at[240:256, :], edge.at[16:32, :]), (rech.at[0:8, :], edge.at[32:40, :]),
             (rech.at[248:256, :], edge.at[40:48, :])]
    pairs += [(halo.at[x : x + 8, :], edge.at[48 + 16 * i + x // 3 : 56 + 16 * i + x // 3, :])
              for i, halo in enumerate((lo_halo, hi_halo)) for x in (0, 24)]
    copies = fetch(pairs, sems)
    copies[0].wait()
    low_half = lax.broadcasted_iota(jnp.int32, (BA, 128), 1) < 64
    for c in range(2):
        for q in range(4):
            for p in range(4):
                even = got_in[pl.ds(16 * p + 4 * c + q, BA, stride=64), :]
                odd = got_in[pl.ds(16 * p + 8 + 4 * c + q, BA, stride=64), :]
                first = jnp.where(low_half, even, pltpu.roll(odd, 64, 1))
                second = jnp.where(low_half, pltpu.roll(even, 64, 1), odd)
                for half, value in enumerate((first, second)):
                    at = slice(256 * c + 128 * half + 32 * q, 256 * c + 128 * half + 32 * q + 32)
                    high, low = split(value)
                    rows[0, at, 128 * p : 128 * p + 128] = high
                    rows[1, at, 128 * p : 128 * p + 128] = low
    leaving = []
    for part in range(2):
        ky = slice(256 * part, 256 * part + 256)
        data = (rows[0], rows[1])
        if part == 0:
            copies[1].wait()
        by_cos = dot3((y_fwd_in[0, 0, ky, :], y_fwd_in[1, 0, ky, :]), data, 1)
        by_sin = dot3((y_fwd_in[0, 1, ky, :], y_fwd_in[1, 1, ky, :]), data, 1)
        real = by_cos[:, :256] + by_sin[:, 256:]
        imag = by_cos[:, 256:] - by_sin[:, :256]
        if part == 0:
            copies[2].wait()
        forward = (z_fwd_in[0], z_fwd_in[1])
        real, imag = dot3(split(real), forward), dot3(split(imag), forward)
        real, imag = real[:, :256] + imag[:, 256:], imag[:, :256] - real[:, 256:]

        held[0, ky, :] = real
        held[1, ky, :] = imag
        leaving += fetch([(held.at[:, ky, :], spectrum.at[:, ky, :])], sems.at[pl.ds(11 + part, 1)])
    for copy in copies[3:]:
        copy.wait()
    corner = lax.broadcasted_iota(jnp.int32, (8, AZ), 0)
    for out, far, near, rech_at, x in ((up, 16, 24, 40, 15), (down, 8, 0, 32, 0)):
        out[0:8, :] = edge[far : far + 8, :]
        out[8:16, :] = edge[near : near + 8, :]
        out[16:24, :] = edge[rech_at : rech_at + 8, :]
        out[24:32, :] = jnp.where(corner == 0, edge[48 + x : 49 + x, :], edge[64 + x : 65 + x, :])
    for copy in leaving:
        copy.wait()


def inverse_kernel(spectrum, amp, amp_row0, amp_row256, z_inv, y_fwd, sent,
                   spectrum_in, amp_in, y_fwd_in, z_inv_in, row0_in, row256_in, lines, amps, sems):
    ga, ba = lax.axis_index("ga"), lax.axis_index("ba")
    packed = (ga == PACKED_GA) & (ba == 0)
    side = lax.rem(ba, 2)
    pairs = [(amp.at[:, 0], amp_in.at[:, side]), (amp.at[:, 1], amp_in.at[:, 1 - side]),
             (amp_row0, row0_in), (amp_row256, row256_in), (spectrum, spectrum_in), (z_inv, z_inv_in),
             (y_fwd.at[:, :, 0:256, :], y_fwd_in)]
    copies = fetch(pairs, sems)
    for i in range(4):
        copies[i].wait()

    @pl.when(packed)
    def _():
        held = amp_in[...].reshape(EY, EZ)
        mirror = mirror_of(held)
        ky = lax.broadcasted_iota(jnp.int32, (EY, EZ), 0)
        amps[...] = jnp.where(ky == 0, row0_in[0:1, :], jnp.where(ky < 256, mirror, held))
        new = jnp.where(ky == 256, row256_in[0:1, :], jnp.where(ky < 256, held, mirror))
        amp_in[...] = new.reshape(amp_in.shape)

    copies[4].wait()
    copies[5].wait()
    for part in range(2):
        ky = slice(256 * part, 256 * part + 256)
        real, imag = spectrum_in[0, ky, :], spectrum_in[1, ky, :]

        def back(scale, at):
            table = (z_inv_in[0], z_inv_in[1])
            re, im = dot3(split(real * scale), table), dot3(split(imag * scale), table)
            for c, value in enumerate((re[:, :128] - im[:, 128:], im[:, :128] + re[:, 128:])):
                lanes = slice(128 * c, 128 * c + 128)
                lines[at, 0, ky, lanes], lines[at, 1, ky, lanes] = split(value)

        back(amp_in[8 * part : 8 * part + 8].reshape(256, EZ), 0)

        @pl.when(packed)
        def _():
            back(amps[ky, :], 1)

    def inverse(at):
        data = (lines[at, 0], lines[at, 1])
        by_cos = dot3((y_fwd_in[0, 0], y_fwd_in[1, 0]), data)
        by_sin = dot3((y_fwd_in[0, 1], y_fwd_in[1, 1]), data)
        return by_cos[:, :AZ] - by_sin[:, AZ:], by_cos[:, AZ:] + by_sin[:, :AZ]

    copies[6].wait()
    real, imag = inverse(0)

    def store(real, imag):
        lane = lax.broadcasted_iota(jnp.int32, (AY, AZ), 1)
        peer = lax.broadcasted_iota(jnp.int32, (AY, AZ), 0) % GA
        first = jnp.where(lane < 64, real, pltpu.roll(imag, 64, 1))
        second = jnp.where(lane < 64, pltpu.roll(real, 64, 1), imag)
        halo = pltpu.roll(first, AY - 8, 0)
        for g, shift in ((1, 7), (2, 7), (3, 6), (4, -6), (5, -7), (6, -7), (7, -8)):
            moved = pltpu.roll(second if g % 2 else first, (AY - shift) % AY, 0)
            halo = jnp.where(peer == g, moved, halo)
        for i, rows in enumerate((real, imag, halo)):
            sent[pl.ds(i, AY, stride=3), :] = rows

    store(real, imag)

    @pl.when(packed)
    def _():
        store(real, inverse(1)[1])


def field_kernel(got, table, lo_x, hi_x, sent, table_in, sems):
    (copy,) = fetch([(table, table_in)], sems)
    ga, ba = lax.axis_index("ga"), lax.axis_index("ba")
    own = jnp.concatenate([got[pl.ds(c, DEVS, stride=3), :] for c in range(2)], 0)
    halo = got[pl.ds(2, DEVS, stride=3), :]
    halo = jnp.concatenate([halo, pltpu.roll(halo, 64, 1)], 0)
    copy.wait()
    log_field = dot3((table_in[0], table_in[1]), split(jnp.concatenate([own, halo], 1)))
    row = lax.broadcasted_iota(jnp.int32, (XROWS, AZ), 0)
    low_half = lax.broadcasted_iota(jnp.int32, (24, AZ), 1) < 64
    in_half = lax.broadcasted_iota(jnp.int32, (XROWS, AZ), 1) < 64
    halo_inside = jnp.where(ga < GA // 2, ba < BA - 1, ba > 0)
    for g in range(GA):
        x = row + (32 * g - 4)
        inside = (x >= 0) & (x < AX)
        value = log_field[XROWS * g : XROWS * g + XROWS, :]
        sent[CHUNK * g : CHUNK * g + XROWS, :] = jnp.where(inside, jnp.exp(value[:, :AZ]), 0.0)
        beside = jnp.where(inside & halo_inside & in_half, jnp.exp(value[:, AZ:]), 0.0)
        late = jnp.concatenate([beside[24:], beside[32:]], 0)
        sent[CHUNK * g + XROWS : CHUNK * g + CHUNK, :] = jnp.where(low_half, beside[:24], pltpu.roll(late, 64, 1))


def sweep_kernel(got, head, rech, lo_halo, hi_halo, lo_x, hi_x, cond_out, press_out,
                 head_ext, rech_ext, staged):
    ga, ba = lax.axis_index("ga"), lax.axis_index("ba")
    head_ext[...] = jnp.zeros_like(head_ext)
    rech_ext[...] = jnp.zeros_like(rech_ext)
    for y in range(8):
        at = XROWS * (y + 2)
        head_ext[at + 4 : at + 36, :] = head[pl.ds(y, 32, stride=8), :]
        rech_ext[at + 4 : at + 36, :] = rech[pl.ds(y, 32, stride=8), :]
    for halo, (first, second, only) in ((lo_halo, (1, 0, 1)), (hi_halo, (10, 11, 10))):
        for ref, y, i in ((head_ext, first, 0), (head_ext, second, 1), (rech_ext, only, 2)):
            ref[XROWS * y + 4 : XROWS * y + 36, :] = halo[32 * i : 32 * i + 32, :]
    for block, far, near in ((lo_x, 2, 3), (hi_x, 37, 36)):
        for y in range(8):
            at = XROWS * (y + 2)
            head_ext[at + far : at + far + 1, :] = block[y : y + 1, :]
            head_ext[at + near : at + near + 1, :] = block[8 + y : 9 + y, :]
            rech_ext[at + near : at + near + 1, :] = block[16 + y : 17 + y, :]
        head_ext[XROWS + near : XROWS + near + 1, :] = block[24:25, :]
        head_ext[10 * XROWS + near : 10 * XROWS + near + 1, :] = block[25:26, :]

    lane = lax.broadcasted_iota(jnp.int32, (XROWS, AZ), 1)
    row = lax.broadcasted_iota(jnp.int32, (XROWS, AZ), 0)
    x = row + (32 * ga - 4)
    inside_x = (x >= 0) & (x < AX)

    def in_plane(value):
        total = pltpu.roll(value, 1, 0) + pltpu.roll(value, XROWS - 1, 0)
        total = total + jnp.where(lane > 0, pltpu.roll(value, 1, 1), 0.0)
        return total + jnp.where(lane < AZ - 1, pltpu.roll(value, AZ - 1, 1), 0.0)

    low_half = lax.broadcasted_iota(jnp.int32, (24, AZ), 1) < 64

    def beside(i):
        first, second = (got[CHUNK * g + XROWS : CHUNK * g + CHUNK, :] for g in (2 * i, 2 * i + 1))
        early = jnp.where(low_half, first, pltpu.roll(second, 64, 1))
        late = jnp.where(low_half, pltpu.roll(first, 64, 1), second)
        return jnp.concatenate([early, late[:16]], 0)

    cond = [beside(2), beside(3)]
    cond += [got[CHUNK * y : CHUNK * y + XROWS, :] for y in range(8)]
    cond += [beside(0), beside(1)]
    planes = [head_ext[XROWS * y : XROWS * y + XROWS, :] for y in range(12)]
    weight = {y: 6.0 * cond[y] + (in_plane(cond[y]) + (cond[y - 1] + cond[y + 1])) for y in range(1, 11)}
    source = {y: 2.0 * rech_ext[XROWS * y : XROWS * y + XROWS, :] for y in range(1, 11)}
    for sweep in range(2):
        flow = {y: cond[y] * planes[y] for y in range(sweep, 12 - sweep)}
        new = dict()
        for y in range(sweep + 1, 11 - sweep):
            heads = in_plane(planes[y]) + (planes[y - 1] + planes[y + 1])
            flows = in_plane(flow[y]) + (flow[y - 1] + flow[y + 1])
            new[y] = (source[y] + (cond[y] * heads + flows)) / weight[y]
            if sweep == 0:
                inside = inside_x
                if y == 1:
                    inside = inside & (ba > 0)
                if y == 10:
                    inside = inside & (ba < BA - 1)
                new[y] = jnp.where(inside, new[y], 0.0)
        planes = new
    for y in range(8):
        cond_out[pl.ds(y, 32, stride=8), :] = got[CHUNK * y + 4 : CHUNK * y + 36, :]
        staged[...] = planes[y + 2]
        press_out[pl.ds(y, 32, stride=8), :] = staged[4:36, :]


def kernel_call(kernel, outs, inputs, scratch=(), held=(), outs_held=(), vmem=VMEM, flops=0, aliases=None):
    whole = pl.BlockSpec(memory_space=pltpu.VMEM)
    there = pl.BlockSpec(memory_space=pl.ANY)
    return pl.pallas_call(
        kernel,
        out_shape=[jax.ShapeDtypeStruct(shape, f32) for shape in outs],
        in_specs=[there if i in held else whole for i in range(len(inputs))],
        out_specs=[there if i in outs_held else whole for i in range(len(outs))],
        scratch_shapes=list(scratch),
        input_output_aliases=aliases or {},
        compiler_params=pltpu.CompilerParams(vmem_limit_bytes=vmem),
        cost_estimate=pl.CostEstimate(flops=flops, bytes_accessed=6 * 2**20, transcendentals=0) if flops else None,
    )(*inputs)


def steps(axis):
    up = [(i, i + 1) for i in range(lax.axis_size(axis) - 1)]
    return up, [(j, i) for i, j in up]


def body(noise, amplitude, recharge, head_guess):
    x_fwd, y_fwd, z_fwd, z_inv, x_inv = (jnp.asarray(t) for t in tables())
    recharge = recharge.reshape(256, AZ)
    head = head_guess.reshape(256, AZ)
    memory, sems = pltpu.VMEM, pltpu.SemaphoreType.DMA
    (sent,) = kernel_call(
        enter_kernel, [(8 * DEVS, 128)], [noise.reshape(512, EX), x_fwd],
        [memory((512, EX), f32), memory(x_fwd.shape, bf16), memory((8 * DEVS, 128), f32), sems((3,))],
        held=(0, 1), outs_held=(0,), flops=10**9,
    )
    got = lax.all_to_all(sent, ("ba", "ga"), 0, 0, tiled=True)
    half, plane = (BA // 2, 16, EZ), (BA // 2, 2, 16, EZ)
    keep, give, amp_first, below, above = kernel_call(
        edges_kernel, [plane, half, (16, EZ), (96, AZ), (96, AZ)], [amplitude, head, recharge],
        [memory((16, 40, EZ), f32), sems((1,))], held=(0,), vmem=8 * 2**20,
    )
    other = lax.ppermute(give, "ba", [(i, i ^ 1) for i in range(BA)])
    zero_near = lax.ppermute(amp_first, "ga", [(0, PACKED_GA)])
    pairs = [(b + 1, PACKED_GA * BA + b) for b in range(BA // 2, BA, 2)]
    zero_far = lax.ppermute(amp_first, ("ga", "ba"), pairs)
    amp_row = lax.ppermute(amp_first, "ba", [(BA // 2, 0)])
    up, down = steps("ba")
    hi_halo = lax.ppermute(below, "ba", down)
    lo_halo = lax.ppermute(above, "ba", up)
    (amp_sent,) = kernel_call(
        join_kernel, [plane], [keep, other, zero_near, zero_far, got, lo_halo, hi_halo],
        [sems((2,))], held=(0, 4, 5, 6), outs_held=(0,), vmem=4 * 2**20, aliases={0: 0},
    )
    halves = [list(range(side, BA, 2)) for side in range(2)]
    amp = lax.all_to_all(amp_sent.reshape(EY, EZ), "ba", 0, 0, tiled=True, axis_index_groups=halves)
    spectrum, to_up, to_down = kernel_call(
        forward_kernel, [(2, EY, EZ), (32, AZ), (32, AZ)], [got, y_fwd, z_fwd, head, recharge, lo_halo, hi_halo],
        [memory(value.shape, value.dtype) for value in (got, y_fwd, z_fwd)]
        + [memory((2, 512, 512), bf16), memory((2, EY, EZ), f32), memory((80, AZ), f32), sems((13,))],
        held=range(7), outs_held=(0,), flops=3 * 10**9,
    )
    (sent,) = kernel_call(
        inverse_kernel, [(3 * AY, AZ)],
        [spectrum, amp.reshape(plane), zero_near, amp_row, z_inv, y_fwd],
        [memory((2, EY, EZ), f32), memory(plane, f32), memory((2, 2, AY, EY), bf16), memory(z_inv.shape, bf16)]
        + [memory((16, EZ), f32)] * 2 + [memory((2, 2, EY, 2 * AZ), bf16), memory((EY, EZ), f32), sems((7,))],
        held=range(6),
    )
    sent = sent.reshape(DEVS, 1, 3 * AZ)
    got = lax.all_to_all(sent, ("ba", "ga"), 0, 0, tiled=True).reshape(3 * DEVS, AZ)
    up, down = steps("ga")
    lo_x = lax.ppermute(to_up, "ga", up)
    hi_x = lax.ppermute(to_down, "ga", down)
    (sent,) = kernel_call(
        field_kernel, [(CHUNK * GA, AZ)], [got, x_inv, lo_x, hi_x],
        [memory(x_inv.shape, bf16), sems((1,))], held=(1, 2, 3), vmem=VMEM_END,
    )
    got = lax.all_to_all(sent, "ga", 0, 0, tiled=True)
    ext = pltpu.VMEM((12 * XROWS, AZ), f32)
    conductivity, pressure = kernel_call(
        sweep_kernel, [(256, AZ), (256, AZ)],
        [got, head, recharge, lo_halo, hi_halo, lo_x, hi_x],
        [ext, ext, pltpu.VMEM((XROWS, AZ), f32)], vmem=VMEM_END,
    )
    return conductivity.reshape(32, 8, AZ), pressure.reshape(32, 8, AZ)


def solution(mesh):
    placed = (P("ba", "ga", None), P("ba", "ga", None), P("ga", "ba", None), P("ga", "ba", None))
    return jax.shard_map(
        body,
        mesh=mesh,
        in_specs=placed,
        out_specs=(P("ga", "ba", None), P("ga", "ba", None)),
        check_vma=False,
    )
```

```python
import functools
import math

import jax
import jax.numpy as jnp
import ml_dtypes
import numpy as np
from jax import lax
from jax.experimental import pallas as pl
from jax.experimental.pallas import tpu as pltpu
from jax.sharding import PartitionSpec as P

AX, AY, AZ = 256, 256, 128
EX, EY, EZ = 512, 512, 256
GA, BA = 8, 32
DEVS = GA * BA
PACKED_GA = 4
XROWS = 40
CHUNK = XROWS + 24
VMEM = 60 * 2**20
VMEM_MIDDLE = 24 * 2**20
VMEM_END = 16 * 2**20
f32, bf16 = jnp.float32, jnp.bfloat16


def split_np(table):
    high = table.astype(np.float32).astype(ml_dtypes.bfloat16)
    low = (table - high.astype(np.float64)).astype(np.float32).astype(ml_dtypes.bfloat16)
    return np.stack([high, low])


def trig(rows, cols, period):
    angles = (np.outer(rows, cols) % period) * (2.0 * math.pi / period)
    return np.cos(angles), np.sin(angles)


def kx_of():
    ids = np.zeros(DEVS, np.int64)
    for b in range(BA):
        for g in range(GA):
            if b:
                kx = 64 * g + b
            elif g < PACKED_GA:
                kx = 64 * g + 32
            else:
                kx = -1 if g == PACKED_GA else 64 * g
            ids[b * GA + g] = kx
    return ids


@functools.cache
def tables():
    kx = kx_of()
    packed = kx < 0
    alternating = 1.0 - 2.0 * (np.arange(EX) % 2)
    cos, sin = trig(np.maximum(kx, 0), np.arange(EX), EX)
    wide_re, wide_im = cos.copy(), -sin
    wide_re[packed], wide_im[packed] = alternating, 1.0
    x_fwd = np.stack([wide_re, wide_im]).reshape(2, BA // 2, 2, GA, EX).transpose(0, 2, 1, 3, 4)
    x_fwd = x_fwd.reshape(2 * DEVS, EX)[:, : EX // 2]

    y_fwd = np.stack(trig(np.arange(EY), np.arange(EY), EY))

    half, quarter, block = np.meshgrid(np.arange(2), np.arange(4), np.arange(BA), indexing="ij")
    z_order = (8 * block + 2 * quarter + half).reshape(-1)
    z_fwd = np.concatenate(trig(z_order, np.arange(EZ), EZ), 1)
    z_inv = np.concatenate(trig(np.arange(EZ), np.arange(AZ), EZ), 1)

    xs = np.clip((32 * np.arange(GA)[:, None] - 4 + np.arange(XROWS)).reshape(-1), 0, AX - 1)
    cos, sin = trig(xs, np.maximum(kx, 0), EX)
    back_re, back_im = 2.0 * cos, -2.0 * sin
    back_re[:, packed] = alternating[xs][:, None]
    back_im[:, packed] = 1.0
    x_inv = np.concatenate([back_re, back_im], 1) / (EX * EY * EZ)
    y_inv = y_fwd[:, :AY]
    y_fwd = np.concatenate([y_fwd[:, 0::2, : EY // 2], y_fwd[:, 1::2, : EY // 2]], 1)
    return tuple(split_np(t) for t in (x_fwd, y_fwd, z_fwd, z_inv, y_inv, x_inv))


def split(value):
    high = value.astype(bf16)
    return high, (value - high.astype(f32)).astype(bf16)


def dot3(a, b, rhs_dim=0):
    dims = (((1,), (rhs_dim,)), ((), ()))
    mul = functools.partial(lax.dot_general, dimension_numbers=dims, preferred_element_type=f32)
    return mul(a[0], b[0]) + (mul(a[0], b[1]) + mul(a[1], b[0]))


def fetch(pairs, sems):
    copies = [pltpu.make_async_copy(src, dst, sems.at[i]) for i, (src, dst) in enumerate(pairs)]
    for copy in copies:
        copy.start()
    return copies


def enter_kernel(noise, table, sent, noise_in, table_in, out, sems):
    pairs = [(table, table_in), (noise.at[0:256, :], noise_in.at[0:256, :]),
             (noise.at[256:512, :], noise_in.at[256:512, :])]
    copies = fetch(pairs, sems)
    copies[0].wait()
    for part in range(2):
        copies[1 + part].wait()
        rows = slice(256 * part, 256 * part + 256)
        early, late = noise_in[rows, 0:256], noise_in[rows, 256:512]
        for parity, value in enumerate((early + late, early - late)):
            folded = split(value)
            for c in range(2):
                own = slice(256 * c + 128 * parity, 256 * c + 128 * parity + 128)
                result = dot3((table_in[0, own, :], table_in[1, own, :]), folded, 1)
                for pair in range(BA // 2):
                    for q in range(2):
                        first = 8 * GA * (2 * pair + parity) + 4 * c + 2 * part + q
                        tile = result[GA * pair : GA * pair + GA, 128 * q : 128 * q + 128]
                        out[pl.ds(first, GA, stride=8), :] = tile
    pltpu.sync_copy(out, sent)


def edges_kernel(amp, head, rech, keep, give, first, below, above, amp_in, sems):
    ga, ba = lax.axis_index("ga"), lax.axis_index("ba")
    (copy,) = fetch([(amp.at[:, 0:40, :], amp_in)], sems)
    for out, near, far in ((below, 0, 1), (above, 7, 6)):
        for i, (ref, y) in enumerate(((head, near), (head, far), (rech, near))):
            out[32 * i : 32 * i + 32, :] = ref[pl.ds(y, 32, stride=8), :]
    copy.wait()
    even = lax.rem(ba, 2) == 0
    for half in range(2):
        lanes = slice(128 * half, 128 * half + 128)
        for b in range(0, BA, 2):
            near, far = amp_in[:, b, lanes], amp_in[:, b + 1, lanes]
            if b == 0:
                first[:, lanes] = near
                near = jnp.where(ga < PACKED_GA, amp_in[:, 32, lanes], near)
            keep[b // 2, 0, :, lanes] = jnp.where(even, near, far)
            give[b // 2, :, lanes] = jnp.where(even, far, near)


def join_kernel(keep, other, zero_near, zero_far, got, lo_halo, hi_halo, sent, sems):
    ga, ba = lax.axis_index("ga"), lax.axis_index("ba")
    (copy,) = fetch([(other, sent.at[:, 1])], sems)
    copy.wait()

    @pl.when((ga == PACKED_GA) & (ba >= BA // 2) & (lax.rem(ba, 2) == 0))
    def _():
        for copy in fetch([(zero_near, sent.at[0, 0]), (zero_far, sent.at[0, 1])], sems):
            copy.wait()


def mirror_of(value):
    i = lax.broadcasted_iota(jnp.int32, (256, 256), 0)
    j = lax.broadcasted_iota(jnp.int32, (256, 256), 1)
    flip = ((i + j) == 256).astype(bf16)
    turn = (((i + j) == 0) | ((i + j) == 256)).astype(bf16)
    value = jnp.concatenate([value[256:], value[:256]], 1)
    total = None
    for _ in range(3):
        part = value.astype(bf16)
        value = value - part.astype(f32)
        part = jnp.dot(flip, part, preferred_element_type=f32).astype(bf16)
        part = jnp.concatenate([part[:, :256], part[:, 256:]], 0)
        part = jnp.dot(part, turn, preferred_element_type=f32)
        total = part if total is None else total + part
    return total


def forward_kernel(got, y_fwd, z_fwd, head, rech, lo_halo, hi_halo, spectrum, up, down,
                   y_fwd_in, z_fwd_in, rows, edge, sems):
    pairs = [(y_fwd, y_fwd_in), (z_fwd, z_fwd_in), (head.at[0:16, :], edge.at[0:16, :]),
             (head.at[240:256, :], edge.at[16:32, :]), (rech.at[0:8, :], edge.at[32:40, :]),
             (rech.at[248:256, :], edge.at[40:48, :])]
    copies = fetch(pairs, sems)
    low_half = lax.broadcasted_iota(jnp.int32, (BA, 128), 1) < 64
    for c in range(2):
        for q in range(4):
            for p in range(2):
                folds = []
                for at in (p, p + 2):
                    even = got[pl.ds(16 * at + 4 * c + q, BA, stride=64), :]
                    odd = got[pl.ds(16 * at + 8 + 4 * c + q, BA, stride=64), :]
                    folds.append((jnp.where(low_half, even, pltpu.roll(odd, 64, 1)),
                                  jnp.where(low_half, pltpu.roll(even, 64, 1), odd)))
                lanes = slice(128 * p, 128 * p + 128)
                for half in range(2):
                    early, late = folds[0][half], folds[1][half]
                    at = slice(256 * c + 128 * half + 32 * q, 256 * c + 128 * half + 32 * q + 32)
                    for parity, value in enumerate((early + late, early - late)):
                        rows[parity, 0, at, lanes], rows[parity, 1, at, lanes] = split(value)
    for part in range(2):
        ky = slice(256 * part, 256 * part + 256)
        data = (rows[part, 0], rows[part, 1])
        if part == 0:
            copies[0].wait()
        by_cos = dot3((y_fwd_in[0, 0, ky, :], y_fwd_in[1, 0, ky, :]), data, 1)
        by_sin = dot3((y_fwd_in[0, 1, ky, :], y_fwd_in[1, 1, ky, :]), data, 1)
        real = by_cos[:, :256] + by_sin[:, 256:]
        imag = by_cos[:, 256:] - by_sin[:, :256]
        if part == 0:
            copies[1].wait()
        forward = (z_fwd_in[0], z_fwd_in[1])
        real, imag = dot3(split(real), forward), dot3(split(imag), forward)
        real, imag = real[:, :256] + imag[:, 256:], imag[:, :256] - real[:, 256:]

        for i, value in enumerate((real[:, :128], real[:, 128:], imag[:, :128], imag[:, 128:])):
            spectrum[pl.ds(512 * i + part, 256, stride=2), :] = value
    for copy in copies[2:]:
        copy.wait()
    corner = lax.broadcasted_iota(jnp.int32, (8, AZ), 0)
    for out, far, near, rech_at, x in ((up, 16, 24, 40, 31), (down, 8, 0, 32, 0)):
        out[0:8, :] = edge[far : far + 8, :]
        out[8:16, :] = edge[near : near + 8, :]
        out[16:24, :] = edge[rech_at : rech_at + 8, :]
        out[24:32, :] = jnp.where(corner == 0, lo_halo[x : x + 1, :], hi_halo[x : x + 1, :])


def inverse_kernel(spectrum, amp, amp_row0, amp_row256, z_inv, y_inv, sent,
                   amp_in, y_inv_in, z_inv_in, lines, amps, out, sems):
    ga, ba = lax.axis_index("ga"), lax.axis_index("ba")
    packed = (ga == PACKED_GA) & (ba == 0)
    side = lax.rem(ba, 2)
    pairs = [(amp.at[:, 0], amp_in.at[:, side]), (amp.at[:, 1], amp_in.at[:, 1 - side]),
             (z_inv, z_inv_in),
             (y_inv, y_inv_in)]
    copies = fetch(pairs, sems)
    for i in range(2):
        copies[i].wait()

    @pl.when(packed)
    def _():
        held = amp_in[...].reshape(EY, EZ)
        mirror = mirror_of(held)
        ky = lax.broadcasted_iota(jnp.int32, (EY, EZ), 0)
        amps[...] = jnp.where(ky == 0, amp_row0[0:1, :], jnp.where(ky < 256, mirror, held))
        new = jnp.where(ky == 256, amp_row256[0:1, :], jnp.where(ky < 256, held, mirror))
        amp_in[...] = new.reshape(amp_in.shape)

    copies[2].wait()
    for part in range(2):
        ky = slice(256 * part, 256 * part + 256)
        quarters = [spectrum[512 * i + 256 * part : 512 * i + 256 * part + 256, :] for i in range(4)]
        real, imag = (jnp.concatenate(quarters[2 * i : 2 * i + 2], 1) for i in range(2))

        def back(scale, at):
            table = (z_inv_in[0], z_inv_in[1])
            re, im = dot3(split(real * scale), table), dot3(split(imag * scale), table)
            for c, value in enumerate((re[:, :128] - im[:, 128:], im[:, :128] + re[:, 128:])):
                lanes = slice(128 * c, 128 * c + 128)
                lines[at, 0, ky, lanes], lines[at, 1, ky, lanes] = split(value)

        back(amp_in[8 * part : 8 * part + 8].reshape(256, EZ), 0)

        @pl.when(packed)
        def _():
            back(amps[ky, :], 1)

    def inverse(at):
        data = (lines[at, 0], lines[at, 1])
        by_cos = dot3((y_inv_in[0, 0], y_inv_in[1, 0]), data)
        by_sin = dot3((y_inv_in[0, 1], y_inv_in[1, 1]), data)
        return by_cos[:, :AZ] - by_sin[:, AZ:], by_cos[:, AZ:] + by_sin[:, :AZ]

    copies[3].wait()
    real, imag = inverse(0)

    def store(real, imag):
        lane = lax.broadcasted_iota(jnp.int32, (AY, AZ), 1)
        peer = lax.broadcasted_iota(jnp.int32, (AY, AZ), 0) % GA
        first = jnp.where(lane < 64, real, pltpu.roll(imag, 64, 1))
        second = jnp.where(lane < 64, pltpu.roll(real, 64, 1), imag)
        halo = pltpu.roll(first, AY - 8, 0)
        for g, shift in ((1, 7), (2, 7), (3, 6), (4, -6), (5, -7), (6, -7), (7, -8)):
            moved = pltpu.roll(second if g % 2 else first, (AY - shift) % AY, 0)
            halo = jnp.where(peer == g, moved, halo)
        for i, rows in enumerate((real, imag, halo)):
            out[pl.ds(i, AY, stride=3), :] = rows

    store(real, imag)

    @pl.when(packed)
    def _():
        store(real, inverse(1)[1])

    pltpu.sync_copy(out, sent)


def field_kernel(got, table, lo_x, hi_x, sent, table_in, sems):
    (copy,) = fetch([(table, table_in)], sems)
    ga, ba = lax.axis_index("ga"), lax.axis_index("ba")
    own = jnp.concatenate([got[pl.ds(c, DEVS, stride=3), :] for c in range(2)], 0)
    halo = got[pl.ds(2, DEVS, stride=3), :]
    halo = jnp.concatenate([halo, pltpu.roll(halo, 64, 1)], 0)
    copy.wait()
    log_field = dot3((table_in[0], table_in[1]), split(jnp.concatenate([own, halo], 1)))
    row = lax.broadcasted_iota(jnp.int32, (XROWS, AZ), 0)
    low_half = lax.broadcasted_iota(jnp.int32, (24, AZ), 1) < 64
    in_half = lax.broadcasted_iota(jnp.int32, (XROWS, AZ), 1) < 64
    halo_inside = jnp.where(ga < GA // 2, ba < BA - 1, ba > 0)
    for g in range(GA):
        x = row + (32 * g - 4)
        inside = (x >= 0) & (x < AX)
        value = log_field[XROWS * g : XROWS * g + XROWS, :]
        sent[CHUNK * g : CHUNK * g + XROWS, :] = jnp.where(inside, jnp.exp(value[:, :AZ]), 0.0)
        beside = jnp.where(inside & halo_inside & in_half, jnp.exp(value[:, AZ:]), 0.0)
        late = jnp.concatenate([beside[24:], beside[32:]], 0)
        sent[CHUNK * g + XROWS : CHUNK * g + CHUNK, :] = jnp.where(low_half, beside[:24], pltpu.roll(late, 64, 1))


def sweep_kernel(got, head, rech, lo_halo, hi_halo, lo_x, hi_x, cond_out, press_out,
                 head_ext, rech_ext, staged):
    ga, ba = lax.axis_index("ga"), lax.axis_index("ba")
    head_ext[...] = jnp.zeros_like(head_ext)
    rech_ext[...] = jnp.zeros_like(rech_ext)
    for y in range(8):
        at = XROWS * (y + 2)
        head_ext[at + 4 : at + 36, :] = head[pl.ds(y, 32, stride=8), :]
        rech_ext[at + 4 : at + 36, :] = rech[pl.ds(y, 32, stride=8), :]
    for halo, (first, second, only) in ((lo_halo, (1, 0, 1)), (hi_halo, (10, 11, 10))):
        for ref, y, i in ((head_ext, first, 0), (head_ext, second, 1), (rech_ext, only, 2)):
            ref[XROWS * y + 4 : XROWS * y + 36, :] = halo[32 * i : 32 * i + 32, :]
    for block, far, near in ((lo_x, 2, 3), (hi_x, 37, 36)):
        for y in range(8):
            at = XROWS * (y + 2)
            head_ext[at + far : at + far + 1, :] = block[y : y + 1, :]
            head_ext[at + near : at + near + 1, :] = block[8 + y : 9 + y, :]
            rech_ext[at + near : at + near + 1, :] = block[16 + y : 17 + y, :]
        head_ext[XROWS + near : XROWS + near + 1, :] = block[24:25, :]
        head_ext[10 * XROWS + near : 10 * XROWS + near + 1, :] = block[25:26, :]

    lane = lax.broadcasted_iota(jnp.int32, (XROWS, AZ), 1)
    row = lax.broadcasted_iota(jnp.int32, (XROWS, AZ), 0)
    x = row + (32 * ga - 4)
    inside_x = (x >= 0) & (x < AX)

    def in_plane(value):
        total = pltpu.roll(value, 1, 0) + pltpu.roll(value, XROWS - 1, 0)
        total = total + jnp.where(lane > 0, pltpu.roll(value, 1, 1), 0.0)
        return total + jnp.where(lane < AZ - 1, pltpu.roll(value, AZ - 1, 1), 0.0)

    low_half = lax.broadcasted_iota(jnp.int32, (24, AZ), 1) < 64

    def beside(i):
        first, second = (got[CHUNK * g + XROWS : CHUNK * g + CHUNK, :] for g in (2 * i, 2 * i + 1))
        early = jnp.where(low_half, first, pltpu.roll(second, 64, 1))
        late = jnp.where(low_half, pltpu.roll(first, 64, 1), second)
        return jnp.concatenate([early, late[:16]], 0)

    cond = [beside(2), beside(3)]
    cond += [got[CHUNK * y : CHUNK * y + XROWS, :] for y in range(8)]
    cond += [beside(0), beside(1)]
    planes = [head_ext[XROWS * y : XROWS * y + XROWS, :] for y in range(12)]
    weight = {y: 6.0 * cond[y] + (in_plane(cond[y]) + (cond[y - 1] + cond[y + 1])) for y in range(1, 11)}
    source = {y: 2.0 * rech_ext[XROWS * y : XROWS * y + XROWS, :] for y in range(1, 11)}
    for sweep in range(2):
        flow = {y: cond[y] * planes[y] for y in range(sweep, 12 - sweep)}
        new = dict()
        for y in range(sweep + 1, 11 - sweep):
            heads = in_plane(planes[y]) + (planes[y - 1] + planes[y + 1])
            flows = in_plane(flow[y]) + (flow[y - 1] + flow[y + 1])
            new[y] = (source[y] + (cond[y] * heads + flows)) / weight[y]
            if sweep == 0:
                inside = inside_x
                if y == 1:
                    inside = inside & (ba > 0)
                if y == 10:
                    inside = inside & (ba < BA - 1)
                new[y] = jnp.where(inside, new[y], 0.0)
        planes = new
    for y in range(8):
        cond_out[pl.ds(y, 32, stride=8), :] = got[CHUNK * y + 4 : CHUNK * y + 36, :]
        staged[...] = planes[y + 2]
        press_out[pl.ds(y, 32, stride=8), :] = staged[4:36, :]


def kernel_call(kernel, outs, inputs, scratch=(), held=(), outs_held=(), vmem=VMEM, flops=0, aliases=None, hbm=()):
    whole = pl.BlockSpec(memory_space=pltpu.VMEM)
    there = pl.BlockSpec(memory_space=pl.ANY)
    pinned = pl.BlockSpec(memory_space=pltpu.HBM)
    return pl.pallas_call(
        kernel,
        out_shape=[jax.ShapeDtypeStruct(shape, f32) for shape in outs],
        in_specs=[pinned if i in hbm else there if i in held else whole for i in range(len(inputs))],
        out_specs=[pinned if i in outs_held else whole for i in range(len(outs))],
        scratch_shapes=list(scratch),
        input_output_aliases=aliases or {},
        compiler_params=pltpu.CompilerParams(vmem_limit_bytes=vmem),
        cost_estimate=pl.CostEstimate(flops=flops, bytes_accessed=6 * 2**20, transcendentals=0) if flops else None,
    )(*inputs)


def steps(axis):
    up = [(i, i + 1) for i in range(lax.axis_size(axis) - 1)]
    return up, [(j, i) for i, j in up]


def body(noise, amplitude, recharge, head_guess):
    x_fwd, y_fwd, z_fwd, z_inv, y_inv, x_inv = (jnp.asarray(t) for t in tables())
    recharge = recharge.reshape(256, AZ)
    head = head_guess.reshape(256, AZ)
    memory, sems = pltpu.VMEM, pltpu.SemaphoreType.DMA
    (sent,) = kernel_call(
        enter_kernel, [(8 * DEVS, 128)], [noise.reshape(512, EX), x_fwd],
        [memory((512, EX), f32), memory(x_fwd.shape, bf16), memory((8 * DEVS, 128), f32), sems((3,))],
        hbm=(0, 1), outs_held=(0,), flops=10**9,
    )
    got = lax.all_to_all(sent, ("ba", "ga"), 0, 0, tiled=True)
    half, plane = (BA // 2, 16, EZ), (BA // 2, 2, 16, EZ)
    keep, give, amp_first, below, above = kernel_call(
        edges_kernel, [plane, half, (16, EZ), (96, AZ), (96, AZ)], [amplitude, head, recharge],
        [memory((16, 40, EZ), f32), sems((1,))], hbm=(0,), vmem=8 * 2**20,
    )
    other = lax.ppermute(give, "ba", [(i, i ^ 1) for i in range(BA)])
    zero_near = lax.ppermute(amp_first, "ga", [(0, PACKED_GA)])
    pairs = [(b + 1, PACKED_GA * BA + b) for b in range(BA // 2, BA, 2)]
    zero_far = lax.ppermute(amp_first, ("ga", "ba"), pairs)
    amp_row = lax.ppermute(amp_first, "ba", [(BA // 2, 0)])
    up, down = steps("ba")
    hi_halo = lax.ppermute(below, "ba", down)
    lo_halo = lax.ppermute(above, "ba", up)
    (amp_sent,) = kernel_call(
        join_kernel, [plane], [keep, other, zero_near, zero_far, got, lo_halo, hi_halo],
        [sems((2,))], held=(0, 4, 5, 6), outs_held=(0,), vmem=4 * 2**20, aliases={0: 0},
    )
    halves = [list(range(side, BA, 2)) for side in range(2)]
    amp = lax.all_to_all(amp_sent.reshape(EY, EZ), "ba", 0, 0, tiled=True, axis_index_groups=halves)
    spectrum, to_up, to_down = kernel_call(
        forward_kernel, [(4 * EY, 128), (32, AZ), (32, AZ)], [got, y_fwd, z_fwd, head, recharge, lo_halo, hi_halo],
        [memory(value.shape, value.dtype) for value in (y_fwd, z_fwd)]
        + [memory((2, 2, 512, 256), bf16), memory((48, AZ), f32), sems((6,))],
        hbm=range(1, 5), flops=3 * 10**9, vmem=VMEM_MIDDLE,
    )
    (sent,) = kernel_call(
        inverse_kernel, [(3 * AY, AZ)],
        [spectrum, amp.reshape(plane), zero_near, amp_row, z_inv, y_inv],
        [memory(plane, f32), memory((2, 2, AY, EY), bf16), memory(z_inv.shape, bf16)]
        + [memory((2, 2, EY, 2 * AZ), bf16), memory((EY, EZ), f32), memory((3 * AY, AZ), f32), sems((4,))],
        hbm=(4, 5), outs_held=(0,), vmem=VMEM_MIDDLE,
    )
    sent = sent.reshape(DEVS, 1, 3 * AZ)
    got = lax.all_to_all(sent, ("ba", "ga"), 0, 0, tiled=True).reshape(3 * DEVS, AZ)
    up, down = steps("ga")
    lo_x = lax.ppermute(to_up, "ga", up)
    hi_x = lax.ppermute(to_down, "ga", down)
    (sent,) = kernel_call(
        field_kernel, [(CHUNK * GA, AZ)], [got, x_inv, lo_x, hi_x],
        [memory(x_inv.shape, bf16), sems((1,))], held=(2, 3), hbm=(1,), vmem=VMEM_END,
    )
    got = lax.all_to_all(sent, "ga", 0, 0, tiled=True)
    ext = pltpu.VMEM((12 * XROWS, AZ), f32)
    conductivity, pressure = kernel_call(
        sweep_kernel, [(256, AZ), (256, AZ)],
        [got, head, recharge, lo_halo, hi_halo, lo_x, hi_x],
        [ext, ext, pltpu.VMEM((XROWS, AZ), f32)], vmem=VMEM_END,
    )
    return conductivity.reshape(32, 8, AZ), pressure.reshape(32, 8, AZ)


def solution(mesh):
    placed = (P("ba", "ga", None), P("ba", "ga", None), P("ga", "ba", None), P("ga", "ba", None))
    return jax.shard_map(
        body,
        mesh=mesh,
        in_specs=placed,
        out_specs=(P("ga", "ba", None), P("ga", "ba", None)),
        check_vma=False,
    )
```

```python
import functools
import math

import jax
import jax.numpy as jnp
import ml_dtypes
import numpy as np
from jax import lax
from jax.experimental import pallas as pl
from jax.experimental.pallas import tpu as pltpu
from jax.sharding import PartitionSpec as P

AX, AY, AZ = 256, 256, 128
EX, EY, EZ = 512, 512, 256
GA, BA = 8, 32
DEVS = GA * BA
PACKED_GA = 4
XROWS = 40
CHUNK = XROWS + 24
VMEM = 60 * 2**20
VMEM_MIDDLE = 24 * 2**20
VMEM_END = 16 * 2**20
f32, bf16 = jnp.float32, jnp.bfloat16


def split_np(table):
    high = table.astype(np.float32).astype(ml_dtypes.bfloat16)
    low = (table - high.astype(np.float64)).astype(np.float32).astype(ml_dtypes.bfloat16)
    return np.stack([high, low])


def trig(rows, cols, period):
    angles = (np.outer(rows, cols) % period) * (2.0 * math.pi / period)
    return np.cos(angles), np.sin(angles)


def kx_of():
    ids = np.zeros(DEVS, np.int64)
    for b in range(BA):
        for g in range(GA):
            if b:
                kx = 64 * g + b
            elif g < PACKED_GA:
                kx = 64 * g + 32
            else:
                kx = -1 if g == PACKED_GA else 64 * g
            ids[b * GA + g] = kx
    return ids


@functools.cache
def tables():
    kx = kx_of()
    packed = kx < 0
    alternating = 1.0 - 2.0 * (np.arange(EX) % 2)
    cos, sin = trig(np.maximum(kx, 0), np.arange(EX), EX)
    wide_re, wide_im = cos.copy(), -sin
    wide_re[packed], wide_im[packed] = alternating, 1.0
    x_fwd = np.stack([wide_re, wide_im]).reshape(2, BA // 2, 2, GA, EX).transpose(0, 2, 1, 3, 4)
    x_fwd = x_fwd.reshape(2 * DEVS, EX)[:, : EX // 2]

    y_fwd = np.stack(trig(np.arange(EY), np.arange(EY), EY))

    half, quarter, block = np.meshgrid(np.arange(2), np.arange(4), np.arange(BA), indexing="ij")
    z_order = (8 * block + 2 * quarter + half).reshape(-1)
    z_fwd = np.concatenate(trig(z_order, np.arange(EZ), EZ), 1)
    z_inv = np.concatenate(trig(np.arange(EZ), np.arange(AZ), EZ), 1)

    xs = np.clip((32 * np.arange(GA)[:, None] - 4 + np.arange(XROWS)).reshape(-1), 0, AX - 1)
    cos, sin = trig(xs, np.maximum(kx, 0), EX)
    back_re, back_im = 2.0 * cos, -2.0 * sin
    back_re[:, packed] = alternating[xs][:, None]
    back_im[:, packed] = 1.0
    x_inv = np.concatenate([back_re, back_im], 1) / (EX * EY * EZ)
    y_inv = y_fwd[:, :AY]
    y_fwd = np.concatenate([y_fwd[:, 0::2, : EY // 2], y_fwd[:, 1::2, : EY // 2]], 1)
    z_fwd = z_fwd.reshape(EZ, 2, EZ).transpose(1, 0, 2)
    forward = np.concatenate([split_np(t).reshape(-1, EZ) for t in (y_fwd, z_fwd)])
    z_inv = split_np(z_inv)
    inverse = np.concatenate([split_np(y_inv).reshape(-1, EY), np.concatenate([z_inv[0], z_inv[1]], 1)])
    return split_np(x_fwd), forward, inverse, split_np(x_inv)


def split(value):
    high = value.astype(bf16)
    return high, (value - high.astype(f32)).astype(bf16)


def dot3(a, b, rhs_dim=0):
    dims = (((1,), (rhs_dim,)), ((), ()))
    mul = functools.partial(lax.dot_general, dimension_numbers=dims, preferred_element_type=f32)
    return mul(a[0], b[0]) + (mul(a[0], b[1]) + mul(a[1], b[0]))


def fetch(pairs, sems):
    copies = [pltpu.make_async_copy(src, dst, sems.at[i]) for i, (src, dst) in enumerate(pairs)]
    for copy in copies:
        copy.start()
    return copies


def enter_kernel(noise, table, sent, noise_in, table_in, out, sems):
    pairs = [(table, table_in), (noise.at[0:256, :], noise_in.at[0:256, :]),
             (noise.at[256:512, :], noise_in.at[256:512, :])]
    copies = fetch(pairs, sems)
    copies[0].wait()
    for part in range(2):
        copies[1 + part].wait()
        rows = slice(256 * part, 256 * part + 256)
        early, late = noise_in[rows, 0:256], noise_in[rows, 256:512]
        for parity, value in enumerate((early + late, early - late)):
            folded = split(value)
            for c in range(2):
                own = slice(256 * c + 128 * parity, 256 * c + 128 * parity + 128)
                result = dot3((table_in[0, own, :], table_in[1, own, :]), folded, 1)
                for pair in range(BA // 2):
                    for q in range(2):
                        first = 8 * GA * (2 * pair + parity) + 4 * c + 2 * part + q
                        tile = result[GA * pair : GA * pair + GA, 128 * q : 128 * q + 128]
                        out[pl.ds(first, GA, stride=8), :] = tile
    pltpu.sync_copy(out, sent)


def edges_kernel(amp, head, rech, keep, give, first, below, above, amp_in, sems):
    ga, ba = lax.axis_index("ga"), lax.axis_index("ba")
    (copy,) = fetch([(amp.at[:, 0:40, :], amp_in)], sems)
    for out, near, far in ((below, 0, 1), (above, 7, 6)):
        for i, (ref, y) in enumerate(((head, near), (head, far), (rech, near))):
            out[32 * i : 32 * i + 32, :] = ref[pl.ds(y, 32, stride=8), :]
    copy.wait()
    even = lax.rem(ba, 2) == 0
    for half in range(2):
        lanes = slice(128 * half, 128 * half + 128)
        for b in range(0, BA, 2):
            near, far = amp_in[:, b, lanes], amp_in[:, b + 1, lanes]
            if b == 0:
                first[:, lanes] = near
                near = jnp.where(ga < PACKED_GA, amp_in[:, 32, lanes], near)
            keep[b // 2, 0, :, lanes] = jnp.where(even, near, far)
            give[b // 2, :, lanes] = jnp.where(even, far, near)


def join_kernel(keep, other, zero_near, zero_far, got, lo_halo, hi_halo, sent, sems):
    ga, ba = lax.axis_index("ga"), lax.axis_index("ba")
    (copy,) = fetch([(other, sent.at[:, 1])], sems)
    copy.wait()

    @pl.when((ga == PACKED_GA) & (ba >= BA // 2) & (lax.rem(ba, 2) == 0))
    def _():
        for copy in fetch([(zero_near, sent.at[0, 0]), (zero_far, sent.at[0, 1])], sems):
            copy.wait()


def mirror_of(value):
    i = lax.broadcasted_iota(jnp.int32, (256, 256), 0)
    j = lax.broadcasted_iota(jnp.int32, (256, 256), 1)
    flip = ((i + j) == 256).astype(bf16)
    turn = (((i + j) == 0) | ((i + j) == 256)).astype(bf16)
    value = jnp.concatenate([value[256:], value[:256]], 1)
    total = None
    for _ in range(3):
        part = value.astype(bf16)
        value = value - part.astype(f32)
        part = jnp.dot(flip, part, preferred_element_type=f32).astype(bf16)
        part = jnp.concatenate([part[:, :256], part[:, 256:]], 0)
        part = jnp.dot(part, turn, preferred_element_type=f32)
        total = part if total is None else total + part
    return total


def forward_kernel(got, table, head, rech, lo_halo, hi_halo, spectrum, up, down,
                   rows, edge, sems):
    pairs = [(head.at[0:16, :], edge.at[0:16, :]),
             (head.at[240:256, :], edge.at[16:32, :]), (rech.at[0:8, :], edge.at[32:40, :]),
             (rech.at[248:256, :], edge.at[40:48, :])]
    copies = fetch(pairs, sems)
    low_half = lax.broadcasted_iota(jnp.int32, (BA, 128), 1) < 64
    for c in range(2):
        for q in range(4):
            for p in range(2):
                folds = []
                for at in (p, p + 2):
                    even = got[pl.ds(16 * at + 4 * c + q, BA, stride=64), :]
                    odd = got[pl.ds(16 * at + 8 + 4 * c + q, BA, stride=64), :]
                    folds.append((jnp.where(low_half, even, pltpu.roll(odd, 64, 1)),
                                  jnp.where(low_half, pltpu.roll(even, 64, 1), odd)))
                lanes = slice(128 * p, 128 * p + 128)
                for half in range(2):
                    early, late = folds[0][half], folds[1][half]
                    at = slice(256 * c + 128 * half + 32 * q, 256 * c + 128 * half + 32 * q + 32)
                    for parity, value in enumerate((early + late, early - late)):
                        rows[parity, 0, at, lanes], rows[parity, 1, at, lanes] = split(value)
    for part in range(2):
        ky = slice(256 * part, 256 * part + 256)
        data = (rows[part, 0], rows[part, 1])
        by_cos, by_sin = (
            dot3([table[at : at + 256, :] for at in (512 * c + 256 * part, 1024 + 512 * c + 256 * part)], data, 1)
            for c in range(2)
        )
        real = by_cos[:, :256] + by_sin[:, 256:]
        imag = by_cos[:, 256:] - by_sin[:, :256]
        forward = [jnp.concatenate([table[at : at + 256, :], table[at + 256 : at + 512, :]], 1) for at in (2048, 2560)]
        real, imag = dot3(split(real), forward), dot3(split(imag), forward)
        real, imag = real[:, :256] + imag[:, 256:], imag[:, :256] - real[:, 256:]

        for i, value in enumerate((real[:, :128], real[:, 128:], imag[:, :128], imag[:, 128:])):
            spectrum[pl.ds(512 * i + part, 256, stride=2), :] = value
    for copy in copies:
        copy.wait()
    corner = lax.broadcasted_iota(jnp.int32, (8, AZ), 0)
    for out, far, near, rech_at, x in ((up, 16, 24, 40, 31), (down, 8, 0, 32, 0)):
        out[0:8, :] = edge[far : far + 8, :]
        out[8:16, :] = edge[near : near + 8, :]
        out[16:24, :] = edge[rech_at : rech_at + 8, :]
        out[24:32, :] = jnp.where(corner == 0, lo_halo[x : x + 1, :], hi_halo[x : x + 1, :])


def inverse_kernel(spectrum, amp, amp_row0, amp_row256, table, sent,
                   amp_in, lines, amps, out, sems):
    ga, ba = lax.axis_index("ga"), lax.axis_index("ba")
    packed = (ga == PACKED_GA) & (ba == 0)
    side = lax.rem(ba, 2)
    pairs = [(amp.at[:, 0], amp_in.at[:, side]), (amp.at[:, 1], amp_in.at[:, 1 - side])]
    copies = fetch(pairs, sems)
    for i in range(2):
        copies[i].wait()

    @pl.when(packed)
    def _():
        held = amp_in[...].reshape(EY, EZ)
        mirror = mirror_of(held)
        ky = lax.broadcasted_iota(jnp.int32, (EY, EZ), 0)
        amps[...] = jnp.where(ky == 0, amp_row0[0:1, :], jnp.where(ky < 256, mirror, held))
        new = jnp.where(ky == 256, amp_row256[0:1, :], jnp.where(ky < 256, held, mirror))
        amp_in[...] = new.reshape(amp_in.shape)

    for part in range(2):
        ky = slice(256 * part, 256 * part + 256)
        quarters = [spectrum[512 * i + 256 * part : 512 * i + 256 * part + 256, :] for i in range(4)]
        real, imag = (jnp.concatenate(quarters[2 * i : 2 * i + 2], 1) for i in range(2))

        def back(scale, at):
            turn = (table[1024:1280, 0:256], table[1024:1280, 256:512])
            re, im = dot3(split(real * scale), turn), dot3(split(imag * scale), turn)
            for c, value in enumerate((re[:, :128] - im[:, 128:], im[:, :128] + re[:, 128:])):
                lanes = slice(128 * c, 128 * c + 128)
                lines[at, 0, ky, lanes], lines[at, 1, ky, lanes] = split(value)

        back(amp_in[8 * part : 8 * part + 8].reshape(256, EZ), 0)

        @pl.when(packed)
        def _():
            back(amps[ky, :], 1)

    def inverse(at):
        data = (lines[at, 0], lines[at, 1])
        by_cos, by_sin = (
            dot3([table[at : at + 256, :] for at in (256 * c, 512 + 256 * c)], data) for c in range(2)
        )
        return by_cos[:, :AZ] - by_sin[:, AZ:], by_cos[:, AZ:] + by_sin[:, :AZ]

    real, imag = inverse(0)

    def store(real, imag):
        lane = lax.broadcasted_iota(jnp.int32, (AY, AZ), 1)
        peer = lax.broadcasted_iota(jnp.int32, (AY, AZ), 0) % GA
        first = jnp.where(lane < 64, real, pltpu.roll(imag, 64, 1))
        second = jnp.where(lane < 64, pltpu.roll(real, 64, 1), imag)
        halo = pltpu.roll(first, AY - 8, 0)
        for g, shift in ((1, 7), (2, 7), (3, 6), (4, -6), (5, -7), (6, -7), (7, -8)):
            moved = pltpu.roll(second if g % 2 else first, (AY - shift) % AY, 0)
            halo = jnp.where(peer == g, moved, halo)
        for i, rows in enumerate((real, imag, halo)):
            out[pl.ds(i, AY, stride=3), :] = rows

    store(real, imag)

    @pl.when(packed)
    def _():
        store(real, inverse(1)[1])

    pltpu.sync_copy(out, sent)


def field_kernel(got, table, lo_x, hi_x, sent, table_in, sems):
    (copy,) = fetch([(table, table_in)], sems)
    ga, ba = lax.axis_index("ga"), lax.axis_index("ba")
    own = jnp.concatenate([got[pl.ds(c, DEVS, stride=3), :] for c in range(2)], 0)
    halo = got[pl.ds(2, DEVS, stride=3), :]
    halo = jnp.concatenate([halo, pltpu.roll(halo, 64, 1)], 0)
    copy.wait()
    log_field = dot3((table_in[0], table_in[1]), split(jnp.concatenate([own, halo], 1)))
    row = lax.broadcasted_iota(jnp.int32, (XROWS, AZ), 0)
    low_half = lax.broadcasted_iota(jnp.int32, (24, AZ), 1) < 64
    in_half = lax.broadcasted_iota(jnp.int32, (XROWS, AZ), 1) < 64
    halo_inside = jnp.where(ga < GA // 2, ba < BA - 1, ba > 0)
    for g in range(GA):
        x = row + (32 * g - 4)
        inside = (x >= 0) & (x < AX)
        value = log_field[XROWS * g : XROWS * g + XROWS, :]
        sent[CHUNK * g : CHUNK * g + XROWS, :] = jnp.where(inside, jnp.exp(value[:, :AZ]), 0.0)
        beside = jnp.where(inside & halo_inside & in_half, jnp.exp(value[:, AZ:]), 0.0)
        late = jnp.concatenate([beside[24:], beside[32:]], 0)
        sent[CHUNK * g + XROWS : CHUNK * g + CHUNK, :] = jnp.where(low_half, beside[:24], pltpu.roll(late, 64, 1))


def sweep_kernel(got, head, rech, lo_halo, hi_halo, lo_x, hi_x, cond_out, press_out,
                 head_ext, rech_ext, staged):
    ga, ba = lax.axis_index("ga"), lax.axis_index("ba")
    head_ext[...] = jnp.zeros_like(head_ext)
    rech_ext[...] = jnp.zeros_like(rech_ext)
    for y in range(8):
        at = XROWS * (y + 2)
        head_ext[at + 4 : at + 36, :] = head[pl.ds(y, 32, stride=8), :]
        rech_ext[at + 4 : at + 36, :] = rech[pl.ds(y, 32, stride=8), :]
    for halo, (first, second, only) in ((lo_halo, (1, 0, 1)), (hi_halo, (10, 11, 10))):
        for ref, y, i in ((head_ext, first, 0), (head_ext, second, 1), (rech_ext, only, 2)):
            ref[XROWS * y + 4 : XROWS * y + 36, :] = halo[32 * i : 32 * i + 32, :]
    for block, far, near in ((lo_x, 2, 3), (hi_x, 37, 36)):
        for y in range(8):
            at = XROWS * (y + 2)
            head_ext[at + far : at + far + 1, :] = block[y : y + 1, :]
            head_ext[at + near : at + near + 1, :] = block[8 + y : 9 + y, :]
            rech_ext[at + near : at + near + 1, :] = block[16 + y : 17 + y, :]
        head_ext[XROWS + near : XROWS + near + 1, :] = block[24:25, :]
        head_ext[10 * XROWS + near : 10 * XROWS + near + 1, :] = block[25:26, :]

    lane = lax.broadcasted_iota(jnp.int32, (XROWS, AZ), 1)
    row = lax.broadcasted_iota(jnp.int32, (XROWS, AZ), 0)
    x = row + (32 * ga - 4)
    inside_x = (x >= 0) & (x < AX)

    def in_plane(value):
        total = pltpu.roll(value, 1, 0) + pltpu.roll(value, XROWS - 1, 0)
        total = total + jnp.where(lane > 0, pltpu.roll(value, 1, 1), 0.0)
        return total + jnp.where(lane < AZ - 1, pltpu.roll(value, AZ - 1, 1), 0.0)

    low_half = lax.broadcasted_iota(jnp.int32, (24, AZ), 1) < 64

    def beside(i):
        first, second = (got[CHUNK * g + XROWS : CHUNK * g + CHUNK, :] for g in (2 * i, 2 * i + 1))
        early = jnp.where(low_half, first, pltpu.roll(second, 64, 1))
        late = jnp.where(low_half, pltpu.roll(first, 64, 1), second)
        return jnp.concatenate([early, late[:16]], 0)

    cond = [beside(2), beside(3)]
    cond += [got[CHUNK * y : CHUNK * y + XROWS, :] for y in range(8)]
    cond += [beside(0), beside(1)]
    planes = [head_ext[XROWS * y : XROWS * y + XROWS, :] for y in range(12)]
    weight = {y: 6.0 * cond[y] + (in_plane(cond[y]) + (cond[y - 1] + cond[y + 1])) for y in range(1, 11)}
    source = {y: 2.0 * rech_ext[XROWS * y : XROWS * y + XROWS, :] for y in range(1, 11)}
    for sweep in range(2):
        flow = {y: cond[y] * planes[y] for y in range(sweep, 12 - sweep)}
        new = dict()
        for y in range(sweep + 1, 11 - sweep):
            heads = in_plane(planes[y]) + (planes[y - 1] + planes[y + 1])
            flows = in_plane(flow[y]) + (flow[y - 1] + flow[y + 1])
            new[y] = (source[y] + (cond[y] * heads + flows)) / weight[y]
            if sweep == 0:
                inside = inside_x
                if y == 1:
                    inside = inside & (ba > 0)
                if y == 10:
                    inside = inside & (ba < BA - 1)
                new[y] = jnp.where(inside, new[y], 0.0)
        planes = new
    for y in range(8):
        cond_out[pl.ds(y, 32, stride=8), :] = got[CHUNK * y + 4 : CHUNK * y + 36, :]
        staged[...] = planes[y + 2]
        press_out[pl.ds(y, 32, stride=8), :] = staged[4:36, :]


def kernel_call(kernel, outs, inputs, scratch=(), held=(), outs_held=(), vmem=VMEM, flops=0, aliases=None, hbm=()):
    whole = pl.BlockSpec(memory_space=pltpu.VMEM)
    there = pl.BlockSpec(memory_space=pl.ANY)
    pinned = pl.BlockSpec(memory_space=pltpu.HBM)
    return pl.pallas_call(
        kernel,
        out_shape=[jax.ShapeDtypeStruct(shape, f32) for shape in outs],
        in_specs=[pinned if i in hbm else there if i in held else whole for i in range(len(inputs))],
        out_specs=[pinned if i in outs_held else whole for i in range(len(outs))],
        scratch_shapes=list(scratch),
        input_output_aliases=aliases or {},
        compiler_params=pltpu.CompilerParams(vmem_limit_bytes=vmem),
        cost_estimate=pl.CostEstimate(flops=flops, bytes_accessed=6 * 2**20, transcendentals=0) if flops else None,
    )(*inputs)


def steps(axis):
    up = [(i, i + 1) for i in range(lax.axis_size(axis) - 1)]
    return up, [(j, i) for i, j in up]


def body(noise, amplitude, recharge, head_guess):
    x_fwd, forward_table, inverse_table, x_inv = (jnp.asarray(t) for t in tables())
    recharge = recharge.reshape(256, AZ)
    head = head_guess.reshape(256, AZ)
    memory, sems = pltpu.VMEM, pltpu.SemaphoreType.DMA
    (sent,) = kernel_call(
        enter_kernel, [(8 * DEVS, 128)], [noise.reshape(512, EX), x_fwd],
        [memory((512, EX), f32), memory(x_fwd.shape, bf16), memory((8 * DEVS, 128), f32), sems((3,))],
        hbm=(0, 1), outs_held=(0,), flops=10**9,
    )
    got = lax.all_to_all(sent, ("ba", "ga"), 0, 0, tiled=True)
    half, plane = (BA // 2, 16, EZ), (BA // 2, 2, 16, EZ)
    keep, give, amp_first, below, above = kernel_call(
        edges_kernel, [plane, half, (16, EZ), (96, AZ), (96, AZ)], [amplitude, head, recharge],
        [memory((16, 40, EZ), f32), sems((1,))], hbm=(0,), vmem=8 * 2**20,
    )
    other = lax.ppermute(give, "ba", [(i, i ^ 1) for i in range(BA)])
    zero_near = lax.ppermute(amp_first, "ga", [(0, PACKED_GA)])
    pairs = [(b + 1, PACKED_GA * BA + b) for b in range(BA // 2, BA, 2)]
    zero_far = lax.ppermute(amp_first, ("ga", "ba"), pairs)
    amp_row = lax.ppermute(amp_first, "ba", [(BA // 2, 0)])
    up, down = steps("ba")
    hi_halo = lax.ppermute(below, "ba", down)
    lo_halo = lax.ppermute(above, "ba", up)
    (amp_sent,) = kernel_call(
        join_kernel, [plane], [keep, other, zero_near, zero_far, got, lo_halo, hi_halo],
        [sems((2,))], held=(0, 4, 5, 6), outs_held=(0,), vmem=4 * 2**20, aliases={0: 0},
    )
    halves = [list(range(side, BA, 2)) for side in range(2)]
    amp = lax.all_to_all(amp_sent.reshape(EY, EZ), "ba", 0, 0, tiled=True, axis_index_groups=halves)
    spectrum, to_up, to_down = kernel_call(
        forward_kernel, [(4 * EY, 128), (32, AZ), (32, AZ)], [got, forward_table, head, recharge, lo_halo, hi_halo],
        [memory((2, 2, 512, 256), bf16), memory((48, AZ), f32), sems((4,))],
        hbm=(2, 3), flops=3 * 10**9, vmem=VMEM_MIDDLE,
    )
    (sent,) = kernel_call(
        inverse_kernel, [(3 * AY, AZ)],
        [spectrum, amp.reshape(plane), zero_near, amp_row, inverse_table],
        [memory(plane, f32), memory((2, 2, EY, 2 * AZ), bf16), memory((EY, EZ), f32), memory((3 * AY, AZ), f32), sems((2,))],
        outs_held=(0,), vmem=VMEM_MIDDLE,
    )
    sent = sent.reshape(DEVS, 1, 3 * AZ)
    got = lax.all_to_all(sent, ("ba", "ga"), 0, 0, tiled=True).reshape(3 * DEVS, AZ)
    up, down = steps("ga")
    lo_x = lax.ppermute(to_up, "ga", up)
    hi_x = lax.ppermute(to_down, "ga", down)
    (sent,) = kernel_call(
        field_kernel, [(CHUNK * GA, AZ)], [got, x_inv, lo_x, hi_x],
        [memory(x_inv.shape, bf16), sems((1,))], held=(2, 3), hbm=(1,), vmem=VMEM_END,
    )
    got = lax.all_to_all(sent, "ga", 0, 0, tiled=True)
    ext = pltpu.VMEM((12 * XROWS, AZ), f32)
    conductivity, pressure = kernel_call(
        sweep_kernel, [(256, AZ), (256, AZ)],
        [got, head, recharge, lo_halo, hi_halo, lo_x, hi_x],
        [ext, ext, pltpu.VMEM((XROWS, AZ), f32)], vmem=VMEM_END,
    )
    return conductivity.reshape(32, 8, AZ), pressure.reshape(32, 8, AZ)


def solution(mesh):
    placed = (P("ba", "ga", None), P("ba", "ga", None), P("ga", "ba", None), P("ga", "ba", None))
    return jax.shard_map(
        body,
        mesh=mesh,
        in_specs=placed,
        out_specs=(P("ga", "ba", None), P("ga", "ba", None)),
        check_vma=False,
    )
```
